32 devices in a mesh: tok: 16 (over z, y, x), feat: 2 (over core).
Axes of the slice: x: 2, y: 2, z: 4, core: 2. Of those that a mesh axis runs over, the one named last changes fastest.
Arguments:
- activations: bfloat16 [32768, 8192], P('tok', 'feat')
- labels: int32 [32768], P('tok'), may hold values from 0 to 7, as said below
Outputs:
- cov_panel: float32 [256, 8192], P('tok', 'feat')
- cross_cov: float32 [8, 8192], P(None, 'feat')
The draws below stay inside these ranges and needn't reach their ends.
Inputs may be any that keep to these rules, and one draw needn't show every extreme that they name: `labels`: each token's class.
All inputs are finite; a program needn't handle non-finite values.
Results may differ from the reference program's by a relative error of at most 0.0017.
Values may be sent and summed in bfloat16 or wider, within the bound.
No kernel may reach another device: no remote copies, remote signals or barrier semaphores. Data moves between devices by JAX's collectives and lax.ppermute only.
A program may use at most 64 MiB of HBM per device.

```python
import jax
import jax.numpy as jnp
from jax import lax

D = 8192
CLASSES = 8
PANEL = 128
TOK_DEV = 2048
TOKENS = 32768
N_TOK = 16
N_FEAT = 2


def shared_labels(key):
    return jax.random.randint(jax.random.fold_in(key, 11), (TOKENS,), 0, CLASSES).astype(jnp.int32)


def draw_labels(key, part):
    return shared_labels(key)


def draw_activations(key, part):
    classes = shared_labels(key)
    latent_count = 512
    offset = 1.5 * jax.random.normal(jax.random.fold_in(key, 12), (D,), jnp.float32)
    embed = 1.2 * jax.random.normal(jax.random.fold_in(key, 13), (CLASSES, D), jnp.float32)
    col_scale = jnp.exp(jax.random.uniform(jax.random.fold_in(key, 14), (D,), jnp.float32, -1.1513, 1.1513))
    row_scale = jnp.exp(jax.random.uniform(jax.random.fold_in(key, 15), (TOKENS,), jnp.float32, -1.1513, 1.1513))
    drift = 1.0 + 2.0 * jnp.arange(TOKENS, dtype=jnp.float32) / (TOKENS - 1)
    mixing = jax.random.normal(jax.random.fold_in(key, 19), (latent_count, D), jnp.float32) / jnp.sqrt(jnp.float32(latent_count))
    signal = offset[None, :] + embed[classes]
    noise = jax.random.normal(jax.random.fold_in(key, 16), (TOKENS, D), jnp.float32)
    latent = jax.random.normal(jax.random.fold_in(key, 20), (TOKENS, latent_count), jnp.float32)
    linked = jnp.dot(latent, mixing, precision=lax.Precision.HIGHEST)
    values = drift[:, None] * signal + row_scale[:, None] * col_scale[None, :] * (noise + 2.0 * linked)
    return values.astype(jnp.bfloat16)


def setup_inputs(seed: int = 0) -> dict:
    key_list = jax.random.split(jax.random.key(seed), 3)
    return {
        "activations": draw_activations(jax.random.fold_in(key_list[2], 71), 0),
        "labels": draw_labels(jax.random.fold_in(key_list[2], 71), 0),
    }


def product(left, right):
    return lax.dot_general(left.astype(jnp.float32), right.astype(jnp.float32), (((0,), (0,)), ((), ())), precision=lax.Precision.HIGHEST, preferred_element_type=jnp.float32)


def reference(activations, labels):
    count = activations.shape[0]
    block = D // N_FEAT
    rows = activations.reshape(N_TOK, TOK_DEV, D)
    tags = labels.reshape(N_TOK, TOK_DEV)

    def add_sum(carry, piece):
        return carry + jnp.sum(piece.astype(jnp.float32), axis=0), None

    column_total, _ = lax.scan(add_sum, jnp.zeros((D,), jnp.float32), rows)
    mean = column_total / count
    classes = jnp.arange(CLASSES, dtype=jnp.int32)

    def add_terms(carry, item):
        piece, tag = item
        centered = (piece.astype(jnp.float32) - mean).astype(jnp.bfloat16)
        onehot = (tag[:, None] == classes[None, :]).astype(jnp.bfloat16)
        panel = centered.reshape(TOK_DEV, N_FEAT, block)[:, :, :PANEL].reshape(TOK_DEV, N_FEAT * PANEL)
        cov_acc = carry[0] + product(panel, centered)
        class_acc = carry[1] + product(onehot, centered)
        return (cov_acc, class_acc), None

    start = (jnp.zeros((N_FEAT * PANEL, D), jnp.float32), jnp.zeros((CLASSES, D), jnp.float32))
    sums, _ = lax.scan(add_terms, start, (rows, tags))
    cov_panel = sums[0] / (count - 1)
    cross_cov = sums[1] / count
    return cov_panel, cross_cov
```

```python
import functools

import jax
import jax.numpy as jnp
from jax import lax
from jax.experimental import pallas as pl
from jax.experimental.pallas import tpu as pltpu
from jax.sharding import PartitionSpec as P

CLASSES = 8
PANEL = 128
PAD = 16


def position(block, order):
    pos = 0
    for bit in order:
        pos = pos * 2 + ((block >> bit) & 1)
    return pos


def local_kernel(orders, steps, bits_ref, x_ref, panel_ref, labels_ref,
                 send_ref, keep_ref, sums_ref, means_ref, left, split, count):
    step = pl.program_id(0)
    tokens, width = x_ref.shape
    rows = panel_ref.shape[1]
    n_tok = 2 ** len(orders[0])
    unit = rows // n_tok
    cols = width * steps

    @pl.when(step == 0)
    def _():
        panel = panel_ref[...].astype(jnp.float32)
        mean = jnp.sum(panel, axis=0, keepdims=True) / tokens
        means_ref[:, cols:] = mean
        left[:rows, :] = (panel - mean).astype(jnp.bfloat16).T
        kind = lax.broadcasted_iota(jnp.int32, (PAD, tokens), 0)
        onehot = (labels_ref[...] == kind).astype(jnp.float32)
        left[rows:, :] = onehot.astype(jnp.bfloat16)
        count[...] = jnp.broadcast_to(
            jnp.sum(onehot[:CLASSES], axis=1, keepdims=True), count.shape
        )
        sums_ref[:, cols:] = count[...]

    x = x_ref[...].astype(jnp.float32)
    mean = jnp.sum(x, axis=0, keepdims=True) / tokens
    y = (x - mean).astype(jnp.bfloat16)
    out = jnp.dot(left[...], y, preferred_element_type=jnp.float32)
    here = pl.ds(pl.multiple_of(step * width, width), width)
    means_ref[:, here] = mean
    sums_ref[:, here] = out[rows:rows + CLASSES] + count[:, :1] * mean

    for part, order in enumerate(orders):
        @pl.when(step // (steps // 2) == part)
        def _(order=order):
            half = n_tok // 2
            for block in range(n_tok):
                pos = position(block, order)
                split[pos // half, pl.ds((pos % half) * unit, unit), :] = (
                    out[block * unit:(block + 1) * unit]
                )
            mine = bits_ref[order[0]]
            keep_ref[...] = split[mine]
            send_ref[...] = split[1 - mine].astype(jnp.bfloat16)


def local_part(activations, panel, labels, bits, orders):
    tokens, cols = activations.shape
    rows = panel.shape[1]
    width = min(512, cols // 2)
    steps = cols // width
    whole = lambda step, *_: (0, 0)
    column = lambda step, *_: (0, step)
    return pl.pallas_call(
        functools.partial(local_kernel, orders, steps),
        grid_spec=pltpu.PrefetchScalarGridSpec(
            num_scalar_prefetch=1,
            grid=(steps,),
            in_specs=[
                pl.BlockSpec((tokens, width), column),
                pl.BlockSpec((tokens, rows), whole),
                pl.BlockSpec((1, tokens), whole),
            ],
            out_specs=[
                pl.BlockSpec((rows // 2, width), column),
                pl.BlockSpec((rows // 2, width), column),
                pl.BlockSpec((CLASSES, cols + PANEL), whole),
                pl.BlockSpec((1, cols + rows), whole),
            ],
            scratch_shapes=[
                pltpu.VMEM((rows + PAD, tokens), jnp.bfloat16),
                pltpu.VMEM((2, rows // 2, width), jnp.float32),
                pltpu.VMEM((CLASSES, PANEL), jnp.float32),
            ],
        ),
        out_shape=[
            jax.ShapeDtypeStruct((rows // 2, cols), jnp.bfloat16),
            jax.ShapeDtypeStruct((rows // 2, cols), jnp.float32),
            jax.ShapeDtypeStruct((CLASSES, cols + PANEL), jnp.float32),
            jax.ShapeDtypeStruct((1, cols + rows), jnp.float32),
        ],
        compiler_params=pltpu.CompilerParams(vmem_limit_bytes=48 * 2**20),
        cost_estimate=pl.CostEstimate(
            flops=2 * tokens * cols * (rows + PAD),
            bytes_accessed=2 * tokens * cols + 6 * (rows // 2) * cols,
            transcendentals=0,
        ),
        name="local_sums",
    )(bits, activations, panel, labels)


def swap(value, bit, n_tok):
    return lax.ppermute(value, "tok", [(i, i ^ (1 << bit)) for i in range(n_tok)])


def gather_panel(activations):
    n_feat = lax.axis_size("feat")
    me = lax.axis_index("feat")
    own = activations[:, :PANEL]
    if n_feat == 2:
        other = lax.ppermute(own, "feat", [(0, 1), (1, 0)])
        first = jnp.where(me == 0, own, other)
        second = jnp.where(me == 0, other, own)
        return jnp.concatenate([first, second], axis=1)
    return lax.all_gather(own, "feat", axis=1, tiled=True)


def body(activations, labels):
    tokens, cols = activations.shape
    n_tok = lax.axis_size("tok")
    levels = n_tok.bit_length() - 1
    assert n_tok == 1 << levels
    me = lax.axis_index("tok")
    total = tokens * n_tok
    bits = jnp.stack([(me >> b) & 1 for b in range(levels)]).astype(jnp.int32)
    orders = [
        list(range(levels)),
        [1, 0] + list(range(2, levels)),
    ]
    panel = gather_panel(activations)
    send, keep, sums, means = local_part(activations, panel, labels[None, :], bits, orders)

    half = cols // 2
    pieces = []
    for part, order in enumerate(orders):
        here = slice(part * half, (part + 1) * half)
        out, mine = send[:, here], keep[:, here]
        for level, bit in enumerate(order):
            came = swap(out, bit, n_tok)
            if level + 1 < levels:
                bit = bits[order[level + 1]]
                size = mine.shape[0] // 2
                pick = lambda a, b: lax.dynamic_slice_in_dim(a, b * size, size, 0)
                out = (pick(mine, 1 - bit) + pick(came, 1 - bit).astype(jnp.float32)).astype(jnp.bfloat16)
                mine = pick(mine, bit) + pick(came, bit).astype(jnp.float32)
            else:
                mine = mine + came.astype(jnp.float32)
        pieces.append(mine)

    for bit in list(range(2, levels)) + [0, 1]:
        sums = sums + swap(sums, bit, n_tok)
        means = jnp.concatenate([means, swap(means, bit, n_tok)], axis=0)

    mean = jnp.sum(means, axis=0, keepdims=True) / n_tok
    away = means - mean
    unit = keep.shape[0] * 2 // n_tok
    rows = lax.dynamic_slice_in_dim(away[:, cols:], me * unit, unit, 1)
    between = lax.dot_general(
        rows, away[:, :cols], (((0,), (0,)), ((), ())),
        precision=lax.Precision.HIGHEST, preferred_element_type=jnp.float32,
    )
    cov_panel = (jnp.concatenate(pieces, axis=1) + tokens * between) / (total - 1)
    cross_cov = (sums[:, :cols] - sums[:, cols:cols + 1] * mean[:, :cols]) / total
    return cov_panel, cross_cov


def solution(mesh):
    in_specs = (P("tok", "feat"), P("tok"))
    out_specs = (P("tok", "feat"), P(None, "feat"))
    return jax.shard_map(body, mesh=mesh, in_specs=in_specs, out_specs=out_specs, check_vma=False)
```

```python
import functools

import jax
import jax.numpy as jnp
from jax import lax
from jax.experimental import pallas as pl
from jax.experimental.pallas import tpu as pltpu
from jax.sharding import PartitionSpec as P

CLASSES = 8
PANEL = 128
PAD = 16
SHIFT_ROWS = 128
VMEM_LIMIT = 48 * 2**20


def orders_of(levels):
    even = list(range(levels))
    odd = list(even)
    for i in range(0, levels - 1, 2):
        odd[i], odd[i + 1] = even[i + 1], even[i]
    return even, odd


def position(block, order):
    pos = 0
    for bit in order:
        pos = pos * 2 + ((block >> bit) & 1)
    return pos


def shifted(x):
    shift = jnp.mean(x[:SHIFT_ROWS].astype(jnp.float32), axis=0, keepdims=True)
    shift = shift.astype(jnp.bfloat16)
    return x - shift, shift.astype(jnp.float32)


def local_kernel(orders, steps, n_pieces, meta_ref, x_ref, *refs):
    pieces, (labels_ref, send_ref, keep_ref, sums_ref, left, split, rowsum) = refs[:n_pieces], refs[n_pieces:]
    step = pl.program_id(0)
    tokens, width = x_ref.shape
    rows = left.shape[0] - PAD
    n_tok = 2 ** len(orders[0])
    unit = rows // n_tok
    cols = width * steps

    @pl.when(step == 0)
    def _():
        sums_ref[:, cols:] = jnp.zeros((CLASSES, rows + PANEL), jnp.float32)
        for i, piece in enumerate(pieces):
            size = piece.shape[1]
            y, shift = shifted(piece[...])
            total = jnp.sum(y.astype(jnp.float32), axis=0, keepdims=True) + tokens * shift
            at = pl.multiple_of(meta_ref[i], PANEL)
            left[pl.ds(at, size), :] = y.T
            sums_ref[0:1, pl.ds(cols + at, size)] = total
        kind = lax.broadcasted_iota(jnp.int32, (PAD, tokens), 0)
        left[rows:, :] = (labels_ref[...] == kind).astype(jnp.float32).astype(jnp.bfloat16)
        rowsum[...] = jnp.broadcast_to(
            jnp.sum(left[...].astype(jnp.float32), axis=1, keepdims=True), rowsum.shape
        )
        sums_ref[:, cols + rows:] = rowsum[rows:rows + CLASSES]

    y, shift = shifted(x_ref[...])
    out = jnp.dot(left[...], y, preferred_element_type=jnp.float32)
    here = pl.ds(pl.multiple_of(step * width, width), width)
    by_class = out[rows:rows + CLASSES]
    sums_ref[:, here] = by_class + rowsum[rows:rows + CLASSES, :1] * shift
    total = jnp.sum(by_class, axis=0, keepdims=True) / tokens
    out = out[:rows] - rowsum[:rows, :1] * total

    for part, order in enumerate(orders):
        @pl.when(meta_ref[n_pieces + 1] == part)
        def _(order=order):
            half = n_tok // 2
            for block in range(n_tok):
                pos = position(block, order)
                split[pos // half, pl.ds((pos % half) * unit, unit), :] = (
                    out[block * unit:(block + 1) * unit]
                )
    mine = meta_ref[n_pieces]
    keep_ref[...] = split[mine]
    send_ref[...] = split[1 - mine].astype(jnp.bfloat16)


def local_part(activations, pieces, labels, meta, orders, rows):
    tokens, cols = activations.shape
    width = min(512, cols)
    steps = cols // width
    whole = lambda step, *_: (0, 0)
    column = lambda step, *_: (0, step)
    return pl.pallas_call(
        functools.partial(local_kernel, orders, steps, len(pieces)),
        grid_spec=pltpu.PrefetchScalarGridSpec(
            num_scalar_prefetch=1,
            grid=(steps,),
            in_specs=[pl.BlockSpec((tokens, width), column)]
            + [pl.BlockSpec((tokens, size), whole) for _, size in pieces]
            + [pl.BlockSpec((1, tokens), whole)],
            out_specs=[
                pl.BlockSpec((rows // 2, width), column),
                pl.BlockSpec((rows // 2, width), column),
                pl.BlockSpec((CLASSES, cols + rows + PANEL), whole),
            ],
            scratch_shapes=[
                pltpu.VMEM((rows + PAD, tokens), jnp.bfloat16),
                pltpu.VMEM((2, rows // 2, width), jnp.float32),
                pltpu.VMEM((rows + PAD, PANEL), jnp.float32),
            ],
        ),
        out_shape=[
            jax.ShapeDtypeStruct((rows // 2, cols), jnp.bfloat16),
            jax.ShapeDtypeStruct((rows // 2, cols), jnp.float32),
            jax.ShapeDtypeStruct((CLASSES, cols + rows + PANEL), jnp.float32),
        ],
        compiler_params=pltpu.CompilerParams(vmem_limit_bytes=VMEM_LIMIT),
        cost_estimate=pl.CostEstimate(
            flops=2 * tokens * cols * (rows + PAD),
            bytes_accessed=2 * tokens * cols + 6 * (rows // 2) * cols,
            transcendentals=0,
        ),
        name="local_sums",
    )(meta, activations, *[piece for piece, _ in pieces], labels)


def apart(mine_sums, came_sums, ids, group, cols, rows):
    diff = (jnp.sum(mine_sums, axis=0, keepdims=True) - jnp.sum(came_sums, axis=0, keepdims=True)) / group
    panel = diff[:, cols:cols + rows]
    lane = lax.broadcasted_iota(jnp.int32, (ids.shape[0], rows), 1)
    column = jnp.sum(jnp.where(lane == ids, panel, 0.0), axis=1, keepdims=True)
    return diff[:, :cols], column * (group / 2)


def row_ids(start, count, weights, base, unit):
    pos = lax.broadcasted_iota(jnp.int32, (count, 1), 0) + start
    ids = pos % unit + base
    block = pos // unit
    for k, weight in enumerate(reversed(weights)):
        ids = ids + ((block >> k) & 1) * weight
    return ids


def merge_kernel(level, levels, group, scale, meta_ref, mine_ref, came_ref, mine_sums, came_sums, *outs):
    size, cols = mine_ref.shape
    rows = size * 2 ** (level + 1)
    unit = rows // 2 ** levels
    weights = [meta_ref[levels + k] for k in range(levels)]
    base = 0
    for k in range(level + 1):
        base = base + meta_ref[k] * weights[k]
    last = level + 1 == levels
    count = size if last else size // 2

    def merged(start):
        ids = row_ids(start, count, weights[level + 1:], base, unit)
        across, down = apart(mine_sums[...], came_sums[...], ids, group, cols, rows)
        here = pl.ds(start, count)
        return mine_ref[here, :] + came_ref[here, :].astype(jnp.float32) + down * across

    if last:
        outs[0][...] = merged(0) * scale
    else:
        send_ref, keep_ref = outs
        mine = meta_ref[level + 1]
        send_ref[...] = merged(pl.multiple_of((1 - mine) * count, count)).astype(jnp.bfloat16)
        keep_ref[...] = merged(pl.multiple_of(mine * count, count))


def merge(level, levels, group, scale, meta, mine, came, mine_sums, came_sums):
    size, cols = mine.shape
    vmem = pl.BlockSpec(memory_space=pltpu.VMEM)
    if level + 1 == levels:
        shapes = [jax.ShapeDtypeStruct((size, cols), jnp.float32)]
    else:
        shapes = [jax.ShapeDtypeStruct((size // 2, cols), t) for t in (jnp.bfloat16, jnp.float32)]
    return pl.pallas_call(
        functools.partial(merge_kernel, level, levels, group, scale),
        in_specs=[pl.BlockSpec(memory_space=pltpu.SMEM)] + [vmem] * 4,
        out_specs=[vmem] * len(shapes),
        out_shape=shapes,
        compiler_params=pltpu.CompilerParams(vmem_limit_bytes=VMEM_LIMIT),
        name="merge",
    )(meta, mine, came, mine_sums, came_sums)


def body(activations, labels):
    tokens, cols = activations.shape
    n_tok, n_feat = lax.axis_size("tok"), lax.axis_size("feat")
    levels = n_tok.bit_length() - 1
    assert n_tok == 1 << levels
    rows = PANEL * n_feat
    unit = rows // n_tok
    me, feat = lax.axis_index("tok"), lax.axis_index("feat")
    total = tokens * n_tok
    even, odd = orders_of(levels)
    parity = feat % 2
    order = [jnp.where(parity == 0, a, b) for a, b in zip(even, odd)]
    bits = [(me >> b) & 1 for b in order]
    meta = jnp.stack(bits + [unit << b for b in order]).astype(jnp.int32)

    def swap(value, level):
        pairs = []
        for i in range(n_tok):
            for f in range(n_feat):
                bit = (even, odd)[f % 2][level]
                pairs.append((i * n_feat + f, (i ^ (1 << bit)) * n_feat + f))
        return lax.ppermute(value, ("tok", "feat"), pairs)

    own = activations[:, :PANEL]
    if n_feat == 2:
        other = lax.ppermute(own, "feat", [(0, 1), (1, 0)])
        pieces = [(activations, PANEL), (other, PANEL)]
        places = [feat * PANEL, (1 - feat) * PANEL]
    else:
        pieces = [(lax.all_gather(own, "feat", axis=1, tiled=True), rows)]
        places = [0]
    places = jnp.stack(places + [bits[0], parity]).astype(jnp.int32)
    send, mine, sums = local_part(activations, pieces, labels[None, :], places, (even, odd), rows)

    for level in range(levels):
        came_sums = swap(sums, level)
        came = swap(send, level)
        out = merge(level, levels, tokens << level, 1.0 / (total - 1), meta, mine, came, sums, came_sums)
        sums = sums + came_sums
        send, mine = out if level + 1 < levels else (None, out[0])

    by_class, count = sums[:, :cols], sums[:, cols + rows:cols + rows + 1]
    mean = jnp.sum(by_class, axis=0, keepdims=True) / total
    cross_cov = (by_class - count * mean) / total
    return mine, cross_cov


def solution(mesh):
    in_specs = (P("tok", "feat"), P("tok"))
    out_specs = (P("tok", "feat"), P(None, "feat"))
    return jax.shard_map(body, mesh=mesh, in_specs=in_specs, out_specs=out_specs, check_vma=False)
```

```python
import functools

import jax
import jax.numpy as jnp
from jax import lax
from jax.experimental import pallas as pl
from jax.experimental.pallas import tpu as pltpu
from jax.sharding import PartitionSpec as P

CLASSES = 8
PANEL = 128
PAD = 16
SHIFT_ROWS = 128
CHUNKS = 2
VMEM_LIMIT = 48 * 2**20


def orders_of(levels):
    even = list(range(levels))
    odd = list(even)
    for i in range(0, levels - 1, 2):
        odd[i], odd[i + 1] = even[i + 1], even[i]
    return even, odd


def position(block, order):
    pos = 0
    for bit in order:
        pos = pos * 2 + ((block >> bit) & 1)
    return pos


def prepare(orders, meta_ref, pieces, labels_ref, left, columns, panel_sums):
    tokens = left.shape[1]
    rows = left.shape[0] - PAD
    unit = rows // 2 ** len(orders[0])
    for i, piece in enumerate(pieces):
        size = piece.shape[1]
        raw = piece[...].T
        shift = jnp.mean(raw[:, :SHIFT_ROWS].astype(jnp.float32), axis=1, keepdims=True)
        shift = shift.astype(jnp.bfloat16)
        y = raw - shift
        shift = jnp.broadcast_to(shift.astype(jnp.float32), (size, PANEL))
        first = meta_ref[i]
        for j in range(size // unit):
            block = first + j
            even, odd = (sum(((block >> bit) & 1) << k for k, bit in enumerate(reversed(order))) for order in orders)
            pos = jnp.where(meta_ref[len(pieces) + 1] == 0, even, odd)
            at = pl.ds(pl.multiple_of(pos * unit, unit), unit)
            here = slice(j * unit, (j + 1) * unit)
            left[at, :] = y[here]
            columns[at, :] = shift[here]
    kind = lax.broadcasted_iota(jnp.int32, (PAD, tokens), 0)
    left[rows:, :] = (labels_ref[...] == kind).astype(jnp.float32).astype(jnp.bfloat16)
    shift = columns[:rows, :]
    total = jnp.sum(left[...].astype(jnp.float32), axis=1, keepdims=True)
    columns[...] = jnp.broadcast_to(total, columns.shape)
    panel_sums[...] = jnp.broadcast_to((columns[:rows, :] + tokens * shift).T[:1, :], panel_sums.shape)


def multiply(mine, x_ref, left, columns, send_ref, keep_ref, sums_ref, split):
    tokens = x_ref.shape[0]
    rows = left.shape[0] - PAD
    half = rows // 2
    x = x_ref[...]
    shift = jnp.mean(x[:SHIFT_ROWS].astype(jnp.float32), axis=0, keepdims=True).astype(jnp.bfloat16)
    out = jnp.dot(left[...], x - shift, preferred_element_type=jnp.float32)
    by_class = out[rows:rows + CLASSES]
    sums_ref[...] = by_class + columns[rows:rows + CLASSES, :1] * shift.astype(jnp.float32)
    total = jnp.sum(by_class, axis=0, keepdims=True) / tokens
    split[...] = out[:rows] - columns[:rows, :1] * total
    keep_ref[...] = split[pl.ds(pl.multiple_of(mine * half, half), half), :]
    send_ref[...] = split[pl.ds(pl.multiple_of((1 - mine) * half, half), half), :].astype(jnp.bfloat16)


def first_kernel(orders, n_pieces, meta_ref, x_ref, *refs):
    pieces, (labels_ref, send_ref, keep_ref, sums_ref, left, columns, panel_sums, split) = (
        refs[:n_pieces], refs[n_pieces:]
    )

    @pl.when(pl.program_id(0) == 0)
    def _():
        prepare(orders, meta_ref, pieces, labels_ref, left, columns, panel_sums)

    multiply(meta_ref[n_pieces], x_ref, left, columns, send_ref, keep_ref, sums_ref, split)


def later_kernel(n_pieces, meta_ref, x_ref, left, columns, send_ref, keep_ref, sums_ref, split):
    multiply(meta_ref[n_pieces], x_ref, left, columns, send_ref, keep_ref, sums_ref, split)


def local_part(chunk, activations, pieces, labels, meta, orders, rows, prepared=None):
    tokens, cols = activations.shape
    part = cols // CHUNKS
    width = min(512, part)
    steps = part // width
    whole = lambda step, *_: (0, 0)
    column = lambda step, *_: (0, step)
    taken = lambda step, *_: (0, chunk * steps + step)
    saved_shape = [
        jax.ShapeDtypeStruct((rows + PAD, tokens), jnp.bfloat16),
        jax.ShapeDtypeStruct((rows + PAD, PANEL), jnp.float32),
    ]
    saved_spec = [pl.BlockSpec(s.shape, whole) for s in saved_shape]
    out_specs = [
        pl.BlockSpec((rows // 2, width), column),
        pl.BlockSpec((rows // 2, width), column),
        pl.BlockSpec((CLASSES, width), column),
    ]
    out_shape = [
        jax.ShapeDtypeStruct((rows // 2, part), jnp.bfloat16),
        jax.ShapeDtypeStruct((rows // 2, part), jnp.float32),
        jax.ShapeDtypeStruct((CLASSES, part), jnp.float32),
    ]
    in_specs = [pl.BlockSpec((tokens, width), taken)]
    if prepared is None:
        kernel = functools.partial(first_kernel, orders, len(pieces))
        in_specs += [pl.BlockSpec((tokens, size), whole) for _, size in pieces]
        in_specs += [pl.BlockSpec((1, tokens), whole)]
        out_specs += saved_spec + [pl.BlockSpec((CLASSES, rows), whole)]
        out_shape += saved_shape + [jax.ShapeDtypeStruct((CLASSES, rows), jnp.float32)]
        args = [piece for piece, _ in pieces] + [labels]
    else:
        kernel = functools.partial(later_kernel, len(pieces))
        in_specs += saved_spec
        args = list(prepared)
    return pl.pallas_call(
        kernel,
        grid_spec=pltpu.PrefetchScalarGridSpec(
            num_scalar_prefetch=1,
            grid=(steps,),
            in_specs=in_specs,
            out_specs=out_specs,
            scratch_shapes=[pltpu.VMEM((rows, width), jnp.float32)],
        ),
        out_shape=out_shape,
        compiler_params=pltpu.CompilerParams(vmem_limit_bytes=VMEM_LIMIT),
        cost_estimate=pl.CostEstimate(
            flops=2 * tokens * part * (rows + PAD),
            bytes_accessed=2 * tokens * part + 6 * (rows // 2) * part,
            transcendentals=0,
        ),
        name="local_sums",
    )(meta, activations, *args)


def body(activations, labels):
    tokens, cols = activations.shape
    n_tok, n_feat = lax.axis_size("tok"), lax.axis_size("feat")
    levels = n_tok.bit_length() - 1
    assert n_tok == 1 << levels
    rows = PANEL * n_feat
    unit = rows // n_tok
    part = cols // CHUNKS
    me, feat = lax.axis_index("tok"), lax.axis_index("feat")
    total = tokens * n_tok
    even, odd = orders_of(levels)
    parity = feat % 2
    bits = [(me >> jnp.where(parity == 0, a, b)) & 1 for a, b in zip(even, odd)]

    def swap(value, level):
        pairs = []
        for i in range(n_tok):
            for f in range(n_feat):
                bit = (even, odd)[f % 2][level]
                pairs.append((i * n_feat + f, (i ^ (1 << bit)) * n_feat + f))
        return lax.ppermute(value, ("tok", "feat"), pairs)

    own = activations[:, :PANEL]
    if n_feat == 2:
        other = lax.ppermute(own, "feat", [(0, 1), (1, 0)])
        pieces = [(activations, PANEL), (other, PANEL)]
        places = [feat * PANEL // unit, (1 - feat) * PANEL // unit]
    else:
        pieces = [(lax.all_gather(own, "feat", axis=1, tiled=True), rows)]
        places = [0]
    meta = jnp.stack(places + [bits[0], parity]).astype(jnp.int32)

    sums, sends, kept, prepared = [], [], [], None
    for chunk in range(CHUNKS):
        out = local_part(chunk, activations, pieces, labels[None, :], meta, (even, odd), rows, prepared)
        sends.append(swap(out[0], 0))
        kept.append(out[1])
        sums.append(out[2])
        if chunk == 0:
            prepared = out[3:5]
            panel_sums = out[5]
    count = jnp.broadcast_to(prepared[1][rows:rows + CLASSES, :1], (CLASSES, PANEL))
    sums = jnp.concatenate(sums + [panel_sums, count], axis=1)

    start = bits[0] * (rows // 2)
    for level in range(levels):
        group = tokens << level
        size = (rows // 2) >> level
        came_sums = swap(sums, level)
        by_class = sums[:, :cols] - came_sums[:, :cols]
        across = jnp.sum(by_class, axis=0) / group
        down = (sums[0, cols:cols + rows] - came_sums[0, cols:cols + rows]) / 2
        sums = sums + came_sums
        last = level + 1 == levels
        nexts = []
        for chunk in range(CHUNKS):
            mine, came = kept[chunk], sends[chunk]
            along = across[chunk * part:(chunk + 1) * part]
            count_rows = size if last else size // 2

            def merged(bit):
                at = bit * count_rows
                pick = lambda a: lax.dynamic_slice_in_dim(a, at, count_rows, 0)
                rank = lax.dynamic_slice_in_dim(down, start + at, count_rows, 0)
                return pick(mine) + pick(came).astype(jnp.float32) + rank[:, None] * along[None, :]

            if last:
                kept[chunk] = merged(0) / (total - 1)
            else:
                bit = bits[level + 1]
                nexts.append(merged(1 - bit).astype(jnp.bfloat16))
                kept[chunk] = merged(bit)
        if not last:
            start = start + bits[level + 1] * count_rows
            sums, _ = lax.optimization_barrier((sums, sends[-1]))
            sends = [swap(send, level + 1) for send in nexts]

    by_class, count = sums[:, :cols], sums[:, cols + rows:cols + rows + 1]
    mean = jnp.sum(by_class, axis=0, keepdims=True) / total
    cross_cov = (by_class - count * mean) / total
    return jnp.concatenate(kept, axis=1), cross_cov


def solution(mesh):
    in_specs = (P("tok", "feat"), P("tok"))
    out_specs = (P("tok", "feat"), P(None, "feat"))
    return jax.shard_map(body, mesh=mesh, in_specs=in_specs, out_specs=out_specs, check_vma=False)
```

```python
import functools

import jax
import jax.numpy as jnp
from jax import lax
from jax.experimental import pallas as pl
from jax.experimental.pallas import tpu as pltpu
from jax.sharding import PartitionSpec as P

CLASSES = 8
PANEL = 128
PAD = 16
SHIFT_ROWS = 128
CHUNKS = 2
VMEM_LIMIT = 48 * 2**20
PIECES = 2


def orders_of(levels):
    even = list(range(levels))
    odd = list(even)
    for i in range(0, levels - 1, 2):
        odd[i], odd[i + 1] = even[i + 1], even[i]
    return even, odd


def position(block, order):
    pos = 0
    for bit in order:
        pos = pos * 2 + ((block >> bit) & 1)
    return pos


def prepare(orders, meta_ref, pieces, onehot_ref, left, columns, extra_ref):
    tokens = left.shape[1]
    rows = left.shape[0] - PAD
    unit = rows // 2 ** len(orders[0])
    for i, piece in enumerate(pieces):
        size = piece.shape[1]
        raw = piece[...].T
        shift = jnp.mean(raw[:, :SHIFT_ROWS].astype(jnp.float32), axis=1, keepdims=True)
        shift = shift.astype(jnp.bfloat16)
        y = raw - shift
        shift = jnp.broadcast_to(shift.astype(jnp.float32), (size, PANEL))
        first = meta_ref[i]
        for j in range(size // unit):
            block = first + j
            even, odd = (
                sum(((block >> bit) & 1) << k for k, bit in enumerate(reversed(order)))
                for order in orders
            )
            pos = jnp.where(meta_ref[len(pieces) + 1] == 0, even, odd)
            at = pl.ds(pl.multiple_of(pos * unit, unit), unit)
            here = slice(j * unit, (j + 1) * unit)
            left[at, :] = y[here]
            columns[at, :] = shift[here]
    left[rows:, :] = onehot_ref[...]
    shift = columns[:rows, :]
    total = jnp.sum(left[...].astype(jnp.float32), axis=1, keepdims=True)
    columns[...] = jnp.broadcast_to(total, columns.shape)
    extra_ref[...] = jnp.zeros(extra_ref.shape, jnp.float32)
    extra_ref[CLASSES:CLASSES + 1, :rows] = (columns[:rows, :] / tokens + shift).T[:1, :]
    extra_ref[:CLASSES, rows:] = columns[rows:rows + CLASSES, :]


def fetches(chunk, steps, x_hbm, x_vmem, sems):
    tokens, width = x_vmem.shape[1:]
    size = tokens // PIECES
    return [
        [
            pltpu.make_async_copy(
                x_hbm.at[pl.ds(p * size, size), pl.ds((chunk * steps + i) * width, width)],
                x_vmem.at[i, pl.ds(p * size, size), :],
                sems.at[i, p],
            )
            for p in range(PIECES)
        ]
        for i in range(steps)
    ]


def multiply(mine, step, copies, x_vmem, left, columns, send_ref, keep_ref, sums_ref, split):
    tokens = x_vmem.shape[1]
    rows = left.shape[0] - PAD
    half = rows // 2
    for i, copy in enumerate(copies):
        @pl.when(step == i)
        def _(copy=copy):
            for piece in copy:
                piece.wait()

    x = x_vmem[step]
    shift = jnp.mean(x[:SHIFT_ROWS].astype(jnp.float32), axis=0, keepdims=True).astype(jnp.bfloat16)
    out = jnp.dot(left[...], x - shift, preferred_element_type=jnp.float32)
    by_class = out[rows:rows + CLASSES]
    total = jnp.sum(by_class, axis=0, keepdims=True) / tokens
    shift = shift.astype(jnp.float32)
    sums_ref[:CLASSES, :] = by_class + columns[rows:rows + CLASSES, :1] * shift
    sums_ref[CLASSES:, :] = jnp.broadcast_to(total + shift, by_class.shape)
    split[...] = out[:rows] - columns[:rows, :1] * total
    keep_ref[...] = split[pl.ds(pl.multiple_of(mine * half, half), half), :]
    send_ref[...] = split[pl.ds(pl.multiple_of((1 - mine) * half, half), half), :].astype(jnp.bfloat16)


def local_kernel(chunk, steps, orders, n_pieces, meta_ref, x_hbm, *refs):
    step = pl.program_id(0)
    if chunk == 0:
        pieces, refs = refs[:n_pieces], refs[n_pieces:]
        onehot_ref, send_ref, keep_ref, sums_ref, left, columns, extra_ref, split, x_vmem, sems = refs
    else:
        left, columns, send_ref, keep_ref, sums_ref, split, x_vmem, sems = refs
    copies = fetches(chunk, steps, x_hbm, x_vmem, sems)

    @pl.when(step == 0)
    def _():
        for copy in copies:
            for piece in copy:
                piece.start()
        if chunk == 0:
            prepare(orders, meta_ref, pieces, onehot_ref, left, columns, extra_ref)

    multiply(meta_ref[n_pieces], step, copies, x_vmem, left, columns, send_ref, keep_ref, sums_ref, split)


def local_part(chunk, activations, pieces, onehot, meta, orders, rows, prepared=None):
    tokens, cols = activations.shape
    part = cols // CHUNKS
    width = min(512, part)
    steps = part // width
    whole = lambda step, *_: (0, 0)
    column = lambda step, *_: (0, step)
    saved_shape = [
        jax.ShapeDtypeStruct((rows + PAD, tokens), jnp.bfloat16),
        jax.ShapeDtypeStruct((rows + PAD, PANEL), jnp.float32),
    ]
    saved_spec = [pl.BlockSpec(s.shape, whole) for s in saved_shape]
    out_specs = [
        pl.BlockSpec((rows // 2, width), column),
        pl.BlockSpec((rows // 2, width), column),
        pl.BlockSpec((2 * CLASSES, width), column),
    ]
    out_shape = [
        jax.ShapeDtypeStruct((rows // 2, part), jnp.bfloat16),
        jax.ShapeDtypeStruct((rows // 2, part), jnp.float32),
        jax.ShapeDtypeStruct((2 * CLASSES, part), jnp.float32),
    ]
    in_specs = [pl.BlockSpec(memory_space=pl.ANY)]
    if prepared is None:
        in_specs += [pl.BlockSpec((tokens, size), whole) for _, size in pieces]
        in_specs += [pl.BlockSpec((PAD, tokens), whole)]
        out_specs += saved_spec + [pl.BlockSpec((2 * CLASSES, rows + PANEL), whole)]
        out_shape += saved_shape + [jax.ShapeDtypeStruct((2 * CLASSES, rows + PANEL), jnp.float32)]
        args = [piece for piece, _ in pieces] + [onehot]
    else:
        in_specs += saved_spec
        args = list(prepared)
    return pl.pallas_call(
        functools.partial(local_kernel, chunk, steps, orders, len(pieces)),
        grid_spec=pltpu.PrefetchScalarGridSpec(
            num_scalar_prefetch=1,
            grid=(steps,),
            in_specs=in_specs,
            out_specs=out_specs,
            scratch_shapes=[
                pltpu.VMEM((rows, width), jnp.float32),
                pltpu.VMEM((steps, tokens, width), jnp.bfloat16),
                pltpu.SemaphoreType.DMA((steps, PIECES)),
            ],
        ),
        out_shape=out_shape,
        compiler_params=pltpu.CompilerParams(vmem_limit_bytes=VMEM_LIMIT),
        cost_estimate=pl.CostEstimate(
            flops=2 * tokens * part * (rows + PAD),
            bytes_accessed=2 * tokens * part + 6 * (rows // 2) * part,
            transcendentals=0,
        ),
        name="local_sums",
    )(meta, activations, *args)


def after(value, *others):
    return lax.optimization_barrier((value, *others))[0]


def body(activations, labels):
    tokens, cols = activations.shape
    n_tok, n_feat = lax.axis_size("tok"), lax.axis_size("feat")
    levels = n_tok.bit_length() - 1
    assert n_tok == 1 << levels
    rows = PANEL * n_feat
    unit = rows // n_tok
    me, feat = lax.axis_index("tok"), lax.axis_index("feat")
    total = tokens * n_tok
    even, odd = orders_of(levels)
    parity = feat % 2
    bits = [(me >> jnp.where(parity == 0, a, b)) & 1 for a, b in zip(even, odd)]

    def swap(value, level):
        pairs = []
        for i in range(n_tok):
            for f in range(n_feat):
                bit = (even, odd)[f % 2][level % levels]
                pairs.append((i * n_feat + f, (i ^ (1 << bit)) * n_feat + f))
        return lax.ppermute(value, ("tok", "feat"), pairs)

    own = activations[:, :PANEL]
    if n_feat == 2:
        other = lax.ppermute(own, "feat", [(0, 1), (1, 0)])
        pieces = [(activations, PANEL), (other, PANEL)]
        places = [feat * PANEL // unit, (1 - feat) * PANEL // unit]
    else:
        pieces = [(lax.all_gather(own, "feat", axis=1, tiled=True), rows)]
        places = [0]
    meta = jnp.stack(places + [bits[0], parity]).astype(jnp.int32)
    onehot = (labels[None, :] == jnp.arange(PAD, dtype=jnp.int32)[:, None]).astype(jnp.bfloat16)

    sends, kept, sums, prepared = [], [], [], None
    for chunk in range(CHUNKS):
        out = local_part(chunk, activations, pieces, onehot, meta, (even, odd), rows, prepared)
        sends.append(out[0])
        kept.append(out[1])
        sums.append(out[2])
        if chunk == 0:
            prepared, extra = out[3:5], out[5]
    sums = jnp.concatenate(sums + [extra], axis=1)[:CLASSES + 1]

    start = bits[0] * (rows // 2)
    done = None
    for level in range(levels):
        size = (rows // 2) >> level
        last = level + 1 == levels
        came = [swap(send, level) for send in sends]
        came_sums = swap(sums, level + 2)
        for chunk in range(CHUNKS):
            if chunk == CHUNKS - 1:
                came_sums = after(came_sums, done) if done is not None else came_sums
                sums = jnp.concatenate(
                    [sums[:CLASSES] + came_sums[:CLASSES], sums[CLASSES:], came_sums[CLASSES:]], axis=0
                )
                if last:
                    means = sums[CLASSES:]
                    mean = jnp.sum(means, axis=0, keepdims=True) / n_tok
                    away = means - mean
                    place = lax.dynamic_slice_in_dim(away[:, cols:cols + rows], start, unit, 1)
                    between = lax.dot_general(
                        place, away[:, :cols], (((0,), (0,)), ((), ())),
                        precision=lax.Precision.HIGHEST, preferred_element_type=jnp.float32,
                    ) * (tokens / (total - 1))
                    count = sums[:CLASSES, cols + rows:cols + rows + 1]
                    cross_cov = (sums[:CLASSES, :cols] - count * mean[:, :cols]) / total
                    came = [after(c, between, cross_cov) for c in came]
                    break
                done = sums
            if last:
                continue
            mine, other = kept[chunk], came[chunk]
            if done is not None:
                other = after(other, done)
            half = size // 2
            bit = bits[level + 1]

            def merged(bit):
                pick = lambda a: lax.dynamic_slice_in_dim(a, bit * half, half, 0)
                return pick(mine) + pick(other).astype(jnp.float32)

            sends[chunk] = merged(1 - bit).astype(jnp.bfloat16)
            kept[chunk] = merged(bit)
            done = sends[chunk]
        if not last:
            start = start + bits[level + 1] * (size // 2)

    cov_panel = jnp.concatenate(
        [mine + other.astype(jnp.float32) for mine, other in zip(kept, came)], axis=1
    ) / (total - 1) + between
    return cov_panel, cross_cov


def solution(mesh):
    in_specs = (P("tok", "feat"), P("tok"))
    out_specs = (P("tok", "feat"), P(None, "feat"))
    return jax.shard_map(body, mesh=mesh, in_specs=in_specs, out_specs=out_specs, check_vma=False)
```

```python
import functools

import jax
import jax.numpy as jnp
from jax import lax
from jax.experimental import pallas as pl
from jax.experimental.pallas import tpu as pltpu
from jax.sharding import PartitionSpec as P

CLASSES = 8
PANEL = 128
PAD = 16
SHIFT_ROWS = 128
CHUNKS = 2
VMEM_LIMIT = 48 * 2**20
PIECES = 2


def orders_of(levels):
    even = list(range(levels))
    odd = list(even)
    for i in range(0, levels - 1, 2):
        odd[i], odd[i + 1] = even[i + 1], even[i]
    return even, odd


def position(block, order):
    pos = 0
    for bit in order:
        pos = pos * 2 + ((block >> bit) & 1)
    return pos


def prepare(orders, meta_ref, pieces, onehot_ref, left, columns, extra_ref):
    tokens = left.shape[1]
    rows = left.shape[0] - PAD
    unit = rows // 2 ** len(orders[0])
    for i, piece in enumerate(pieces):
        size = piece.shape[1]
        raw = piece[...].T
        shift = jnp.mean(raw[:, :SHIFT_ROWS].astype(jnp.float32), axis=1, keepdims=True)
        shift = shift.astype(jnp.bfloat16)
        y = raw - shift
        shift = jnp.broadcast_to(shift.astype(jnp.float32), (size, PANEL))
        first = meta_ref[i]
        for j in range(size // unit):
            block = first + j
            even, odd = (
                sum(((block >> bit) & 1) << k for k, bit in enumerate(reversed(order)))
                for order in orders
            )
            pos = jnp.where(meta_ref[len(pieces) + 1] == 0, even, odd)
            at = pl.ds(pl.multiple_of(pos * unit, unit), unit)
            here = slice(j * unit, (j + 1) * unit)
            left[at, :] = y[here]
            columns[at, :] = shift[here]
    left[rows:, :] = onehot_ref[...]
    shift = columns[:rows, :]
    total = jnp.sum(left[...].astype(jnp.float32), axis=1, keepdims=True)
    columns[...] = jnp.broadcast_to(total, columns.shape)
    extra_ref[...] = jnp.zeros(extra_ref.shape, jnp.float32)
    extra_ref[:, :PANEL] = columns[rows:rows + CLASSES, :]
    means = columns[:rows, :] / tokens + shift
    for i in range(rows // PANEL):
        extra_ref[i:i + 1, PANEL:] = means[i * PANEL:(i + 1) * PANEL].T[:1, :]


def fetches(chunk, steps, x_hbm, x_vmem, sems):
    tokens, width = x_vmem.shape[1:]
    size = tokens // PIECES
    return [
        [
            pltpu.make_async_copy(
                x_hbm.at[pl.ds(p * size, size), pl.ds((chunk * steps + i) * width, width)],
                x_vmem.at[i, pl.ds(p * size, size), :],
                sems.at[i, p],
            )
            for p in range(PIECES)
        ]
        for i in range(steps)
    ]


def multiply(mine, step, copies, x_vmem, left, columns, send_ref, keep_ref, sums_ref, means_ref, split):
    tokens, width = x_vmem.shape[1:]
    lanes = means_ref.shape[1]
    rows = left.shape[0] - PAD
    half = rows // 2
    for i, copy in enumerate(copies):
        @pl.when(step == i)
        def _(copy=copy):
            for piece in copy:
                piece.wait()

    x = x_vmem[step]
    shift = jnp.mean(x[:SHIFT_ROWS].astype(jnp.float32), axis=0, keepdims=True).astype(jnp.bfloat16)
    out = jnp.dot(left[...], x - shift, preferred_element_type=jnp.float32)
    by_class = out[rows:rows + CLASSES]
    total = jnp.sum(by_class, axis=0, keepdims=True) / tokens
    shift = shift.astype(jnp.float32)
    sums_ref[...] = by_class + columns[rows:rows + CLASSES, :1] * shift
    for i in range(width // lanes):
        means_ref[pl.ds(step * (width // lanes) + i, 1), :] = (total + shift)[:, i * lanes:(i + 1) * lanes]
    split[...] = out[:rows] - columns[:rows, :1] * total
    keep_ref[...] = split[pl.ds(pl.multiple_of(mine * half, half), half), :]
    send_ref[...] = split[pl.ds(pl.multiple_of((1 - mine) * half, half), half), :].astype(jnp.bfloat16)


def local_kernel(chunk, steps, orders, n_pieces, meta_ref, x_hbm, *refs):
    step = pl.program_id(0)
    if chunk == 0:
        pieces, refs = refs[:n_pieces], refs[n_pieces:]
        onehot_ref, send_ref, keep_ref, sums_ref, means_ref, left, columns, extra_ref, split, x_vmem, sems = refs
    else:
        left, columns, send_ref, keep_ref, sums_ref, means_ref, split, x_vmem, sems = refs
    copies = fetches(chunk, steps, x_hbm, x_vmem, sems)

    @pl.when(step == 0)
    def _():
        for copy in copies:
            for piece in copy:
                piece.start()
        if chunk == 0:
            prepare(orders, meta_ref, pieces, onehot_ref, left, columns, extra_ref)

    multiply(
        meta_ref[n_pieces], step, copies, x_vmem, left, columns,
        send_ref, keep_ref, sums_ref, means_ref, split,
    )


def local_part(chunk, activations, pieces, onehot, meta, orders, rows, prepared=None):
    tokens, cols = activations.shape
    part = cols // CHUNKS
    width = min(512, part)
    steps = part // width
    whole = lambda step, *_: (0, 0)
    column = lambda step, *_: (0, step)
    saved_shape = [
        jax.ShapeDtypeStruct((rows + PAD, tokens), jnp.bfloat16),
        jax.ShapeDtypeStruct((rows + PAD, PANEL), jnp.float32),
    ]
    saved_spec = [pl.BlockSpec(s.shape, whole) for s in saved_shape]
    out_specs = [
        pl.BlockSpec((rows // 2, width), column),
        pl.BlockSpec((rows // 2, width), column),
        pl.BlockSpec((CLASSES, width), column),
        pl.BlockSpec((CLASSES // CHUNKS, cols // CLASSES), whole),
    ]
    out_shape = [
        jax.ShapeDtypeStruct((rows // 2, part), jnp.bfloat16),
        jax.ShapeDtypeStruct((rows // 2, part), jnp.float32),
        jax.ShapeDtypeStruct((CLASSES, part), jnp.float32),
        jax.ShapeDtypeStruct((CLASSES // CHUNKS, cols // CLASSES), jnp.float32),
    ]
    in_specs = [pl.BlockSpec(memory_space=pl.ANY)]
    if prepared is None:
        in_specs += [pl.BlockSpec((tokens, size), whole) for _, size in pieces]
        in_specs += [pl.BlockSpec((PAD, tokens), whole)]
        out_specs += saved_spec + [pl.BlockSpec((CLASSES, 2 * PANEL), whole)]
        out_shape += saved_shape + [jax.ShapeDtypeStruct((CLASSES, 2 * PANEL), jnp.float32)]
        args = [piece for piece, _ in pieces] + [onehot]
    else:
        in_specs += saved_spec
        args = list(prepared)
    return pl.pallas_call(
        functools.partial(local_kernel, chunk, steps, orders, len(pieces)),
        grid_spec=pltpu.PrefetchScalarGridSpec(
            num_scalar_prefetch=1,
            grid=(steps,),
            in_specs=in_specs,
            out_specs=out_specs,
            scratch_shapes=[
                pltpu.VMEM((rows, width), jnp.float32),
                pltpu.VMEM((steps, tokens, width), jnp.bfloat16),
                pltpu.SemaphoreType.DMA((steps, PIECES)),
            ],
        ),
        out_shape=out_shape,
        compiler_params=pltpu.CompilerParams(vmem_limit_bytes=VMEM_LIMIT),
        cost_estimate=pl.CostEstimate(
            flops=2 * tokens * part * (rows + PAD),
            bytes_accessed=2 * tokens * part + 6 * (rows // 2) * part,
            transcendentals=0,
        ),
        name="local_sums",
    )(meta, activations, *args)


def after(value, *others):
    return lax.optimization_barrier((value, *others))[0]


def body(activations, labels):
    tokens, cols = activations.shape
    n_tok, n_feat = lax.axis_size("tok"), lax.axis_size("feat")
    levels = n_tok.bit_length() - 1
    assert n_tok == 1 << levels
    rows = PANEL * n_feat
    unit = rows // n_tok
    me, feat = lax.axis_index("tok"), lax.axis_index("feat")
    total = tokens * n_tok
    even, odd = orders_of(levels)
    parity = feat % 2
    bits = [(me >> jnp.where(parity == 0, a, b)) & 1 for a, b in zip(even, odd)]

    def swap(value, level):
        pairs = []
        for i in range(n_tok):
            for f in range(n_feat):
                bit = (even, odd)[f % 2][level % levels]
                pairs.append((i * n_feat + f, (i ^ (1 << bit)) * n_feat + f))
        return lax.ppermute(value, ("tok", "feat"), pairs)

    own = activations[:, :PANEL]
    if n_feat == 2:
        other = lax.ppermute(own, "feat", [(0, 1), (1, 0)])
        pieces = [(activations, PANEL), (other, PANEL)]
        places = [feat * PANEL // unit, (1 - feat) * PANEL // unit]
    else:
        pieces = [(lax.all_gather(own, "feat", axis=1, tiled=True), rows)]
        places = [0]
    meta = jnp.stack(places + [bits[0], parity]).astype(jnp.int32)
    onehot = (labels[None, :] == jnp.arange(PAD, dtype=jnp.int32)[:, None]).astype(jnp.bfloat16)

    sends, kept, sums, means, prepared = [], [], [], [], None
    for chunk in range(CHUNKS):
        out = local_part(chunk, activations, pieces, onehot, meta, (even, odd), rows, prepared)
        sends.append(out[0])
        kept.append(out[1])
        sums.append(out[2])
        means.append(out[3])
        if chunk == 0:
            prepared, extra = out[4:6], out[6]
    head, lanes = cols + PANEL, cols // CLASSES
    sums = jnp.concatenate(
        sums + [extra[:, :PANEL], jnp.concatenate(means, axis=0), extra[:, PANEL:]], axis=1
    )

    start = bits[0] * (rows // 2)
    done = None
    for level in range(levels):
        size = (rows // 2) >> level
        last = level + 1 == levels
        came = [swap(send, level) for send in sends]
        came_sums = swap(sums, level + 2)
        for chunk in range(CHUNKS):
            if chunk == CHUNKS - 1:
                came_sums = after(came_sums, done) if done is not None else came_sums
                sums = jnp.concatenate(
                    [sums[:, :head] + came_sums[:, :head], sums[:, head:], came_sums[:, head:]], axis=1
                )
                if last:
                    means = sums[:, head:].reshape(CLASSES, n_tok, lanes + PANEL)
                    away = (means - jnp.mean(means, axis=1, keepdims=True)).transpose(1, 0, 2)
                    place = lax.dynamic_slice(
                        away, (0, start // PANEL, lanes + start % PANEL), (n_tok, 1, unit)
                    ).reshape(n_tok, unit)
                    between = lax.dot_general(
                        place, away[:, :, :lanes].reshape(n_tok, cols), (((0,), (0,)), ((), ())),
                        precision=lax.Precision.HIGHEST, preferred_element_type=jnp.float32,
                    ) * (tokens / (total - 1))
                    by_class, count = sums[:, :cols], sums[:, cols:cols + 1]
                    cross_cov = (by_class - count * (jnp.sum(by_class, axis=0) / total)) / total
                    came = [after(c, between, cross_cov) for c in came]
                    break
                done = sums
            if last:
                continue
            mine, other = kept[chunk], came[chunk]
            if done is not None:
                other = after(other, done)
            half = size // 2
            bit = bits[level + 1]

            def merged(bit):
                pick = lambda a: lax.dynamic_slice_in_dim(a, bit * half, half, 0)
                return pick(mine) + pick(other).astype(jnp.float32)

            sends[chunk] = merged(1 - bit).astype(jnp.bfloat16)
            kept[chunk] = merged(bit)
            done = sends[chunk]
        if not last:
            start = start + bits[level + 1] * (size // 2)

    cov_panel = jnp.concatenate(
        [mine + other.astype(jnp.float32) for mine, other in zip(kept, came)], axis=1
    ) / (total - 1) + between
    return cov_panel, cross_cov


def solution(mesh):
    in_specs = (P("tok", "feat"), P("tok"))
    out_specs = (P("tok", "feat"), P(None, "feat"))
    return jax.shard_map(body, mesh=mesh, in_specs=in_specs, out_specs=out_specs, check_vma=False)
```

```python
import functools

import jax
import jax.numpy as jnp
from jax import lax
from jax.experimental import pallas as pl
from jax.experimental.pallas import tpu as pltpu
from jax.sharding import PartitionSpec as P

CLASSES = 8
PANEL = 128
PAD = 16
SHIFT_ROWS = 128
LARGE = 1e12
CHUNKS = 2
VMEM_LIMIT = 48 * 2**20
PIECES = 2


def orders_of(levels):
    even = list(range(levels))
    odd = list(even)
    for i in range(0, levels - 1, 2):
        odd[i], odd[i + 1] = even[i + 1], even[i]
    return even, odd


def position(block, order):
    pos = 0
    for bit in order:
        pos = pos * 2 + ((block >> bit) & 1)
    return pos


def prepare(orders, meta_ref, pieces, onehot_ref, left, columns, extra_ref):
    tokens = left.shape[1]
    rows = left.shape[0] - PAD
    unit = rows // 2 ** len(orders[0])
    for i, piece in enumerate(pieces):
        size = piece.shape[1]
        raw = piece[...].T
        shift = jnp.mean(raw[:, :SHIFT_ROWS].astype(jnp.float32), axis=1, keepdims=True)
        shift = shift.astype(jnp.bfloat16)
        y = raw - shift
        shift = jnp.broadcast_to(shift.astype(jnp.float32), (size, PANEL))
        first = meta_ref[i]
        for j in range(size // unit):
            block = first + j
            even, odd = (
                sum(((block >> bit) & 1) << k for k, bit in enumerate(reversed(order)))
                for order in orders
            )
            pos = jnp.where(meta_ref[len(pieces) + 1] == 0, even, odd)
            at = pl.ds(pl.multiple_of(pos * unit, unit), unit)
            here = slice(j * unit, (j + 1) * unit)
            left[at, :] = y[here]
            columns[at, :] = shift[here]
    left[rows:, :] = onehot_ref[...]
    shift = columns[:rows, :]
    total = jnp.sum(left[...].astype(jnp.float32), axis=1, keepdims=True)
    columns[...] = jnp.broadcast_to(total, columns.shape)
    extra_ref[...] = jnp.zeros(extra_ref.shape, jnp.float32)
    extra_ref[:, :PANEL] = columns[rows:rows + CLASSES, :]
    means = columns[:rows, :] / tokens + shift
    for i in range(rows // PANEL):
        extra_ref[i:i + 1, PANEL:] = means[i * PANEL:(i + 1) * PANEL].T[:1, :]


def fetches(chunk, steps, x_hbm, x_vmem, sems):
    tokens, width = x_vmem.shape[1:]
    size = tokens // PIECES
    return [
        [
            pltpu.make_async_copy(
                x_hbm.at[pl.ds(p * size, size), pl.ds((chunk * steps + i) * width, width)],
                x_vmem.at[i, pl.ds(p * size, size), :],
                sems.at[i, p],
            )
            for p in range(PIECES)
        ]
        for i in range(steps)
    ]


def multiply(mine, step, copies, x_vmem, left, columns, send_ref, keep_ref, sums_ref, means_ref, split):
    tokens, width = x_vmem.shape[1:]
    lanes = means_ref.shape[1]
    rows = left.shape[0] - PAD
    half = rows // 2
    for i, copy in enumerate(copies):
        @pl.when(step == i)
        def _(copy=copy):
            for piece in copy:
                piece.wait()

    x = x_vmem[step, :SHIFT_ROWS, :]
    shift = jnp.mean(x.astype(jnp.float32), axis=0, keepdims=True).astype(jnp.bfloat16)
    large = jnp.max(jnp.abs(shift.astype(jnp.float32))) > LARGE

    @pl.when(jnp.logical_not(large))
    def _():
        split[...] = jnp.dot(left[...], x_vmem[step], preferred_element_type=jnp.float32)

    @pl.when(large)
    def _():
        split[...] = jnp.dot(left[...], x_vmem[step] - shift, preferred_element_type=jnp.float32)

    by_class = split[rows:rows + CLASSES, :]
    total = jnp.sum(by_class, axis=0, keepdims=True) / tokens
    shift = jnp.where(large, shift.astype(jnp.float32), 0.0)
    sums_ref[...] = by_class + columns[rows:rows + CLASSES, :1] * shift
    for i in range(width // lanes):
        means_ref[pl.ds(step * (width // lanes) + i, 1), :] = (total + shift)[:, i * lanes:(i + 1) * lanes]
    keep = pl.ds(pl.multiple_of(mine * half, half), half)
    send = pl.ds(pl.multiple_of((1 - mine) * half, half), half)
    keep_ref[...] = split[keep, :] - columns[keep, :1] * total
    send_ref[...] = (split[send, :] - columns[send, :1] * total).astype(jnp.bfloat16)


def local_kernel(chunk, steps, orders, n_pieces, meta_ref, x_hbm, *refs):
    step = pl.program_id(0)
    if chunk == 0:
        pieces, refs = refs[:n_pieces], refs[n_pieces:]
        onehot_ref, send_ref, keep_ref, sums_ref, means_ref, left, columns, extra_ref, split, x_vmem, sems = refs
    else:
        left, columns, send_ref, keep_ref, sums_ref, means_ref, split, x_vmem, sems = refs
    copies = fetches(chunk, steps, x_hbm, x_vmem, sems)

    @pl.when(step == 0)
    def _():
        for copy in copies:
            for piece in copy:
                piece.start()
        if chunk == 0:
            prepare(orders, meta_ref, pieces, onehot_ref, left, columns, extra_ref)

    multiply(
        meta_ref[n_pieces], step, copies, x_vmem, left, columns,
        send_ref, keep_ref, sums_ref, means_ref, split,
    )


def local_part(chunk, activations, pieces, onehot, meta, orders, rows, prepared=None):
    tokens, cols = activations.shape
    part = cols // CHUNKS
    width = min(512, part)
    steps = part // width
    whole = lambda step, *_: (0, 0)
    column = lambda step, *_: (0, step)
    saved_shape = [
        jax.ShapeDtypeStruct((rows + PAD, tokens), jnp.bfloat16),
        jax.ShapeDtypeStruct((rows + PAD, PANEL), jnp.float32),
    ]
    saved_spec = [pl.BlockSpec(s.shape, whole) for s in saved_shape]
    out_specs = [
        pl.BlockSpec((rows // 2, width), column),
        pl.BlockSpec((rows // 2, width), column),
        pl.BlockSpec((CLASSES, width), column),
        pl.BlockSpec((CLASSES // CHUNKS, cols // CLASSES), whole),
    ]
    out_shape = [
        jax.ShapeDtypeStruct((rows // 2, part), jnp.bfloat16),
        jax.ShapeDtypeStruct((rows // 2, part), jnp.float32),
        jax.ShapeDtypeStruct((CLASSES, part), jnp.float32),
        jax.ShapeDtypeStruct((CLASSES // CHUNKS, cols // CLASSES), jnp.float32),
    ]
    in_specs = [pl.BlockSpec(memory_space=pl.ANY)]
    if prepared is None:
        in_specs += [pl.BlockSpec((tokens, size), whole) for _, size in pieces]
        in_specs += [pl.BlockSpec((PAD, tokens), whole)]
        out_specs += saved_spec + [pl.BlockSpec((CLASSES, 2 * PANEL), whole)]
        out_shape += saved_shape + [jax.ShapeDtypeStruct((CLASSES, 2 * PANEL), jnp.float32)]
        args = [piece for piece, _ in pieces] + [onehot]
    else:
        in_specs += saved_spec
        args = list(prepared)
    return pl.pallas_call(
        functools.partial(local_kernel, chunk, steps, orders, len(pieces)),
        grid_spec=pltpu.PrefetchScalarGridSpec(
            num_scalar_prefetch=1,
            grid=(steps,),
            in_specs=in_specs,
            out_specs=out_specs,
            scratch_shapes=[
                pltpu.VMEM((rows + PAD, width), jnp.float32),
                pltpu.VMEM((steps, tokens, width), jnp.bfloat16),
                pltpu.SemaphoreType.DMA((steps, PIECES)),
            ],
        ),
        out_shape=out_shape,
        compiler_params=pltpu.CompilerParams(vmem_limit_bytes=VMEM_LIMIT),
        cost_estimate=pl.CostEstimate(
            flops=2 * tokens * part * (rows + PAD),
            bytes_accessed=2 * tokens * part + 6 * (rows // 2) * part,
            transcendentals=0,
        ),
        name="local_sums",
    )(meta, activations, *args)


def after(value, *others):
    return lax.optimization_barrier((value, *others))[0]


def body(activations, labels):
    tokens, cols = activations.shape
    n_tok, n_feat = lax.axis_size("tok"), lax.axis_size("feat")
    levels = n_tok.bit_length() - 1
    assert n_tok == 1 << levels
    rows = PANEL * n_feat
    unit = rows // n_tok
    me, feat = lax.axis_index("tok"), lax.axis_index("feat")
    total = tokens * n_tok
    even, odd = orders_of(levels)
    parity = feat % 2
    bits = [(me >> jnp.where(parity == 0, a, b)) & 1 for a, b in zip(even, odd)]

    def swap(value, level):
        pairs = []
        for i in range(n_tok):
            for f in range(n_feat):
                bit = (even, odd)[f % 2][level % levels]
                pairs.append((i * n_feat + f, (i ^ (1 << bit)) * n_feat + f))
        return lax.ppermute(value, ("tok", "feat"), pairs)

    own = activations[:, :PANEL]
    if n_feat == 2:
        other = lax.ppermute(own, "feat", [(0, 1), (1, 0)])
        pieces = [(activations, PANEL), (other, PANEL)]
        places = [feat * PANEL // unit, (1 - feat) * PANEL // unit]
    else:
        pieces = [(lax.all_gather(own, "feat", axis=1, tiled=True), rows)]
        places = [0]
    meta = jnp.stack(places + [bits[0], parity]).astype(jnp.int32)
    onehot = (labels[None, :] == jnp.arange(PAD, dtype=jnp.int32)[:, None]).astype(jnp.bfloat16)

    sends, kept, sums, means, prepared = [], [], [], [], None
    for chunk in range(CHUNKS):
        out = local_part(chunk, activations, pieces, onehot, meta, (even, odd), rows, prepared)
        sends.append(out[0])
        kept.append(out[1])
        sums.append(out[2])
        means.append(out[3])
        if chunk == 0:
            prepared, extra = out[4:6], out[6]
    head, lanes = cols + PANEL, cols // CLASSES
    sums = jnp.concatenate(
        sums + [extra[:, :PANEL], jnp.concatenate(means, axis=0), extra[:, PANEL:]], axis=1
    )

    start = bits[0] * (rows // 2)
    done = None
    for level in range(levels):
        size = (rows // 2) >> level
        last = level + 1 == levels
        came = [swap(send, level) for send in sends]
        came_sums = swap(sums, level + 2)
        for chunk in range(CHUNKS):
            if chunk == CHUNKS - 1:
                came_sums = after(came_sums, done) if done is not None else came_sums
                sums = jnp.concatenate(
                    [sums[:, :head] + came_sums[:, :head], sums[:, head:], came_sums[:, head:]], axis=1
                )
                if last:
                    means = sums[:, head:].reshape(CLASSES, n_tok, lanes + PANEL)
                    away = (means - jnp.mean(means, axis=1, keepdims=True)).transpose(1, 0, 2)
                    place = lax.dynamic_slice(
                        away, (0, start // PANEL, lanes + start % PANEL), (n_tok, 1, unit)
                    ).reshape(n_tok, unit)
                    between = lax.dot_general(
                        place, away[:, :, :lanes].reshape(n_tok, cols), (((0,), (0,)), ((), ())),
                        precision=lax.Precision.HIGHEST, preferred_element_type=jnp.float32,
                    ) * (tokens / (total - 1))
                    by_class, count = sums[:, :cols], sums[:, cols:cols + 1]
                    cross_cov = (by_class - count * (jnp.sum(by_class, axis=0) / total)) / total
                    came = [after(c, between, cross_cov) for c in came]
                    break
                done = sums
            if last:
                continue
            mine, other = kept[chunk], came[chunk]
            if done is not None:
                other = after(other, done)
            half = size // 2
            bit = bits[level + 1]

            def merged(bit):
                pick = lambda a: lax.dynamic_slice_in_dim(a, bit * half, half, 0)
                return pick(mine) + pick(other).astype(jnp.float32)

            sends[chunk] = merged(1 - bit).astype(jnp.bfloat16)
            kept[chunk] = merged(bit)
            done = sends[chunk]
        if not last:
            start = start + bits[level + 1] * (size // 2)

    cov_panel = jnp.concatenate(
        [mine + other.astype(jnp.float32) for mine, other in zip(kept, came)], axis=1
    ) / (total - 1) + between
    return cov_panel, cross_cov


def solution(mesh):
    in_specs = (P("tok", "feat"), P("tok"))
    out_specs = (P("tok", "feat"), P(None, "feat"))
    return jax.shard_map(body, mesh=mesh, in_specs=in_specs, out_specs=out_specs, check_vma=False)
```

```python
import functools

import jax
import jax.numpy as jnp
from jax import lax
from jax.experimental import pallas as pl
from jax.experimental.pallas import tpu as pltpu
from jax.sharding import PartitionSpec as P

CLASSES = 8
PANEL = 128
PAD = 16
SHIFT_ROWS = 128
CHUNKS = (4, 4)
VMEM_LIMIT = 48 * 2**20
PIECES = 2


def orders_of(levels):
    even = list(range(levels))
    odd = list(even)
    for i in range(0, levels - 1, 2):
        odd[i], odd[i + 1] = even[i + 1], even[i]
    return even, odd


def position(block, order):
    pos = 0
    for bit in order:
        pos = pos * 2 + ((block >> bit) & 1)
    return pos


def prepare(orders, meta_ref, pieces, onehot_ref, left, columns, extra_ref):
    tokens = left.shape[1]
    rows = left.shape[0] - PAD
    unit = rows // 2 ** len(orders[0])
    for i, piece in enumerate(pieces):
        size = piece.shape[1]
        raw = piece[...].T
        shift = jnp.mean(raw[:, :SHIFT_ROWS].astype(jnp.float32), axis=1, keepdims=True)
        shift = shift.astype(jnp.bfloat16)
        y = raw - shift
        shift = jnp.broadcast_to(shift.astype(jnp.float32), (size, PANEL))
        first = meta_ref[i]
        for j in range(size // unit):
            block = first + j
            even, odd = (
                sum(((block >> bit) & 1) << k for k, bit in enumerate(reversed(order)))
                for order in orders
            )
            pos = jnp.where(meta_ref[len(pieces) + 1] == 0, even, odd)
            at = pl.ds(pl.multiple_of(pos * unit, unit), unit)
            here = slice(j * unit, (j + 1) * unit)
            left[at, :] = y[here]
            columns[at, :] = shift[here]
    left[rows:, :] = onehot_ref[...]
    shift = columns[:rows, :]
    total = jnp.sum(left[...].astype(jnp.float32), axis=1, keepdims=True)
    columns[...] = jnp.broadcast_to(total, columns.shape)
    extra_ref[...] = jnp.zeros(extra_ref.shape, jnp.float32)
    extra_ref[:, :PANEL] = columns[rows:rows + CLASSES, :]
    means = columns[:rows, :] / tokens + shift
    for i in range(rows // PANEL):
        extra_ref[i:i + 1, PANEL:] = means[i * PANEL:(i + 1) * PANEL].T[:1, :]


def local_kernel(first, blocks, orders, n_pieces, meta_ref, x_hbm, *refs):
    if first == 0:
        pieces, refs = refs[:n_pieces], refs[n_pieces:]
        onehot_ref, send_ref, keep_ref, sums_ref, means_ref, left, columns, extra_ref, split, x_vmem, sems = refs
    else:
        left, columns, send_ref, keep_ref, sums_ref, means_ref, split, x_vmem, sems = refs
    tokens, width = x_vmem.shape[1:]
    rows = left.shape[0] - PAD
    half = rows // 2
    size = tokens // PIECES
    copies = [
        [
            pltpu.make_async_copy(
                x_hbm.at[pl.ds(p * size, size), pl.ds((first + i) * width, width)],
                x_vmem.at[i, pl.ds(p * size, size), :],
                sems.at[i, p],
            )
            for p in range(PIECES)
        ]
        for i in range(blocks)
    ]
    for copy in copies:
        for piece in copy:
            piece.start()
    if first == 0:
        prepare(orders, meta_ref, pieces, onehot_ref, left, columns, extra_ref)

    mine = meta_ref[n_pieces]
    keep = pl.ds(pl.multiple_of(mine * half, half), half)
    send = pl.ds(pl.multiple_of((1 - mine) * half, half), half)
    for i, copy in enumerate(copies):
        for piece in copy:
            piece.wait()
        x = x_vmem[i]
        shift = jnp.mean(x[:SHIFT_ROWS].astype(jnp.float32), axis=0, keepdims=True).astype(jnp.bfloat16)
        out = jnp.dot(left[...], x - shift, preferred_element_type=jnp.float32)
        by_class = out[rows:rows + CLASSES]
        total = jnp.sum(by_class, axis=0, keepdims=True) / tokens
        shift = shift.astype(jnp.float32)
        here = slice(i * width, (i + 1) * width)
        sums_ref[:, here] = by_class + columns[rows:rows + CLASSES, :1] * shift
        means_ref[i:i + 1, :] = total + shift
        split[...] = out[:rows] - columns[:rows, :1] * total
        keep_ref[:, here] = split[keep, :]
        send_ref[:, here] = split[send, :].astype(jnp.bfloat16)


def local_part(first, blocks, activations, pieces, onehot, meta, orders, rows, prepared=None):
    tokens, cols = activations.shape
    width = cols // CLASSES
    part = blocks * width
    vmem = pl.BlockSpec(memory_space=pltpu.VMEM)
    out_shape = [
        jax.ShapeDtypeStruct((rows // 2, part), jnp.bfloat16),
        jax.ShapeDtypeStruct((rows // 2, part), jnp.float32),
        jax.ShapeDtypeStruct((CLASSES, part), jnp.float32),
        jax.ShapeDtypeStruct((blocks, width), jnp.float32),
    ]
    if prepared is None:
        out_shape += [
            jax.ShapeDtypeStruct((rows + PAD, tokens), jnp.bfloat16),
            jax.ShapeDtypeStruct((rows + PAD, PANEL), jnp.float32),
            jax.ShapeDtypeStruct((CLASSES, 2 * PANEL), jnp.float32),
        ]
        args = list(pieces) + [onehot]
    else:
        args = list(prepared)
    return pl.pallas_call(
        functools.partial(local_kernel, first, blocks, orders, len(pieces)),
        in_specs=[pl.BlockSpec(memory_space=pltpu.SMEM), pl.BlockSpec(memory_space=pl.ANY)]
        + [vmem] * len(args),
        out_specs=[vmem] * len(out_shape),
        scratch_shapes=[
            pltpu.VMEM((rows, width), jnp.float32),
            pltpu.VMEM((blocks, tokens, width), jnp.bfloat16),
            pltpu.SemaphoreType.DMA((blocks, PIECES)),
        ],
        out_shape=out_shape,
        compiler_params=pltpu.CompilerParams(vmem_limit_bytes=VMEM_LIMIT),
        cost_estimate=pl.CostEstimate(
            flops=2 * tokens * part * (rows + PAD),
            bytes_accessed=2 * tokens * part + 6 * (rows // 2) * part,
            transcendentals=0,
        ),
        name="local_sums",
    )(meta, activations, *args)


def after(value, *others):
    return lax.optimization_barrier((value, *others))[0]


def body(activations, labels):
    tokens, cols = activations.shape
    n_tok, n_feat = lax.axis_size("tok"), lax.axis_size("feat")
    levels = n_tok.bit_length() - 1
    assert n_tok == 1 << levels
    rows = PANEL * n_feat
    unit = rows // n_tok
    me, feat = lax.axis_index("tok"), lax.axis_index("feat")
    total = tokens * n_tok
    even, odd = orders_of(levels)
    parity = feat % 2
    bits = [(me >> jnp.where(parity == 0, a, b)) & 1 for a, b in zip(even, odd)]

    def swap(value, level):
        pairs = []
        for i in range(n_tok):
            for f in range(n_feat):
                bit = (even, odd)[f % 2][level % levels]
                pairs.append((i * n_feat + f, (i ^ (1 << bit)) * n_feat + f))
        return lax.ppermute(value, ("tok", "feat"), pairs)

    own = activations[:, :PANEL]
    if n_feat == 2:
        other = lax.ppermute(own, "feat", [(0, 1), (1, 0)])
        pieces = [own, other]
        places = [feat * PANEL // unit, (1 - feat) * PANEL // unit]
    else:
        pieces = [lax.all_gather(own, "feat", axis=1, tiled=True)]
        places = [0]
    meta = jnp.stack(places + [bits[0], parity]).astype(jnp.int32)
    onehot = (labels[None, :] == jnp.arange(PAD, dtype=jnp.int32)[:, None]).astype(jnp.bfloat16)

    sends, kept, sums, means, prepared = [], [], [], [], None
    for chunk, blocks in enumerate(CHUNKS):
        first = sum(CHUNKS[:chunk])
        out = local_part(first, blocks, activations, pieces, onehot, meta, (even, odd), rows, prepared)
        sends.append(out[0])
        kept.append(out[1])
        sums.append(out[2])
        means.append(out[3])
        if chunk == 0:
            prepared, extra = out[4:6], out[6]
    head, lanes = cols + PANEL, cols // CLASSES
    sums = jnp.concatenate(
        sums + [extra[:, :PANEL], jnp.concatenate(means, axis=0), extra[:, PANEL:]], axis=1
    )

    start = bits[0] * (rows // 2)
    done = None
    for level in range(levels):
        size = (rows // 2) >> level
        last = level + 1 == levels
        came = [swap(send, level) for send in sends]
        came_sums = swap(sums, level + 2)
        for chunk in range(len(CHUNKS)):
            if chunk == len(CHUNKS) - 1:
                came_sums = after(came_sums, done) if done is not None else came_sums
                sums = jnp.concatenate(
                    [sums[:, :head] + came_sums[:, :head], sums[:, head:], came_sums[:, head:]], axis=1
                )
                if last:
                    means = sums[:, head:].reshape(CLASSES, n_tok, lanes + PANEL)
                    away = (means - jnp.mean(means, axis=1, keepdims=True)).transpose(1, 0, 2)
                    place = lax.dynamic_slice(
                        away, (0, start // PANEL, lanes + start % PANEL), (n_tok, 1, unit)
                    ).reshape(n_tok, unit)
                    between = lax.dot_general(
                        place, away[:, :, :lanes].reshape(n_tok, cols), (((0,), (0,)), ((), ())),
                        precision=lax.Precision.HIGHEST, preferred_element_type=jnp.float32,
                    ) * (tokens / (total - 1))
                    by_class, count = sums[:, :cols], sums[:, cols:cols + 1]
                    cross_cov = (by_class - count * (jnp.sum(by_class, axis=0) / total)) / total
                    came = [after(c, between, cross_cov) for c in came]
                    break
                done = sums
            if last:
                continue
            mine, other = kept[chunk], came[chunk]
            if done is not None:
                other = after(other, done)
            half = size // 2
            bit = bits[level + 1]

            def merged(bit):
                pick = lambda a: lax.dynamic_slice_in_dim(a, bit * half, half, 0)
                return pick(mine) + pick(other).astype(jnp.float32)

            sends[chunk] = merged(1 - bit).astype(jnp.bfloat16)
            kept[chunk] = merged(bit)
            done = sends[chunk]
        if not last:
            start = start + bits[level + 1] * (size // 2)

    cov_panel = jnp.concatenate(
        [mine + other.astype(jnp.float32) for mine, other in zip(kept, came)], axis=1
    ) / (total - 1) + between
    return cov_panel, cross_cov


def solution(mesh):
    in_specs = (P("tok", "feat"), P("tok"))
    out_specs = (P("tok", "feat"), P(None, "feat"))
    return jax.shard_map(body, mesh=mesh, in_specs=in_specs, out_specs=out_specs, check_vma=False)
```

```python
import functools

import jax
import jax.numpy as jnp
from jax import lax
from jax.experimental import pallas as pl
from jax.experimental.pallas import tpu as pltpu
from jax.sharding import PartitionSpec as P

CLASSES = 8
PANEL = 128
PAD = 16
SHIFT_ROWS = 128
CHUNKS = (2, 3, 3)
VMEM_LIMIT = 48 * 2**20
PIECES = 2


def orders_of(levels):
    even = list(range(levels))
    odd = list(even)
    for i in range(0, levels - 1, 2):
        odd[i], odd[i + 1] = even[i + 1], even[i]
    return even, odd


def position(block, order):
    pos = 0
    for bit in order:
        pos = pos * 2 + ((block >> bit) & 1)
    return pos


def prepare(orders, meta_ref, pieces, onehot_ref, left, columns, extra_ref):
    tokens = left.shape[1]
    rows = left.shape[0] - PAD
    unit = rows // 2 ** len(orders[0])
    for i, piece in enumerate(pieces):
        size = piece.shape[1]
        raw = piece[...].T
        shift = jnp.mean(raw[:, :SHIFT_ROWS].astype(jnp.float32), axis=1, keepdims=True)
        shift = shift.astype(jnp.bfloat16)
        y = raw - shift
        shift = jnp.broadcast_to(shift.astype(jnp.float32), (size, PANEL))
        first = meta_ref[i]
        for j in range(size // unit):
            block = first + j
            even, odd = (
                sum(((block >> bit) & 1) << k for k, bit in enumerate(reversed(order)))
                for order in orders
            )
            pos = jnp.where(meta_ref[len(pieces) + 1] == 0, even, odd)
            at = pl.ds(pl.multiple_of(pos * unit, unit), unit)
            here = slice(j * unit, (j + 1) * unit)
            left[at, :] = y[here]
            columns[at, :] = shift[here]
    left[rows:, :] = onehot_ref[...]
    shift = columns[:rows, :]
    total = jnp.sum(left[...].astype(jnp.float32), axis=1, keepdims=True)
    columns[...] = jnp.broadcast_to(total, columns.shape)
    extra_ref[...] = jnp.zeros(extra_ref.shape, jnp.float32)
    extra_ref[:, :PANEL] = columns[rows:rows + CLASSES, :]
    means = columns[:rows, :] / tokens + shift
    for i in range(rows // PANEL):
        extra_ref[i:i + 1, PANEL:] = means[i * PANEL:(i + 1) * PANEL].T[:1, :]


def local_kernel(first, blocks, orders, n_pieces, meta_ref, x_hbm, *refs):
    if first == 0:
        pieces, refs = refs[:n_pieces], refs[n_pieces:]
        onehot_ref, send_ref, keep_ref, sums_ref, means_ref, left, columns, extra_ref, split, x_vmem, sems = refs
    else:
        left, columns, send_ref, keep_ref, sums_ref, means_ref, split, x_vmem, sems = refs
    tokens, part = x_vmem.shape
    width = part // blocks
    rows = left.shape[0] - PAD
    half = rows // 2
    size = tokens // PIECES
    copies = [
        pltpu.make_async_copy(
            x_hbm.at[pl.ds(p * size, size), pl.ds(first * width, part)],
            x_vmem.at[pl.ds(p * size, size), :],
            sems.at[p],
        )
        for p in range(PIECES)
    ]
    for copy in copies:
        copy.start()
    if first == 0:
        prepare(orders, meta_ref, pieces, onehot_ref, left, columns, extra_ref)

    mine = meta_ref[n_pieces]
    keep = pl.ds(pl.multiple_of(mine * half, half), half)
    send = pl.ds(pl.multiple_of((1 - mine) * half, half), half)
    shifts = []
    for p, copy in enumerate(copies):
        copy.wait()
        at = slice(p * size, (p + 1) * size)
        for i in range(blocks):
            here = slice(i * width, (i + 1) * width)
            x = x_vmem[at, here]
            if p == 0:
                shift = jnp.mean(x[:SHIFT_ROWS].astype(jnp.float32), axis=0, keepdims=True)
                shifts.append(shift.astype(jnp.bfloat16))
            shift = shifts[i]
            out = jnp.dot(left[:, at], x - shift, preferred_element_type=jnp.float32)
            if p > 0:
                out = split[:, here] + out
            if p + 1 < PIECES:
                split[:, here] = out
                continue
            by_class = out[rows:rows + CLASSES]
            total = jnp.sum(by_class, axis=0, keepdims=True) / tokens
            shift = shift.astype(jnp.float32)
            sums_ref[:, here] = by_class + columns[rows:rows + CLASSES, :1] * shift
            means_ref[i:i + 1, :] = total + shift
            split[:rows, here] = out[:rows] - columns[:rows, :1] * total
            keep_ref[:, here] = split[keep, here]
            send_ref[:, here] = split[send, here].astype(jnp.bfloat16)


def local_part(first, blocks, activations, pieces, onehot, meta, orders, rows, prepared=None):
    tokens, cols = activations.shape
    width = cols // CLASSES
    part = blocks * width
    vmem = pl.BlockSpec(memory_space=pltpu.VMEM)
    out_shape = [
        jax.ShapeDtypeStruct((rows // 2, part), jnp.bfloat16),
        jax.ShapeDtypeStruct((rows // 2, part), jnp.float32),
        jax.ShapeDtypeStruct((CLASSES, part), jnp.float32),
        jax.ShapeDtypeStruct((blocks, width), jnp.float32),
    ]
    if prepared is None:
        out_shape += [
            jax.ShapeDtypeStruct((rows + PAD, tokens), jnp.bfloat16),
            jax.ShapeDtypeStruct((rows + PAD, PANEL), jnp.float32),
            jax.ShapeDtypeStruct((CLASSES, 2 * PANEL), jnp.float32),
        ]
        args = list(pieces) + [onehot]
    else:
        args = list(prepared)
    return pl.pallas_call(
        functools.partial(local_kernel, first, blocks, orders, len(pieces)),
        in_specs=[pl.BlockSpec(memory_space=pltpu.SMEM), pl.BlockSpec(memory_space=pl.ANY)]
        + [vmem] * len(args),
        out_specs=[vmem] * len(out_shape),
        scratch_shapes=[
            pltpu.VMEM((rows + PAD, part), jnp.float32),
            pltpu.VMEM((tokens, part), jnp.bfloat16),
            pltpu.SemaphoreType.DMA((PIECES,)),
        ],
        out_shape=out_shape,
        compiler_params=pltpu.CompilerParams(vmem_limit_bytes=VMEM_LIMIT),
        cost_estimate=pl.CostEstimate(
            flops=2 * tokens * part * (rows + PAD),
            bytes_accessed=2 * tokens * part + 6 * (rows // 2) * part,
            transcendentals=0,
        ),
        name="local_sums",
    )(meta, activations, *args)


def after(value, *others):
    return lax.optimization_barrier((value, *others))[0]


def body(activations, labels):
    tokens, cols = activations.shape
    n_tok, n_feat = lax.axis_size("tok"), lax.axis_size("feat")
    levels = n_tok.bit_length() - 1
    assert n_tok == 1 << levels
    rows = PANEL * n_feat
    unit = rows // n_tok
    me, feat = lax.axis_index("tok"), lax.axis_index("feat")
    total = tokens * n_tok
    even, odd = orders_of(levels)
    parity = feat % 2
    bits = [(me >> jnp.where(parity == 0, a, b)) & 1 for a, b in zip(even, odd)]

    def swap(value, level):
        pairs = []
        for i in range(n_tok):
            for f in range(n_feat):
                bit = (even, odd)[f % 2][level % levels]
                pairs.append((i * n_feat + f, (i ^ (1 << bit)) * n_feat + f))
        return lax.ppermute(value, ("tok", "feat"), pairs)

    own = activations[:, :PANEL]
    if n_feat == 2:
        other = lax.ppermute(own, "feat", [(0, 1), (1, 0)])
        pieces = [own, other]
        places = [feat * PANEL // unit, (1 - feat) * PANEL // unit]
    else:
        pieces = [lax.all_gather(own, "feat", axis=1, tiled=True)]
        places = [0]
    meta = jnp.stack(places + [bits[0], parity]).astype(jnp.int32)
    onehot = (labels[None, :] == jnp.arange(PAD, dtype=jnp.int32)[:, None]).astype(jnp.bfloat16)

    sends, kept, sums, means, prepared = [], [], [], [], None
    for chunk, blocks in enumerate(CHUNKS):
        first = sum(CHUNKS[:chunk])
        out = local_part(first, blocks, activations, pieces, onehot, meta, (even, odd), rows, prepared)
        sends.append(out[0])
        kept.append(out[1])
        sums.append(out[2])
        means.append(out[3])
        if chunk == 0:
            prepared, extra = out[4:6], out[6]
    head, lanes = cols + PANEL, cols // CLASSES
    sums = jnp.concatenate(
        sums + [extra[:, :PANEL], jnp.concatenate(means, axis=0), extra[:, PANEL:]], axis=1
    )

    start = bits[0] * (rows // 2)
    done = None
    for level in range(levels):
        size = (rows // 2) >> level
        last = level + 1 == levels
        came = [swap(send, level) for send in sends]
        came_sums = swap(sums, level + 2)
        for chunk in range(len(CHUNKS)):
            if chunk == len(CHUNKS) - 1:
                came_sums = after(came_sums, done) if done is not None else came_sums
                sums = jnp.concatenate(
                    [sums[:, :head] + came_sums[:, :head], sums[:, head:], came_sums[:, head:]], axis=1
                )
                if last:
                    means = sums[:, head:].reshape(CLASSES, n_tok, lanes + PANEL)
                    away = (means - jnp.mean(means, axis=1, keepdims=True)).transpose(1, 0, 2)
                    place = lax.dynamic_slice(
                        away, (0, start // PANEL, lanes + start % PANEL), (n_tok, 1, unit)
                    ).reshape(n_tok, unit)
                    between = lax.dot_general(
                        place, away[:, :, :lanes].reshape(n_tok, cols), (((0,), (0,)), ((), ())),
                        precision=lax.Precision.HIGHEST, preferred_element_type=jnp.float32,
                    ) * (tokens / (total - 1))
                    by_class, count = sums[:, :cols], sums[:, cols:cols + 1]
                    cross_cov = (by_class - count * (jnp.sum(by_class, axis=0) / total)) / total
                    came = [after(c, between, cross_cov) for c in came]
                    break
                done = sums
            if last:
                continue
            mine, other = kept[chunk], came[chunk]
            if done is not None:
                other = after(other, done)
            half = size // 2
            bit = bits[level + 1]

            def merged(bit):
                pick = lambda a: lax.dynamic_slice_in_dim(a, bit * half, half, 0)
                return pick(mine) + pick(other).astype(jnp.float32)

            sends[chunk] = merged(1 - bit).astype(jnp.bfloat16)
            kept[chunk] = merged(bit)
            done = sends[chunk]
        if not last:
            start = start + bits[level + 1] * (size // 2)

    cov_panel = jnp.concatenate(
        [mine + other.astype(jnp.float32) for mine, other in zip(kept, came)], axis=1
    ) / (total - 1) + between
    return cov_panel, cross_cov


def solution(mesh):
    in_specs = (P("tok", "feat"), P("tok"))
    out_specs = (P("tok", "feat"), P(None, "feat"))
    return jax.shard_map(body, mesh=mesh, in_specs=in_specs, out_specs=out_specs, check_vma=False)
```

```python
import functools

import jax
import jax.numpy as jnp
from jax import lax
from jax.experimental import pallas as pl
from jax.experimental.pallas import tpu as pltpu
from jax.sharding import PartitionSpec as P

CLASSES = 8
PANEL = 128
PAD = 16
SHIFT_ROWS = 128
CHUNKS = (4, 4)
VMEM_LIMIT = 48 * 2**20
PIECES = 2
SUMS = -1


def orders_of(levels):
    even = list(range(levels))
    odd = list(even)
    for i in range(0, levels - 1, 2):
        odd[i], odd[i + 1] = even[i + 1], even[i]
    return even, odd


def position(block, order):
    pos = 0
    for bit in order:
        pos = pos * 2 + ((block >> bit) & 1)
    return pos


def prepare(orders, meta_ref, pieces, onehot_ref, left, columns, extra_ref):
    tokens = left.shape[1]
    rows = left.shape[0] - PAD
    unit = rows // 2 ** len(orders[0])
    for i, piece in enumerate(pieces):
        size = piece.shape[1]
        raw = piece[...].T
        shift = jnp.mean(raw[:, :SHIFT_ROWS].astype(jnp.float32), axis=1, keepdims=True)
        shift = shift.astype(jnp.bfloat16)
        y = raw - shift
        shift = jnp.broadcast_to(shift.astype(jnp.float32), (size, PANEL))
        first = meta_ref[i]
        for j in range(size // unit):
            block = first + j
            even, odd = (
                sum(((block >> bit) & 1) << k for k, bit in enumerate(reversed(order)))
                for order in orders
            )
            pos = jnp.where(meta_ref[len(pieces) + 1] == 0, even, odd)
            at = pl.ds(pl.multiple_of(pos * unit, unit), unit)
            here = slice(j * unit, (j + 1) * unit)
            left[at, :] = y[here]
            columns[at, :] = shift[here]
    left[rows:, :] = onehot_ref[...]
    shift = columns[:rows, :]
    total = jnp.sum(left[...].astype(jnp.float32), axis=1, keepdims=True)
    columns[...] = jnp.broadcast_to(total, columns.shape)
    extra_ref[...] = jnp.zeros(extra_ref.shape, jnp.float32)
    extra_ref[:, :PANEL] = columns[rows:rows + CLASSES, :]
    means = columns[:rows, :] / tokens + shift
    for i in range(rows // PANEL):
        extra_ref[i:i + 1, PANEL:] = means[i * PANEL:(i + 1) * PANEL].T[:1, :]


def local_kernel(first, blocks, orders, n_pieces, meta_ref, x_hbm, *refs):
    if first == 0:
        pieces, refs = refs[:n_pieces], refs[n_pieces:]
        onehot_ref, send_ref, keep_ref, sums_ref, means_ref, left, columns, extra_ref, split, x_vmem, sems = refs
    else:
        left, columns, send_ref, keep_ref, sums_ref, means_ref, split, x_vmem, sems = refs
    tokens, width = x_vmem.shape[1:]
    rows = left.shape[0] - PAD
    half = rows // 2
    size = tokens // PIECES
    copies = [
        [
            pltpu.make_async_copy(
                x_hbm.at[pl.ds(p * size, size), pl.ds((first + i) * width, width)],
                x_vmem.at[i, pl.ds(p * size, size), :],
                sems.at[i, p],
            )
            for p in range(PIECES)
        ]
        for i in range(blocks)
    ]
    for copy in copies:
        for piece in copy:
            piece.start()
    if first == 0:
        prepare(orders, meta_ref, pieces, onehot_ref, left, columns, extra_ref)

    mine = meta_ref[n_pieces]
    keep = pl.ds(pl.multiple_of(mine * half, half), half)
    send = pl.ds(pl.multiple_of((1 - mine) * half, half), half)
    for i, copy in enumerate(copies):
        for piece in copy:
            piece.wait()
        x = x_vmem[i]
        shift = jnp.mean(x[:SHIFT_ROWS].astype(jnp.float32), axis=0, keepdims=True).astype(jnp.bfloat16)
        out = jnp.dot(left[...], x - shift, preferred_element_type=jnp.float32)
        by_class = out[rows:rows + CLASSES]
        total = jnp.sum(by_class, axis=0, keepdims=True) / tokens
        shift = shift.astype(jnp.float32)
        here = slice(i * width, (i + 1) * width)
        sums_ref[:, here] = by_class + columns[rows:rows + CLASSES, :1] * shift
        means_ref[i:i + 1, :] = total + shift
        split[...] = out[:rows] - columns[:rows, :1] * total
        keep_ref[:, here] = split[keep, :]
        send_ref[:, here] = split[send, :].astype(jnp.bfloat16)


def local_part(first, blocks, activations, pieces, onehot, meta, orders, rows, prepared=None):
    tokens, cols = activations.shape
    width = cols // CLASSES
    part = blocks * width
    vmem = pl.BlockSpec(memory_space=pltpu.VMEM)
    out_shape = [
        jax.ShapeDtypeStruct((rows // 2, part), jnp.bfloat16),
        jax.ShapeDtypeStruct((rows // 2, part), jnp.float32),
        jax.ShapeDtypeStruct((CLASSES, part), jnp.float32),
        jax.ShapeDtypeStruct((blocks, width), jnp.float32),
    ]
    if prepared is None:
        out_shape += [
            jax.ShapeDtypeStruct((rows + PAD, tokens), jnp.bfloat16),
            jax.ShapeDtypeStruct((rows + PAD, PANEL), jnp.float32),
            jax.ShapeDtypeStruct((CLASSES, 2 * PANEL), jnp.float32),
        ]
        args = list(pieces) + [onehot]
    else:
        args = list(prepared)
    return pl.pallas_call(
        functools.partial(local_kernel, first, blocks, orders, len(pieces)),
        in_specs=[pl.BlockSpec(memory_space=pltpu.SMEM), pl.BlockSpec(memory_space=pl.ANY)]
        + [vmem] * len(args),
        out_specs=[vmem] * len(out_shape),
        scratch_shapes=[
            pltpu.VMEM((rows, width), jnp.float32),
            pltpu.VMEM((blocks, tokens, width), jnp.bfloat16),
            pltpu.SemaphoreType.DMA((blocks, PIECES)),
        ],
        out_shape=out_shape,
        compiler_params=pltpu.CompilerParams(vmem_limit_bytes=VMEM_LIMIT),
        cost_estimate=pl.CostEstimate(
            flops=2 * tokens * part * (rows + PAD),
            bytes_accessed=2 * tokens * part + 6 * (rows // 2) * part,
            transcendentals=0,
        ),
        name="local_sums",
    )(meta, activations, *args)


def after(value, *others):
    return lax.optimization_barrier((value, *others))[0]


def body(activations, labels):
    tokens, cols = activations.shape
    n_tok, n_feat = lax.axis_size("tok"), lax.axis_size("feat")
    levels = n_tok.bit_length() - 1
    assert n_tok == 1 << levels
    rows = PANEL * n_feat
    unit = rows // n_tok
    me, feat = lax.axis_index("tok"), lax.axis_index("feat")
    total = tokens * n_tok
    even, odd = orders_of(levels)
    parity = feat % 2
    bits = [(me >> jnp.where(parity == 0, a, b)) & 1 for a, b in zip(even, odd)]

    def swap(value, level):
        pairs = []
        for i in range(n_tok):
            for f in range(n_feat):
                bit = (even, odd)[f % 2][level % levels]
                pairs.append((i * n_feat + f, (i ^ (1 << bit)) * n_feat + f))
        return lax.ppermute(value, ("tok", "feat"), pairs)

    own = activations[:, :PANEL]
    if n_feat == 2:
        other = lax.ppermute(own, "feat", [(0, 1), (1, 0)])
        pieces = [own, other]
        places = [feat * PANEL // unit, (1 - feat) * PANEL // unit]
    else:
        pieces = [lax.all_gather(own, "feat", axis=1, tiled=True)]
        places = [0]
    meta = jnp.stack(places + [bits[0], parity]).astype(jnp.int32)
    onehot = (labels[None, :] == jnp.arange(PAD, dtype=jnp.int32)[:, None]).astype(jnp.bfloat16)

    sends, kept, sums, means, prepared = [], [], [], [], None
    for chunk, blocks in enumerate(CHUNKS):
        first = sum(CHUNKS[:chunk])
        out = local_part(first, blocks, activations, pieces, onehot, meta, (even, odd), rows, prepared)
        sends.append(out[0])
        kept.append(out[1])
        sums.append(out[2])
        means.append(out[3])
        if chunk == 0:
            prepared, extra = out[4:6], out[6]
    head, lanes = cols + PANEL, cols // CLASSES
    sums = jnp.concatenate(
        sums + [extra[:, :PANEL], jnp.concatenate(means, axis=0), extra[:, PANEL:]], axis=1
    )

    start = bits[0] * (rows // 2)
    done = None
    for level in range(levels):
        size = (rows // 2) >> level
        last = level + 1 == levels
        came = [swap(send, level) for send in sends]
        came_sums = swap(sums, level + 2)
        turns = list(range(len(CHUNKS)))
        turns.insert(len(turns) if level == 1 else len(turns) - 1, SUMS)
        for turn in turns:
            if turn == SUMS:
                came_sums = after(came_sums, done)
                sums = jnp.concatenate(
                    [sums[:, :head] + came_sums[:, :head], sums[:, head:], came_sums[:, head:]], axis=1
                )
                if last:
                    means = sums[:, head:].reshape(CLASSES, n_tok, lanes + PANEL)
                    away = (means - jnp.mean(means, axis=1, keepdims=True)).transpose(1, 0, 2)
                    place = lax.dynamic_slice(
                        away, (0, start // PANEL, lanes + start % PANEL), (n_tok, 1, unit)
                    ).reshape(n_tok, unit)
                    between = lax.dot_general(
                        place, away[:, :, :lanes].reshape(n_tok, cols), (((0,), (0,)), ((), ())),
                        precision=lax.Precision.HIGHEST, preferred_element_type=jnp.float32,
                    ) * (tokens / (total - 1))
                    by_class, count = sums[:, :cols], sums[:, cols:cols + 1]
                    cross_cov = (by_class - count * (jnp.sum(by_class, axis=0) / total)) / total
                    came = [after(c, between, cross_cov) for c in came]
                    break
                done = sums
                continue
            if last:
                continue
            mine, other = kept[turn], came[turn]
            if done is not None:
                other = after(other, done)
            half = size // 2
            bit = bits[level + 1]

            def merged(bit):
                pick = lambda a: lax.dynamic_slice_in_dim(a, bit * half, half, 0)
                return pick(mine) + pick(other).astype(jnp.float32)

            sends[turn] = merged(1 - bit).astype(jnp.bfloat16)
            kept[turn] = merged(bit)
            done = sends[turn]
        if not last:
            start = start + bits[level + 1] * (size // 2)

    cov_panel = jnp.concatenate(
        [mine + other.astype(jnp.float32) for mine, other in zip(kept, came)], axis=1
    ) / (total - 1) + between
    return cov_panel, cross_cov


def solution(mesh):
    in_specs = (P("tok", "feat"), P("tok"))
    out_specs = (P("tok", "feat"), P(None, "feat"))
    return jax.shard_map(body, mesh=mesh, in_specs=in_specs, out_specs=out_specs, check_vma=False)
```

```python
import functools

import jax
import jax.numpy as jnp
from jax import lax
from jax.experimental import pallas as pl
from jax.experimental.pallas import tpu as pltpu
from jax.sharding import PartitionSpec as P

CLASSES = 8
PANEL = 128
PAD = 16
SHIFT_ROWS = 128
CHUNKS = (4, 4)
VMEM_LIMIT = 48 * 2**20
PIECES = 2
SUMS = -1


def orders_of(levels):
    even = list(range(levels))
    odd = list(even)
    for i in range(0, levels - 1, 2):
        odd[i], odd[i + 1] = even[i + 1], even[i]
    return even, odd


def position(block, order):
    pos = 0
    for bit in order:
        pos = pos * 2 + ((block >> bit) & 1)
    return pos


def prepare(orders, meta_ref, pieces, onehot_ref, left, columns, extra_ref):
    tokens = left.shape[1]
    rows = left.shape[0] - PAD
    unit = rows // 2 ** len(orders[0])
    for i, piece in enumerate(pieces):
        size = piece.shape[1]
        raw = piece[...].T
        shift = jnp.mean(raw[:, :SHIFT_ROWS].astype(jnp.float32), axis=1, keepdims=True)
        shift = shift.astype(jnp.bfloat16)
        y = raw - shift
        shift = jnp.broadcast_to(shift.astype(jnp.float32), (size, PANEL))
        first = meta_ref[i]
        for j in range(size // unit):
            block = first + j
            even, odd = (
                sum(((block >> bit) & 1) << k for k, bit in enumerate(reversed(order)))
                for order in orders
            )
            pos = jnp.where(meta_ref[len(pieces) + 1] == 0, even, odd)
            at = pl.ds(pl.multiple_of(pos * unit, unit), unit)
            here = slice(j * unit, (j + 1) * unit)
            left[at, :] = y[here]
            columns[at, :] = shift[here]
    left[rows:, :] = onehot_ref[...]
    shift = columns[:rows, :]
    total = jnp.sum(left[...].astype(jnp.float32), axis=1, keepdims=True)
    columns[...] = jnp.broadcast_to(total, columns.shape)
    extra_ref[...] = jnp.zeros(extra_ref.shape, jnp.float32)
    extra_ref[:, :PANEL] = columns[rows:rows + CLASSES, :]
    means = columns[:rows, :] / tokens + shift
    for i in range(rows // PANEL):
        extra_ref[i:i + 1, PANEL:] = means[i * PANEL:(i + 1) * PANEL].T[:1, :]


def local_kernel(first, blocks, orders, n_pieces, meta_ref, x_hbm, *refs):
    if first == 0:
        pieces, refs = refs[:n_pieces], refs[n_pieces:]
        onehot_ref, send_ref, keep_ref, sums_ref, means_ref, left, columns, extra_ref, split, x_vmem, sems = refs
    else:
        left, columns, send_ref, keep_ref, sums_ref, means_ref, split, x_vmem, sems = refs
    tokens, width = x_vmem.shape[1:]
    rows = left.shape[0] - PAD
    half = rows // 2
    size = tokens // PIECES
    copies = [
        [
            pltpu.make_async_copy(
                x_hbm.at[pl.ds(p * size, size), pl.ds((first + i) * width, width)],
                x_vmem.at[i, pl.ds(p * size, size), :],
                sems.at[i, p],
            )
            for p in range(PIECES)
        ]
        for i in range(blocks)
    ]
    for copy in copies:
        for piece in copy:
            piece.start()
    if first == 0:
        prepare(orders, meta_ref, pieces, onehot_ref, left, columns, extra_ref)

    mine = meta_ref[n_pieces]
    keep = pl.ds(pl.multiple_of(mine * half, half), half)
    send = pl.ds(pl.multiple_of((1 - mine) * half, half), half)
    for i, copy in enumerate(copies):
        for piece in copy:
            piece.wait()
        x = x_vmem[i]
        shift = jnp.mean(x[:SHIFT_ROWS].astype(jnp.float32), axis=0, keepdims=True).astype(jnp.bfloat16)
        out = jnp.dot(left[...], x - shift, preferred_element_type=jnp.float32)
        by_class = out[rows:rows + CLASSES]
        total = jnp.sum(by_class, axis=0, keepdims=True) / tokens
        shift = shift.astype(jnp.float32)
        here = slice(i * width, (i + 1) * width)
        sums_ref[:, here] = by_class + columns[rows:rows + CLASSES, :1] * shift
        means_ref[i:i + 1, :] = total + shift
        split[...] = out[:rows] - columns[:rows, :1] * total
        keep_ref[:, here] = split[keep, :]
        send_ref[:, here] = split[send, :].astype(jnp.bfloat16)


def local_part(first, blocks, activations, pieces, onehot, meta, orders, rows, prepared=None):
    tokens, cols = activations.shape
    width = cols // CLASSES
    part = blocks * width
    vmem = pl.BlockSpec(memory_space=pltpu.VMEM)
    out_shape = [
        jax.ShapeDtypeStruct((rows // 2, part), jnp.bfloat16),
        jax.ShapeDtypeStruct((rows // 2, part), jnp.float32),
        jax.ShapeDtypeStruct((CLASSES, part), jnp.float32),
        jax.ShapeDtypeStruct((blocks, width), jnp.float32),
    ]
    if prepared is None:
        out_shape += [
            jax.ShapeDtypeStruct((rows + PAD, tokens), jnp.bfloat16),
            jax.ShapeDtypeStruct((rows + PAD, PANEL), jnp.float32),
            jax.ShapeDtypeStruct((CLASSES, 2 * PANEL), jnp.float32),
        ]
        args = list(pieces) + [onehot]
    else:
        args = list(prepared)
    return pl.pallas_call(
        functools.partial(local_kernel, first, blocks, orders, len(pieces)),
        in_specs=[pl.BlockSpec(memory_space=pltpu.SMEM), pl.BlockSpec(memory_space=pl.ANY)]
        + [vmem] * len(args),
        out_specs=[vmem] * len(out_shape),
        scratch_shapes=[
            pltpu.VMEM((rows, width), jnp.float32),
            pltpu.VMEM((blocks, tokens, width), jnp.bfloat16),
            pltpu.SemaphoreType.DMA((blocks, PIECES)),
        ],
        out_shape=out_shape,
        compiler_params=pltpu.CompilerParams(vmem_limit_bytes=VMEM_LIMIT),
        cost_estimate=pl.CostEstimate(
            flops=2 * tokens * part * (rows + PAD),
            bytes_accessed=2 * tokens * part + 6 * (rows // 2) * part,
            transcendentals=0,
        ),
        name="local_sums",
    )(meta, activations, *args)


def after(value, *others):
    return lax.optimization_barrier((value, *others))[0]


def body(activations, labels):
    tokens, cols = activations.shape
    n_tok, n_feat = lax.axis_size("tok"), lax.axis_size("feat")
    levels = n_tok.bit_length() - 1
    assert n_tok == 1 << levels
    rows = PANEL * n_feat
    unit = rows // n_tok
    me, feat = lax.axis_index("tok"), lax.axis_index("feat")
    total = tokens * n_tok
    even, odd = orders_of(levels)
    parity = feat % 2
    bits = [(me >> jnp.where(parity == 0, a, b)) & 1 for a, b in zip(even, odd)]

    def swap(value, level):
        pairs = []
        for i in range(n_tok):
            for f in range(n_feat):
                bit = (even, odd)[f % 2][level % levels]
                pairs.append((i * n_feat + f, (i ^ (1 << bit)) * n_feat + f))
        return lax.ppermute(value, ("tok", "feat"), pairs)

    own = activations[:, :PANEL]
    if n_feat == 2:
        other = lax.ppermute(own, "feat", [(0, 1), (1, 0)])
        pieces = [own, other]
        places = [feat * PANEL // unit, (1 - feat) * PANEL // unit]
    else:
        pieces = [lax.all_gather(own, "feat", axis=1, tiled=True)]
        places = [0]
    meta = jnp.stack(places + [bits[0], parity]).astype(jnp.int32)
    onehot = (labels[None, :] == jnp.arange(PAD, dtype=jnp.int32)[:, None]).astype(jnp.bfloat16)

    sends, kept, sums, means, prepared = [], [], [], [], None
    for chunk, blocks in enumerate(CHUNKS):
        first = sum(CHUNKS[:chunk])
        out = local_part(first, blocks, activations, pieces, onehot, meta, (even, odd), rows, prepared)
        sends.append(out[0])
        kept.append(out[1])
        sums.append(out[2])
        means.append(out[3])
        if chunk == 0:
            prepared, extra = out[4:6], out[6]
    head, lanes = cols + PANEL, cols // CLASSES
    sums = jnp.concatenate(
        sums + [extra[:, :PANEL], jnp.concatenate(means, axis=0), extra[:, PANEL:]], axis=1
    )

    start = bits[0] * (rows // 2)
    done = None
    for level in range(levels):
        size = (rows // 2) >> level
        last = level + 1 == levels
        came = [swap(send, level) for send in sends]
        came_sums = swap(sums, level + 2)
        turns = list(range(len(CHUNKS)))
        turns.insert(len(turns) - 1, SUMS)
        for turn in turns:
            if turn == SUMS:
                came_sums = after(came_sums, done) if done is not None else came_sums
                sums = jnp.concatenate(
                    [sums[:, :head] + came_sums[:, :head], sums[:, head:], came_sums[:, head:]], axis=1
                )
                if last:
                    means = sums[:, head:].reshape(CLASSES, n_tok, lanes + PANEL)
                    away = (means - jnp.mean(means, axis=1, keepdims=True)).transpose(1, 0, 2)
                    place = lax.dynamic_slice(
                        away, (0, start // PANEL, lanes + start % PANEL), (n_tok, 1, unit)
                    ).reshape(n_tok, unit)
                    between = lax.dot_general(
                        place, away[:, :, :lanes].reshape(n_tok, cols), (((0,), (0,)), ((), ())),
                        precision=lax.Precision.HIGHEST, preferred_element_type=jnp.float32,
                    ) * (tokens / (total - 1))
                    by_class, count = sums[:, :cols], sums[:, cols:cols + 1]
                    cross_cov = (by_class - count * (jnp.sum(by_class, axis=0) / total)) / total
                    came = [after(c, between, cross_cov) for c in came]
                    break
                done = sums
                continue
            if last:
                continue
            mine, other = kept[turn], came[turn]
            if done is not None:
                other = after(other, done)
            half = size // 2
            bit = bits[level + 1]

            def merged(bit):
                pick = lambda a: lax.dynamic_slice_in_dim(a, bit * half, half, 0)
                return pick(mine) + pick(other).astype(jnp.float32)

            sends[turn] = merged(1 - bit).astype(jnp.bfloat16)
            kept[turn] = merged(bit)
            done = sends[turn]
        if level == 1:
            sums = after(sums, sends[-1])
        if not last:
            start = start + bits[level + 1] * (size // 2)

    cov_panel = jnp.concatenate(
        [mine + other.astype(jnp.float32) for mine, other in zip(kept, came)], axis=1
    ) / (total - 1) + between
    return cov_panel, cross_cov


def solution(mesh):
    in_specs = (P("tok", "feat"), P("tok"))
    out_specs = (P("tok", "feat"), P(None, "feat"))
    return jax.shard_map(body, mesh=mesh, in_specs=in_specs, out_specs=out_specs, check_vma=False)
```

```python
import functools

import jax
import jax.numpy as jnp
from jax import lax
from jax.experimental import pallas as pl
from jax.experimental.pallas import tpu as pltpu
from jax.sharding import PartitionSpec as P

CLASSES = 8
PANEL = 128
PAD = 16
SHIFT_ROWS = 128
CHUNKS = (5, 3)
VMEM_LIMIT = 48 * 2**20
PIECES = 2


def orders_of(levels):
    even = list(range(levels))
    odd = list(even)
    for i in range(0, levels - 1, 2):
        odd[i], odd[i + 1] = even[i + 1], even[i]
    return even, odd


def position(block, order):
    pos = 0
    for bit in order:
        pos = pos * 2 + ((block >> bit) & 1)
    return pos


def prepare(orders, meta_ref, pieces, onehot_ref, left, columns, extra_ref):
    tokens = left.shape[1]
    rows = left.shape[0] - PAD
    unit = rows // 2 ** len(orders[0])
    for i, piece in enumerate(pieces):
        size = piece.shape[1]
        raw = piece[...].T
        shift = jnp.mean(raw[:, :SHIFT_ROWS].astype(jnp.float32), axis=1, keepdims=True)
        shift = shift.astype(jnp.bfloat16)
        y = raw - shift
        shift = jnp.broadcast_to(shift.astype(jnp.float32), (size, PANEL))
        first = meta_ref[i]
        for j in range(size // unit):
            block = first + j
            even, odd = (
                sum(((block >> bit) & 1) << k for k, bit in enumerate(reversed(order)))
                for order in orders
            )
            pos = jnp.where(meta_ref[len(pieces) + 1] == 0, even, odd)
            at = pl.ds(pl.multiple_of(pos * unit, unit), unit)
            here = slice(j * unit, (j + 1) * unit)
            left[at, :] = y[here]
            columns[at, :] = shift[here]
    left[rows:, :] = onehot_ref[...]
    shift = columns[:rows, :]
    total = jnp.sum(left[...].astype(jnp.float32), axis=1, keepdims=True)
    columns[...] = jnp.broadcast_to(total, columns.shape)
    extra_ref[...] = jnp.zeros(extra_ref.shape, jnp.float32)
    extra_ref[:, :PANEL] = columns[rows:rows + CLASSES, :]
    means = columns[:rows, :] / tokens + shift
    for i in range(rows // PANEL):
        extra_ref[i:i + 1, PANEL:] = means[i * PANEL:(i + 1) * PANEL].T[:1, :]


def local_kernel(first, blocks, orders, n_pieces, meta_ref, x_hbm, *refs):
    if first == 0:
        pieces, refs = refs[:n_pieces], refs[n_pieces:]
        onehot_ref, send_ref, keep_ref, sums_ref, means_ref, left, columns, extra_ref, split, x_vmem, sems = refs
    else:
        left, columns, send_ref, keep_ref, sums_ref, means_ref, split, x_vmem, sems = refs
    tokens, width = x_vmem.shape[1:]
    rows = left.shape[0] - PAD
    half = rows // 2
    size = tokens // PIECES
    copies = [
        [
            pltpu.make_async_copy(
                x_hbm.at[pl.ds(p * size, size), pl.ds((first + i) * width, width)],
                x_vmem.at[i, pl.ds(p * size, size), :],
                sems.at[i, p],
            )
            for p in range(PIECES)
        ]
        for i in range(blocks)
    ]
    for copy in copies:
        for piece in copy:
            piece.start()
    if first == 0:
        prepare(orders, meta_ref, pieces, onehot_ref, left, columns, extra_ref)

    mine = meta_ref[n_pieces]
    keep = pl.ds(pl.multiple_of(mine * half, half), half)
    send = pl.ds(pl.multiple_of((1 - mine) * half, half), half)
    for i, copy in enumerate(copies):
        for piece in copy:
            piece.wait()
        x = x_vmem[i]
        shift = jnp.mean(x[:SHIFT_ROWS].astype(jnp.float32), axis=0, keepdims=True).astype(jnp.bfloat16)
        out = jnp.dot(left[...], x - shift, preferred_element_type=jnp.float32)
        by_class = out[rows:rows + CLASSES]
        total = jnp.sum(by_class, axis=0, keepdims=True) / tokens
        shift = shift.astype(jnp.float32)
        here = slice(i * width, (i + 1) * width)
        sums_ref[:, here] = by_class + columns[rows:rows + CLASSES, :1] * shift
        means_ref[i:i + 1, :] = total + shift
        split[...] = out[:rows] - columns[:rows, :1] * total
        keep_ref[:, here] = split[keep, :]
        send_ref[:, here] = split[send, :].astype(jnp.bfloat16)


def local_part(first, blocks, activations, pieces, onehot, meta, orders, rows, prepared=None):
    tokens, cols = activations.shape
    width = cols // CLASSES
    part = blocks * width
    vmem = pl.BlockSpec(memory_space=pltpu.VMEM)
    out_shape = [
        jax.ShapeDtypeStruct((rows // 2, part), jnp.bfloat16),
        jax.ShapeDtypeStruct((rows // 2, part), jnp.float32),
        jax.ShapeDtypeStruct((CLASSES, part), jnp.float32),
        jax.ShapeDtypeStruct((blocks, width), jnp.float32),
    ]
    if prepared is None:
        out_shape += [
            jax.ShapeDtypeStruct((rows + PAD, tokens), jnp.bfloat16),
            jax.ShapeDtypeStruct((rows + PAD, PANEL), jnp.float32),
            jax.ShapeDtypeStruct((CLASSES, 2 * PANEL), jnp.float32),
        ]
        args = list(pieces) + [onehot]
    else:
        args = list(prepared)
    return pl.pallas_call(
        functools.partial(local_kernel, first, blocks, orders, len(pieces)),
        in_specs=[pl.BlockSpec(memory_space=pltpu.SMEM), pl.BlockSpec(memory_space=pl.ANY)]
        + [vmem] * len(args),
        out_specs=[vmem] * len(out_shape),
        scratch_shapes=[
            pltpu.VMEM((rows, width), jnp.float32),
            pltpu.VMEM((blocks, tokens, width), jnp.bfloat16),
            pltpu.SemaphoreType.DMA((blocks, PIECES)),
        ],
        out_shape=out_shape,
        compiler_params=pltpu.CompilerParams(vmem_limit_bytes=VMEM_LIMIT),
        cost_estimate=pl.CostEstimate(
            flops=2 * tokens * part * (rows + PAD),
            bytes_accessed=2 * tokens * part + 6 * (rows // 2) * part,
            transcendentals=0,
        ),
        name="local_sums",
    )(meta, activations, *args)


def after(value, *others):
    return lax.optimization_barrier((value, *others))[0]


def body(activations, labels):
    tokens, cols = activations.shape
    n_tok, n_feat = lax.axis_size("tok"), lax.axis_size("feat")
    levels = n_tok.bit_length() - 1
    assert n_tok == 1 << levels
    rows = PANEL * n_feat
    unit = rows // n_tok
    me, feat = lax.axis_index("tok"), lax.axis_index("feat")
    total = tokens * n_tok
    even, odd = orders_of(levels)
    parity = feat % 2
    bits = [(me >> jnp.where(parity == 0, a, b)) & 1 for a, b in zip(even, odd)]

    def swap(value, level):
        pairs = []
        for i in range(n_tok):
            for f in range(n_feat):
                bit = (even, odd)[f % 2][level % levels]
                pairs.append((i * n_feat + f, (i ^ (1 << bit)) * n_feat + f))
        return lax.ppermute(value, ("tok", "feat"), pairs)

    own = activations[:, :PANEL]
    if n_feat == 2:
        other = lax.ppermute(own, "feat", [(0, 1), (1, 0)])
        pieces = [own, other]
        places = [feat * PANEL // unit, (1 - feat) * PANEL // unit]
    else:
        pieces = [lax.all_gather(own, "feat", axis=1, tiled=True)]
        places = [0]
    meta = jnp.stack(places + [bits[0], parity]).astype(jnp.int32)
    onehot = (labels[None, :] == jnp.arange(PAD, dtype=jnp.int32)[:, None]).astype(jnp.bfloat16)

    sends, kept, sums, means, prepared = [], [], [], [], None
    for chunk, blocks in enumerate(CHUNKS):
        first = sum(CHUNKS[:chunk])
        out = local_part(first, blocks, activations, pieces, onehot, meta, (even, odd), rows, prepared)
        sends.append(out[0])
        kept.append(out[1])
        sums.append(out[2])
        means.append(out[3])
        if chunk == 0:
            prepared, extra = out[4:6], out[6]
    head, lanes = cols + PANEL, cols // CLASSES
    sums = jnp.concatenate(
        sums + [extra[:, :PANEL], jnp.concatenate(means, axis=0), extra[:, PANEL:]], axis=1
    )

    start = bits[0] * (rows // 2)
    done = None
    for level in range(levels):
        size = (rows // 2) >> level
        last = level + 1 == levels
        came = [swap(send, level) for send in sends]
        came_sums = swap(sums, level + 2)
        for chunk in range(len(CHUNKS)):
            if chunk == len(CHUNKS) - 1:
                came_sums = after(came_sums, done) if done is not None else came_sums
                sums = jnp.concatenate(
                    [sums[:, :head] + came_sums[:, :head], sums[:, head:], came_sums[:, head:]], axis=1
                )
                if last:
                    means = sums[:, head:].reshape(CLASSES, n_tok, lanes + PANEL)
                    away = (means - jnp.mean(means, axis=1, keepdims=True)).transpose(1, 0, 2)
                    place = lax.dynamic_slice(
                        away, (0, start // PANEL, lanes + start % PANEL), (n_tok, 1, unit)
                    ).reshape(n_tok, unit)
                    between = lax.dot_general(
                        place, away[:, :, :lanes].reshape(n_tok, cols), (((0,), (0,)), ((), ())),
                        precision=lax.Precision.HIGHEST, preferred_element_type=jnp.float32,
                    ) * (tokens / (total - 1))
                    by_class, count = sums[:, :cols], sums[:, cols:cols + 1]
                    cross_cov = (by_class - count * (jnp.sum(by_class, axis=0) / total)) / total
                    came = [after(c, between, cross_cov) for c in came]
                    break
                done = sums
            if last:
                continue
            mine, other = kept[chunk], came[chunk]
            if done is not None:
                other = after(other, done)
            half = size // 2
            bit = bits[level + 1]

            def merged(bit):
                pick = lambda a: lax.dynamic_slice_in_dim(a, bit * half, half, 0)
                return pick(mine) + pick(other).astype(jnp.float32)

            sends[chunk] = merged(1 - bit).astype(jnp.bfloat16)
            kept[chunk] = merged(bit)
            done = sends[chunk]
        if not last:
            start = start + bits[level + 1] * (size // 2)

    cov_panel = jnp.concatenate(
        [mine + other.astype(jnp.float32) for mine, other in zip(kept, came)], axis=1
    ) / (total - 1) + between
    return cov_panel, cross_cov


def solution(mesh):
    in_specs = (P("tok", "feat"), P("tok"))
    out_specs = (P("tok", "feat"), P(None, "feat"))
    return jax.shard_map(body, mesh=mesh, in_specs=in_specs, out_specs=out_specs, check_vma=False)
```

```python
import functools

import jax
import jax.numpy as jnp
from jax import lax
from jax.experimental import pallas as pl
from jax.experimental.pallas import tpu as pltpu
from jax.sharding import PartitionSpec as P

CLASSES = 8
PANEL = 128
PAD = 16
SHIFT_ROWS = 128
CHUNKS = (5, 3)
VMEM_LIMIT = 48 * 2**20
PIECES = 2
SUMS = -1


def orders_of(levels):
    even = list(range(levels))
    odd = list(even)
    for i in range(0, levels - 1, 2):
        odd[i], odd[i + 1] = even[i + 1], even[i]
    return even, odd


def position(block, order):
    pos = 0
    for bit in order:
        pos = pos * 2 + ((block >> bit) & 1)
    return pos


def prepare(orders, meta_ref, pieces, onehot_ref, left, columns, extra_ref):
    tokens = left.shape[1]
    rows = left.shape[0] - PAD
    unit = rows // 2 ** len(orders[0])
    for i, piece in enumerate(pieces):
        size = piece.shape[1]
        raw = piece[...].T
        shift = jnp.mean(raw[:, :SHIFT_ROWS].astype(jnp.float32), axis=1, keepdims=True)
        shift = shift.astype(jnp.bfloat16)
        y = raw - shift
        shift = jnp.broadcast_to(shift.astype(jnp.float32), (size, PANEL))
        first = meta_ref[i]
        for j in range(size // unit):
            block = first + j
            even, odd = (
                sum(((block >> bit) & 1) << k for k, bit in enumerate(reversed(order)))
                for order in orders
            )
            pos = jnp.where(meta_ref[len(pieces) + 1] == 0, even, odd)
            at = pl.ds(pl.multiple_of(pos * unit, unit), unit)
            here = slice(j * unit, (j + 1) * unit)
            left[at, :] = y[here]
            columns[at, :] = shift[here]
    left[rows:, :] = onehot_ref[...]
    shift = columns[:rows, :]
    total = jnp.sum(left[...].astype(jnp.float32), axis=1, keepdims=True)
    columns[...] = jnp.broadcast_to(total, columns.shape)
    extra_ref[...] = jnp.zeros(extra_ref.shape, jnp.float32)
    extra_ref[:, :PANEL] = columns[rows:rows + CLASSES, :]
    means = columns[:rows, :] / tokens + shift
    for i in range(rows // PANEL):
        extra_ref[i:i + 1, PANEL:] = means[i * PANEL:(i + 1) * PANEL].T[:1, :]


def local_kernel(first, blocks, orders, n_pieces, meta_ref, x_hbm, *refs):
    if first == 0:
        pieces, refs = refs[:n_pieces], refs[n_pieces:]
        onehot_ref, send_ref, keep_ref, sums_ref, means_ref, left, columns, extra_ref, split, x_vmem, sems = refs
    else:
        left, columns, send_ref, keep_ref, sums_ref, means_ref, split, x_vmem, sems = refs
    tokens, width = x_vmem.shape[1:]
    rows = left.shape[0] - PAD
    half = rows // 2
    size = tokens // PIECES
    copies = [
        [
            pltpu.make_async_copy(
                x_hbm.at[pl.ds(p * size, size), pl.ds((first + i) * width, width)],
                x_vmem.at[i, pl.ds(p * size, size), :],
                sems.at[i, p],
            )
            for p in range(PIECES)
        ]
        for i in range(blocks)
    ]
    for copy in copies:
        for piece in copy:
            piece.start()
    if first == 0:
        prepare(orders, meta_ref, pieces, onehot_ref, left, columns, extra_ref)

    mine = meta_ref[n_pieces]
    keep = pl.ds(pl.multiple_of(mine * half, half), half)
    send = pl.ds(pl.multiple_of((1 - mine) * half, half), half)
    for i, copy in enumerate(copies):
        for piece in copy:
            piece.wait()
        x = x_vmem[i]
        shift = jnp.mean(x[:SHIFT_ROWS].astype(jnp.float32), axis=0, keepdims=True).astype(jnp.bfloat16)
        out = jnp.dot(left[...], x - shift, preferred_element_type=jnp.float32)
        by_class = out[rows:rows + CLASSES]
        total = jnp.sum(by_class, axis=0, keepdims=True) / tokens
        shift = shift.astype(jnp.float32)
        here = slice(i * width, (i + 1) * width)
        sums_ref[:, here] = by_class + columns[rows:rows + CLASSES, :1] * shift
        means_ref[i:i + 1, :] = total + shift
        split[...] = out[:rows] - columns[:rows, :1] * total
        keep_ref[:, here] = split[keep, :]
        send_ref[:, here] = split[send, :].astype(jnp.bfloat16)


def local_part(first, blocks, activations, pieces, onehot, meta, orders, rows, prepared=None):
    tokens, cols = activations.shape
    width = cols // CLASSES
    part = blocks * width
    vmem = pl.BlockSpec(memory_space=pltpu.VMEM)
    out_shape = [
        jax.ShapeDtypeStruct((rows // 2, part), jnp.bfloat16),
        jax.ShapeDtypeStruct((rows // 2, part), jnp.float32),
        jax.ShapeDtypeStruct((CLASSES, part), jnp.float32),
        jax.ShapeDtypeStruct((blocks, width), jnp.float32),
    ]
    if prepared is None:
        out_shape += [
            jax.ShapeDtypeStruct((rows + PAD, tokens), jnp.bfloat16),
            jax.ShapeDtypeStruct((rows + PAD, PANEL), jnp.float32),
            jax.ShapeDtypeStruct((CLASSES, 2 * PANEL), jnp.float32),
        ]
        args = list(pieces) + [onehot]
    else:
        args = list(prepared)
    return pl.pallas_call(
        functools.partial(local_kernel, first, blocks, orders, len(pieces)),
        in_specs=[pl.BlockSpec(memory_space=pltpu.SMEM), pl.BlockSpec(memory_space=pl.ANY)]
        + [vmem] * len(args),
        out_specs=[vmem] * len(out_shape),
        scratch_shapes=[
            pltpu.VMEM((rows, width), jnp.float32),
            pltpu.VMEM((blocks, tokens, width), jnp.bfloat16),
            pltpu.SemaphoreType.DMA((blocks, PIECES)),
        ],
        out_shape=out_shape,
        compiler_params=pltpu.CompilerParams(vmem_limit_bytes=VMEM_LIMIT),
        cost_estimate=pl.CostEstimate(
            flops=2 * tokens * part * (rows + PAD),
            bytes_accessed=2 * tokens * part + 6 * (rows // 2) * part,
            transcendentals=0,
        ),
        name="local_sums",
    )(meta, activations, *args)


def after(value, *others):
    return lax.optimization_barrier((value, *others))[0]


def body(activations, labels):
    tokens, cols = activations.shape
    n_tok, n_feat = lax.axis_size("tok"), lax.axis_size("feat")
    levels = n_tok.bit_length() - 1
    assert n_tok == 1 << levels
    rows = PANEL * n_feat
    unit = rows // n_tok
    me, feat = lax.axis_index("tok"), lax.axis_index("feat")
    total = tokens * n_tok
    even, odd = orders_of(levels)
    parity = feat % 2
    bits = [(me >> jnp.where(parity == 0, a, b)) & 1 for a, b in zip(even, odd)]

    def swap(value, level):
        pairs = []
        for i in range(n_tok):
            for f in range(n_feat):
                bit = (even, odd)[f % 2][level]
                pairs.append((i * n_feat + f, (i ^ (1 << bit)) * n_feat + f))
        return lax.ppermute(value, ("tok", "feat"), pairs)

    own = activations[:, :PANEL]
    if n_feat == 2:
        other = lax.ppermute(own, "feat", [(0, 1), (1, 0)])
        pieces = [own, other]
        places = [feat * PANEL // unit, (1 - feat) * PANEL // unit]
    else:
        pieces = [lax.all_gather(own, "feat", axis=1, tiled=True)]
        places = [0]
    meta = jnp.stack(places + [bits[0], parity]).astype(jnp.int32)
    onehot = (labels[None, :] == jnp.arange(PAD, dtype=jnp.int32)[:, None]).astype(jnp.bfloat16)

    sends, kept, sums, means, prepared = [], [], [], [], None
    for chunk, blocks in enumerate(CHUNKS):
        first = sum(CHUNKS[:chunk])
        out = local_part(first, blocks, activations, pieces, onehot, meta, (even, odd), rows, prepared)
        sends.append(out[0])
        kept.append(out[1])
        sums.append(out[2])
        means.append(out[3])
        if chunk == 0:
            prepared, extra = out[4:6], out[6]
    head, lanes = cols + PANEL, cols // CLASSES
    sums = jnp.concatenate(
        sums + [extra[:, :PANEL], jnp.concatenate(means, axis=0), extra[:, PANEL:]], axis=1
    )

    start = sum(bit * (rows >> (k + 1)) for k, bit in enumerate(bits))
    last = len(CHUNKS) - 1
    turns = []
    for level in range(levels - 1):
        turns += [(chunk, level) for chunk in range(last)]
        turns.insert(len(turns) - (level == 1), (SUMS, level))
        turns += [(last, level)]
    turns += [(SUMS, levels - 1)]

    came = [swap(send, 0) for send in sends]
    route = list(range(2, levels)) + [1, 0]
    came_sums = swap(sums, route[0])
    done = ()
    for chunk, level in turns:
        if chunk == SUMS:
            other = after(came_sums, *done)
            sums = jnp.concatenate([sums[:, :head] + other[:, :head], sums[:, head:], other[:, head:]], axis=1)
            if level + 1 < levels:
                came_sums = swap(sums, route[level + 1])
            done = (sums,)
        else:
            mine, other = kept[chunk], after(came[chunk], *done)
            half = mine.shape[0] // 2
            bit = bits[level + 1]

            def merged(bit):
                pick = lambda a: lax.dynamic_slice_in_dim(a, bit * half, half, 0)
                return pick(mine) + pick(other).astype(jnp.float32)

            send = merged(1 - bit).astype(jnp.bfloat16)
            kept[chunk] = merged(bit)
            came[chunk] = swap(send, level + 1)
            done = (send,)

    means = sums[:, head:].reshape(CLASSES, n_tok, lanes + PANEL)
    away = (means - jnp.mean(means, axis=1, keepdims=True)).transpose(1, 0, 2)
    place = lax.dynamic_slice(
        away, (0, start // PANEL, lanes + start % PANEL), (n_tok, 1, unit)
    ).reshape(n_tok, unit)
    between = lax.dot_general(
        place, away[:, :, :lanes].reshape(n_tok, cols), (((0,), (0,)), ((), ())),
        precision=lax.Precision.HIGHEST, preferred_element_type=jnp.float32,
    ) * (tokens / (total - 1))
    by_class, count = sums[:, :cols], sums[:, cols:cols + 1]
    cross_cov = (by_class - count * (jnp.sum(by_class, axis=0) / total)) / total
    came = [after(c, between, cross_cov) for c in came]
    cov_panel = jnp.concatenate(
        [mine + other.astype(jnp.float32) for mine, other in zip(kept, came)], axis=1
    ) / (total - 1) + between
    return cov_panel, cross_cov


def solution(mesh):
    in_specs = (P("tok", "feat"), P("tok"))
    out_specs = (P("tok", "feat"), P(None, "feat"))
    return jax.shard_map(body, mesh=mesh, in_specs=in_specs, out_specs=out_specs, check_vma=False)
```

```python
import functools

import jax
import jax.numpy as jnp
from jax import lax
from jax.experimental import pallas as pl
from jax.experimental.pallas import tpu as pltpu
from jax.sharding import PartitionSpec as P

CLASSES = 8
PANEL = 128
PAD = 16
SHIFT_ROWS = 128
CHUNKS = (5, 3)
VMEM_LIMIT = 48 * 2**20
PIECES = 2
SUMS = -1


def orders_of(levels):
    even = list(range(levels))
    odd = list(even)
    for i in range(0, levels - 1, 2):
        odd[i], odd[i + 1] = even[i + 1], even[i]
    return even, odd


def position(block, order):
    pos = 0
    for bit in order:
        pos = pos * 2 + ((block >> bit) & 1)
    return pos


def prepare(orders, meta_ref, pieces, onehot_ref, left, columns, extra_ref):
    tokens = left.shape[1]
    rows = left.shape[0] - PAD
    unit = rows // 2 ** len(orders[0])
    for i, piece in enumerate(pieces):
        size = piece.shape[1]
        raw = piece[...].T
        shift = jnp.mean(raw[:, :SHIFT_ROWS].astype(jnp.float32), axis=1, keepdims=True)
        shift = shift.astype(jnp.bfloat16)
        y = raw - shift
        shift = jnp.broadcast_to(shift.astype(jnp.float32), (size, PANEL))
        first = meta_ref[i]
        for j in range(size // unit):
            block = first + j
            even, odd = (
                sum(((block >> bit) & 1) << k for k, bit in enumerate(reversed(order)))
                for order in orders
            )
            pos = jnp.where(meta_ref[len(pieces) + 1] == 0, even, odd)
            at = pl.ds(pl.multiple_of(pos * unit, unit), unit)
            here = slice(j * unit, (j + 1) * unit)
            left[at, :] = y[here]
            columns[at, :] = shift[here]
    left[rows:, :] = onehot_ref[...]
    shift = columns[:rows, :]
    total = jnp.sum(left[...].astype(jnp.float32), axis=1, keepdims=True)
    columns[...] = jnp.broadcast_to(total, columns.shape)
    extra_ref[...] = jnp.zeros(extra_ref.shape, jnp.float32)
    extra_ref[:, :PANEL] = columns[rows:rows + CLASSES, :]
    means = columns[:rows, :] / tokens + shift
    for i in range(rows // PANEL):
        extra_ref[i:i + 1, PANEL:] = means[i * PANEL:(i + 1) * PANEL].T[:1, :]


def local_kernel(first, blocks, orders, n_pieces, meta_ref, x_hbm, *refs):
    if first == 0:
        pieces, refs = refs[:n_pieces], refs[n_pieces:]
        onehot_ref, send_ref, keep_ref, sums_ref, means_ref, left, columns, extra_ref, split, x_vmem, sems = refs
    else:
        left, columns, send_ref, keep_ref, sums_ref, means_ref, split, x_vmem, sems = refs
    tokens, width = x_vmem.shape[1:]
    rows = left.shape[0] - PAD
    half = rows // 2
    size = tokens // PIECES
    copies = [
        [
            pltpu.make_async_copy(
                x_hbm.at[pl.ds(p * size, size), pl.ds((first + i) * width, width)],
                x_vmem.at[i, pl.ds(p * size, size), :],
                sems.at[i, p],
            )
            for p in range(PIECES)
        ]
        for i in range(blocks)
    ]
    for copy in copies:
        for piece in copy:
            piece.start()
    if first == 0:
        prepare(orders, meta_ref, pieces, onehot_ref, left, columns, extra_ref)

    mine = meta_ref[n_pieces]
    keep = pl.ds(pl.multiple_of(mine * half, half), half)
    send = pl.ds(pl.multiple_of((1 - mine) * half, half), half)
    for i, copy in enumerate(copies):
        for piece in copy:
            piece.wait()
        x = x_vmem[i]
        shift = jnp.mean(x[:SHIFT_ROWS].astype(jnp.float32), axis=0, keepdims=True).astype(jnp.bfloat16)
        out = jnp.dot(left[...], x - shift, preferred_element_type=jnp.float32)
        by_class = out[rows:rows + CLASSES]
        total = jnp.sum(by_class, axis=0, keepdims=True) / tokens
        shift = shift.astype(jnp.float32)
        here = slice(i * width, (i + 1) * width)
        sums_ref[:, here] = by_class + columns[rows:rows + CLASSES, :1] * shift
        means_ref[i:i + 1, :] = total + shift
        split[...] = out[:rows] - columns[:rows, :1] * total
        keep_ref[:, here] = split[keep, :]
        send_ref[:, here] = split[send, :].astype(jnp.bfloat16)


def local_part(first, blocks, activations, pieces, onehot, meta, orders, rows, prepared=None):
    tokens, cols = activations.shape
    width = cols // CLASSES
    part = blocks * width
    vmem = pl.BlockSpec(memory_space=pltpu.VMEM)
    out_shape = [
        jax.ShapeDtypeStruct((rows // 2, part), jnp.bfloat16),
        jax.ShapeDtypeStruct((rows // 2, part), jnp.float32),
        jax.ShapeDtypeStruct((CLASSES, part), jnp.float32),
        jax.ShapeDtypeStruct((blocks, width), jnp.float32),
    ]
    if prepared is None:
        out_shape += [
            jax.ShapeDtypeStruct((rows + PAD, tokens), jnp.bfloat16),
            jax.ShapeDtypeStruct((rows + PAD, PANEL), jnp.float32),
            jax.ShapeDtypeStruct((CLASSES, 2 * PANEL), jnp.float32),
        ]
        args = list(pieces) + [onehot]
    else:
        args = list(prepared)
    return pl.pallas_call(
        functools.partial(local_kernel, first, blocks, orders, len(pieces)),
        in_specs=[pl.BlockSpec(memory_space=pltpu.SMEM), pl.BlockSpec(memory_space=pl.ANY)]
        + [vmem] * len(args),
        out_specs=[vmem] * len(out_shape),
        scratch_shapes=[
            pltpu.VMEM((rows, width), jnp.float32),
            pltpu.VMEM((blocks, tokens, width), jnp.bfloat16),
            pltpu.SemaphoreType.DMA((blocks, PIECES)),
        ],
        out_shape=out_shape,
        compiler_params=pltpu.CompilerParams(vmem_limit_bytes=VMEM_LIMIT),
        cost_estimate=pl.CostEstimate(
            flops=2 * tokens * part * (rows + PAD),
            bytes_accessed=2 * tokens * part + 6 * (rows // 2) * part,
            transcendentals=0,
        ),
        name="local_sums",
    )(meta, activations, *args)


def after(value, *others):
    return lax.optimization_barrier((value, *others))[0]


def body(activations, labels):
    tokens, cols = activations.shape
    n_tok, n_feat = lax.axis_size("tok"), lax.axis_size("feat")
    levels = n_tok.bit_length() - 1
    assert n_tok == 1 << levels
    rows = PANEL * n_feat
    unit = rows // n_tok
    me, feat = lax.axis_index("tok"), lax.axis_index("feat")
    total = tokens * n_tok
    even, odd = orders_of(levels)
    parity = feat % 2
    bits = [(me >> jnp.where(parity == 0, a, b)) & 1 for a, b in zip(even, odd)]

    def swap(value, level):
        pairs = []
        for i in range(n_tok):
            for f in range(n_feat):
                bit = (even, odd)[f % 2][level]
                pairs.append((i * n_feat + f, (i ^ (1 << bit)) * n_feat + f))
        return lax.ppermute(value, ("tok", "feat"), pairs)

    own = activations[:, :PANEL]
    if n_feat == 2:
        other = lax.ppermute(own, "feat", [(0, 1), (1, 0)])
        pieces = [own, other]
        places = [feat * PANEL // unit, (1 - feat) * PANEL // unit]
    else:
        pieces = [lax.all_gather(own, "feat", axis=1, tiled=True)]
        places = [0]
    meta = jnp.stack(places + [bits[0], parity]).astype(jnp.int32)
    onehot = (labels[None, :] == jnp.arange(PAD, dtype=jnp.int32)[:, None]).astype(jnp.bfloat16)

    sends, kept, sums, means, prepared = [], [], [], [], None
    for chunk, blocks in enumerate(CHUNKS):
        first = sum(CHUNKS[:chunk])
        out = local_part(first, blocks, activations, pieces, onehot, meta, (even, odd), rows, prepared)
        sends.append(out[0])
        kept.append(out[1])
        sums.append(out[2])
        means.append(out[3])
        if chunk == 0:
            prepared, extra = out[4:6], out[6]
    head, lanes = cols + PANEL, cols // CLASSES
    sums = jnp.concatenate(
        sums + [extra[:, :PANEL], jnp.concatenate(means, axis=0), extra[:, PANEL:]], axis=1
    )

    start = sum(bit * (rows >> (k + 1)) for k, bit in enumerate(bits))
    last = len(CHUNKS) - 1
    turns = []
    for level in range(levels - 1):
        turns += [(chunk, level) for chunk in range(last)]
        turns.insert(len(turns) - (level == 2), (SUMS, level))
        turns += [(last, level)]
    turns += [(SUMS, levels - 1)]

    came = [swap(send, 0) for send in sends]
    route = list(range(2, levels)) + [1, 0]
    came_sums = swap(sums, route[0])
    done = ()
    for chunk, level in turns:
        if chunk == SUMS:
            other = after(came_sums, *done)
            sums = jnp.concatenate([sums[:, :head] + other[:, :head], sums[:, head:], other[:, head:]], axis=1)
            if level + 1 < levels:
                came_sums = swap(sums, route[level + 1])
            done = (sums,)
        else:
            mine, other = kept[chunk], after(came[chunk], *done)
            half = mine.shape[0] // 2
            bit = bits[level + 1]

            def merged(bit):
                pick = lambda a: lax.dynamic_slice_in_dim(a, bit * half, half, 0)
                return pick(mine) + pick(other).astype(jnp.float32)

            send = merged(1 - bit).astype(jnp.bfloat16)
            kept[chunk] = merged(bit)
            came[chunk] = swap(send, level + 1)
            done = (send,)

    means = sums[:, head:].reshape(CLASSES, n_tok, lanes + PANEL)
    away = (means - jnp.mean(means, axis=1, keepdims=True)).transpose(1, 0, 2)
    place = lax.dynamic_slice(
        away, (0, start // PANEL, lanes + start % PANEL), (n_tok, 1, unit)
    ).reshape(n_tok, unit)
    between = lax.dot_general(
        place, away[:, :, :lanes].reshape(n_tok, cols), (((0,), (0,)), ((), ())),
        precision=lax.Precision.HIGHEST, preferred_element_type=jnp.float32,
    ) * (tokens / (total - 1))
    by_class, count = sums[:, :cols], sums[:, cols:cols + 1]
    cross_cov = (by_class - count * (jnp.sum(by_class, axis=0) / total)) / total
    came = [after(c, between, cross_cov) for c in came]
    cov_panel = jnp.concatenate(
        [mine + other.astype(jnp.float32) for mine, other in zip(kept, came)], axis=1
    ) / (total - 1) + between
    return cov_panel, cross_cov


def solution(mesh):
    in_specs = (P("tok", "feat"), P("tok"))
    out_specs = (P("tok", "feat"), P(None, "feat"))
    return jax.shard_map(body, mesh=mesh, in_specs=in_specs, out_specs=out_specs, check_vma=False)
```

```python
import functools

import jax
import jax.numpy as jnp
from jax import lax
from jax.experimental import pallas as pl
from jax.experimental.pallas import tpu as pltpu
from jax.sharding import PartitionSpec as P

CLASSES = 8
PANEL = 128
PAD = 16
SHIFT_ROWS = 128
CHUNKS = (5, 3)
VMEM_LIMIT = 48 * 2**20
PIECES = 2
SUMS = -1


def orders_of(levels):
    even = list(range(levels))
    odd = list(even)
    for i in range(0, levels - 1, 2):
        odd[i], odd[i + 1] = even[i + 1], even[i]
    return even, odd


def position(block, order):
    pos = 0
    for bit in order:
        pos = pos * 2 + ((block >> bit) & 1)
    return pos


def prepare(orders, meta_ref, pieces, onehot_ref, left, columns, extra_ref):
    tokens = left.shape[1]
    rows = left.shape[0] - PAD
    unit = rows // 2 ** len(orders[0])
    for i, piece in enumerate(pieces):
        size = piece.shape[1]
        raw = piece[...].T
        shift = jnp.mean(raw[:, :SHIFT_ROWS].astype(jnp.float32), axis=1, keepdims=True)
        shift = shift.astype(jnp.bfloat16)
        y = raw - shift
        shift = jnp.broadcast_to(shift.astype(jnp.float32), (size, PANEL))
        first = meta_ref[i]
        for j in range(size // unit):
            block = first + j
            even, odd = (
                sum(((block >> bit) & 1) << k for k, bit in enumerate(reversed(order)))
                for order in orders
            )
            pos = jnp.where(meta_ref[len(pieces) + 1] == 0, even, odd)
            at = pl.ds(pl.multiple_of(pos * unit, unit), unit)
            here = slice(j * unit, (j + 1) * unit)
            left[at, :] = y[here]
            columns[at, :] = shift[here]
    left[rows:, :] = onehot_ref[...]
    shift = columns[:rows, :]
    total = jnp.sum(left[...].astype(jnp.float32), axis=1, keepdims=True)
    columns[...] = jnp.broadcast_to(total, columns.shape)
    extra_ref[...] = jnp.zeros(extra_ref.shape, jnp.float32)
    extra_ref[:, :PANEL] = columns[rows:rows + CLASSES, :]
    means = columns[:rows, :] / tokens + shift
    for i in range(rows // PANEL):
        extra_ref[i:i + 1, PANEL:] = means[i * PANEL:(i + 1) * PANEL].T[:1, :]


def local_kernel(first, blocks, orders, n_pieces, meta_ref, x_hbm, *refs):
    if first == 0:
        pieces, refs = refs[:n_pieces], refs[n_pieces:]
        onehot_ref, send_ref, keep_ref, sums_ref, means_ref, left, columns, extra_ref, split, x_vmem, sems = refs
    else:
        left, columns, send_ref, keep_ref, sums_ref, means_ref, split, x_vmem, sems = refs
    tokens, width = x_vmem.shape[1:]
    rows = left.shape[0] - PAD
    half = rows // 2
    size = tokens // PIECES
    copies = [
        [
            pltpu.make_async_copy(
                x_hbm.at[pl.ds(p * size, size), pl.ds((first + i) * width, width)],
                x_vmem.at[i, pl.ds(p * size, size), :],
                sems.at[i, p],
            )
            for p in range(PIECES)
        ]
        for i in range(blocks)
    ]
    for copy in copies:
        for piece in copy:
            piece.start()
    if first == 0:
        prepare(orders, meta_ref, pieces, onehot_ref, left, columns, extra_ref)

    mine = meta_ref[n_pieces]
    keep = pl.ds(pl.multiple_of(mine * half, half), half)
    send = pl.ds(pl.multiple_of((1 - mine) * half, half), half)
    for i, copy in enumerate(copies):
        for piece in copy:
            piece.wait()
        x = x_vmem[i]
        shift = jnp.mean(x[:SHIFT_ROWS].astype(jnp.float32), axis=0, keepdims=True).astype(jnp.bfloat16)
        out = jnp.dot(left[...], x - shift, preferred_element_type=jnp.float32)
        by_class = out[rows:rows + CLASSES]
        total = jnp.sum(by_class, axis=0, keepdims=True) / tokens
        shift = shift.astype(jnp.float32)
        here = slice(i * width, (i + 1) * width)
        sums_ref[:, here] = by_class + columns[rows:rows + CLASSES, :1] * shift
        means_ref[i:i + 1, :] = total + shift
        split[...] = out[:rows] - columns[:rows, :1] * total
        keep_ref[:, here] = split[keep, :]
        send_ref[:, here] = split[send, :].astype(jnp.bfloat16)


def local_part(first, blocks, activations, pieces, onehot, meta, orders, rows, prepared=None):
    tokens, cols = activations.shape
    width = cols // CLASSES
    part = blocks * width
    vmem = pl.BlockSpec(memory_space=pltpu.VMEM)
    out_shape = [
        jax.ShapeDtypeStruct((rows // 2, part), jnp.bfloat16),
        jax.ShapeDtypeStruct((rows // 2, part), jnp.float32),
        jax.ShapeDtypeStruct((CLASSES, part), jnp.float32),
        jax.ShapeDtypeStruct((blocks, width), jnp.float32),
    ]
    if prepared is None:
        out_shape += [
            jax.ShapeDtypeStruct((rows + PAD, tokens), jnp.bfloat16),
            jax.ShapeDtypeStruct((rows + PAD, PANEL), jnp.float32),
            jax.ShapeDtypeStruct((CLASSES, 2 * PANEL), jnp.float32),
        ]
        args = list(pieces) + [onehot]
    else:
        args = list(prepared)
    return pl.pallas_call(
        functools.partial(local_kernel, first, blocks, orders, len(pieces)),
        in_specs=[pl.BlockSpec(memory_space=pltpu.SMEM), pl.BlockSpec(memory_space=pl.ANY)]
        + [vmem] * len(args),
        out_specs=[vmem] * len(out_shape),
        scratch_shapes=[
            pltpu.VMEM((rows, width), jnp.float32),
            pltpu.VMEM((blocks, tokens, width), jnp.bfloat16),
            pltpu.SemaphoreType.DMA((blocks, PIECES)),
        ],
        out_shape=out_shape,
        compiler_params=pltpu.CompilerParams(vmem_limit_bytes=VMEM_LIMIT),
        cost_estimate=pl.CostEstimate(
            flops=2 * tokens * part * (rows + PAD),
            bytes_accessed=2 * tokens * part + 6 * (rows // 2) * part,
            transcendentals=0,
        ),
        name="local_sums",
    )(meta, activations, *args)


def finish_kernel(total, tokens, n, sums_ref, place_ref, away_ref, *refs):
    kept, came, (cov_hbm, cross_hbm, cov, cross, sems) = refs[:n], refs[n:2 * n], refs[2 * n:]
    cols = cov.shape[1]
    by_class = sums_ref[:, :cols]
    mean = jnp.sum(by_class, axis=0, keepdims=True) / total
    cross[...] = (by_class - sums_ref[:, cols:cols + 1] * mean) / total
    cross_copy = pltpu.make_async_copy(cross, cross_hbm, sems.at[0])
    cross_copy.start()
    between = jnp.dot(
        place_ref[...], away_ref[...],
        precision=lax.Precision.HIGHEST, preferred_element_type=jnp.float32,
    ) * (tokens / (total - 1))
    first = 0
    for mine, other in zip(kept, came):
        here = slice(first, first + mine.shape[1])
        within = mine[...] + other[...].astype(jnp.float32)
        cov[:, here] = within / (total - 1) + between[:, here]
        first += mine.shape[1]
    cov_copy = pltpu.make_async_copy(cov, cov_hbm, sems.at[1])
    cov_copy.start()
    cross_copy.wait()
    cov_copy.wait()


def finish(total, tokens, sums, place, away, kept, came):
    cols = away.shape[1]
    shapes = [(place.shape[0], cols), (CLASSES, cols)]
    args = [sums, place, away, *kept, *came]
    return pl.pallas_call(
        functools.partial(finish_kernel, total, tokens, len(kept)),
        in_specs=[pl.BlockSpec(memory_space=pltpu.VMEM)] * len(args),
        out_specs=[pl.BlockSpec(memory_space=pl.ANY)] * 2,
        out_shape=[jax.ShapeDtypeStruct(s, jnp.float32) for s in shapes],
        scratch_shapes=[pltpu.VMEM(s, jnp.float32) for s in shapes] + [pltpu.SemaphoreType.DMA((2,))],
        compiler_params=pltpu.CompilerParams(vmem_limit_bytes=16 * 2**20),
        name="finish",
    )(*args)


def after(value, *others):
    return lax.optimization_barrier((value, *others))[0]


def body(activations, labels):
    tokens, cols = activations.shape
    n_tok, n_feat = lax.axis_size("tok"), lax.axis_size("feat")
    levels = n_tok.bit_length() - 1
    assert n_tok == 1 << levels
    rows = PANEL * n_feat
    unit = rows // n_tok
    me, feat = lax.axis_index("tok"), lax.axis_index("feat")
    total = tokens * n_tok
    even, odd = orders_of(levels)
    parity = feat % 2
    bits = [(me >> jnp.where(parity == 0, a, b)) & 1 for a, b in zip(even, odd)]

    def swap(value, level):
        pairs = []
        for i in range(n_tok):
            for f in range(n_feat):
                bit = (even, odd)[f % 2][level]
                pairs.append((i * n_feat + f, (i ^ (1 << bit)) * n_feat + f))
        return lax.ppermute(value, ("tok", "feat"), pairs)

    own = activations[:, :PANEL]
    if n_feat == 2:
        other = lax.ppermute(own, "feat", [(0, 1), (1, 0)])
        pieces = [own, other]
        places = [feat * PANEL // unit, (1 - feat) * PANEL // unit]
    else:
        pieces = [lax.all_gather(own, "feat", axis=1, tiled=True)]
        places = [0]
    meta = jnp.stack(places + [bits[0], parity]).astype(jnp.int32)
    onehot = (labels[None, :] == jnp.arange(PAD, dtype=jnp.int32)[:, None]).astype(jnp.bfloat16)

    sends, kept, sums, means, prepared = [], [], [], [], None
    for chunk, blocks in enumerate(CHUNKS):
        first = sum(CHUNKS[:chunk])
        out = local_part(first, blocks, activations, pieces, onehot, meta, (even, odd), rows, prepared)
        sends.append(out[0])
        kept.append(out[1])
        sums.append(out[2])
        means.append(out[3])
        if chunk == 0:
            prepared, extra = out[4:6], out[6]
    head, lanes = cols + PANEL, cols // CLASSES
    sums = jnp.concatenate(
        sums + [extra[:, :PANEL], jnp.concatenate(means, axis=0), extra[:, PANEL:]], axis=1
    )

    start = sum(bit * (rows >> (k + 1)) for k, bit in enumerate(bits))
    last = len(CHUNKS) - 1
    turns = []
    for level in range(levels - 1):
        turns += [(chunk, level) for chunk in range(last)]
        turns.insert(len(turns) - (level == 2), (SUMS, level))
        turns += [(last, level)]
    turns += [(SUMS, levels - 1)]

    came = [swap(send, 0) for send in sends]
    route = list(range(2, levels)) + [1, 0]
    came_sums = swap(sums, route[0])
    done = ()
    for chunk, level in turns:
        if chunk == SUMS:
            other = after(came_sums, *done)
            sums = jnp.concatenate([sums[:, :head] + other[:, :head], sums[:, head:], other[:, head:]], axis=1)
            if level + 1 < levels:
                came_sums = swap(sums, route[level + 1])
            done = (sums,)
        else:
            mine, other = kept[chunk], after(came[chunk], *done)
            half = mine.shape[0] // 2
            bit = bits[level + 1]

            def merged(bit):
                pick = lambda a: lax.dynamic_slice_in_dim(a, bit * half, half, 0)
                return pick(mine) + pick(other).astype(jnp.float32)

            send = merged(1 - bit).astype(jnp.bfloat16)
            kept[chunk] = merged(bit)
            came[chunk] = swap(send, level + 1)
            done = (send,)

    means = sums[:, head:].reshape(CLASSES, n_tok, lanes + PANEL)
    away = (means - jnp.mean(means, axis=1, keepdims=True)).transpose(1, 0, 2)
    place = lax.dynamic_slice(
        away, (0, start // PANEL, lanes + start % PANEL), (n_tok, 1, unit)
    ).reshape(n_tok, unit).T
    away = away[:, :, :lanes].reshape(n_tok, cols)
    sums = sums[:, :head]
    came = [after(c, place, away, sums) for c in came]
    return tuple(finish(total, tokens, sums, place, away, kept, came))


def solution(mesh):
    in_specs = (P("tok", "feat"), P("tok"))
    out_specs = (P("tok", "feat"), P(None, "feat"))
    return jax.shard_map(body, mesh=mesh, in_specs=in_specs, out_specs=out_specs, check_vma=False)
```

```python
import functools

import jax
import jax.numpy as jnp
from jax import lax
from jax.experimental import pallas as pl
from jax.experimental.pallas import tpu as pltpu
from jax.sharding import PartitionSpec as P

CLASSES = 8
PANEL = 128
PAD = 16
SHIFT_ROWS = 128
CHUNKS = (5, 3)
VMEM_LIMIT = 48 * 2**20
PIECES = 2
SUMS = -1


def orders_of(levels):
    even = list(range(levels))
    odd = list(even)
    for i in range(0, levels - 1, 2):
        odd[i], odd[i + 1] = even[i + 1], even[i]
    return even, odd


def position(block, order):
    pos = 0
    for bit in order:
        pos = pos * 2 + ((block >> bit) & 1)
    return pos


def turned(raw):
    raw = raw.T
    shift = jnp.mean(raw[:, :SHIFT_ROWS].astype(jnp.float32), axis=1, keepdims=True)
    shift = shift.astype(jnp.bfloat16)
    return raw - shift, jnp.broadcast_to(shift.astype(jnp.float32), (raw.shape[0], PANEL))


def turn_kernel(raw_ref, y_ref, shift_ref):
    y_ref[...], shift_ref[...] = turned(raw_ref[...])


def turn(raw):
    tokens, size = raw.shape
    vmem = pl.BlockSpec(memory_space=pltpu.VMEM)
    return pl.pallas_call(
        turn_kernel,
        in_specs=[vmem],
        out_specs=[vmem] * 2,
        out_shape=[
            jax.ShapeDtypeStruct((size, tokens), jnp.bfloat16),
            jax.ShapeDtypeStruct((size, PANEL), jnp.float32),
        ],
        compiler_params=pltpu.CompilerParams(vmem_limit_bytes=16 * 2**20),
        cost_estimate=pl.CostEstimate(flops=0, bytes_accessed=4 * tokens * size, transcendentals=0),
        name="turn",
    )(raw)


def prepare(orders, meta_ref, pieces, onehot_ref, left, columns, extra_ref):
    tokens = left.shape[1]
    rows = left.shape[0] - PAD
    unit = rows // 2 ** len(orders[0])
    for i, piece in enumerate(pieces):
        if len(piece) == 2:
            y, shift = (ref[...] for ref in piece)
        else:
            y, shift = turned(piece[0][...])
        size = y.shape[0]
        first = meta_ref[i]
        for j in range(size // unit):
            block = first + j
            even, odd = (
                sum(((block >> bit) & 1) << k for k, bit in enumerate(reversed(order)))
                for order in orders
            )
            pos = jnp.where(meta_ref[len(pieces) + 1] == 0, even, odd)
            at = pl.ds(pl.multiple_of(pos * unit, unit), unit)
            here = slice(j * unit, (j + 1) * unit)
            left[at, :] = y[here]
            columns[at, :] = shift[here]
    left[rows:, :] = onehot_ref[...]
    shift = columns[:rows, :]
    total = jnp.sum(left[...].astype(jnp.float32), axis=1, keepdims=True)
    columns[...] = jnp.broadcast_to(total, columns.shape)
    extra_ref[...] = jnp.zeros(extra_ref.shape, jnp.float32)
    extra_ref[:, :PANEL] = columns[rows:rows + CLASSES, :]
    means = columns[:rows, :] / tokens + shift
    for i in range(rows // PANEL):
        extra_ref[i:i + 1, PANEL:] = means[i * PANEL:(i + 1) * PANEL].T[:1, :]


def local_kernel(first, blocks, orders, lengths, meta_ref, x_hbm, *refs):
    n_pieces = len(lengths)
    if first == 0:
        pieces = []
        for length in lengths:
            pieces.append(refs[:length])
            refs = refs[length:]
        onehot_ref, send_ref, keep_ref, sums_ref, means_ref, left, columns, extra_ref, split, x_vmem, sems = refs
    else:
        left, columns, send_ref, keep_ref, sums_ref, means_ref, split, x_vmem, sems = refs
    tokens, width = x_vmem.shape[1:]
    rows = left.shape[0] - PAD
    half = rows // 2
    size = tokens // PIECES
    copies = [
        [
            pltpu.make_async_copy(
                x_hbm.at[pl.ds(p * size, size), pl.ds((first + i) * width, width)],
                x_vmem.at[i, pl.ds(p * size, size), :],
                sems.at[i, p],
            )
            for p in range(PIECES)
        ]
        for i in range(blocks)
    ]
    for copy in copies:
        for piece in copy:
            piece.start()
    if first == 0:
        prepare(orders, meta_ref, pieces, onehot_ref, left, columns, extra_ref)

    mine = meta_ref[n_pieces]
    keep = pl.ds(pl.multiple_of(mine * half, half), half)
    send = pl.ds(pl.multiple_of((1 - mine) * half, half), half)
    for i, copy in enumerate(copies):
        for piece in copy:
            piece.wait()
        x = x_vmem[i]
        shift = jnp.mean(x[:SHIFT_ROWS].astype(jnp.float32), axis=0, keepdims=True).astype(jnp.bfloat16)
        out = jnp.dot(left[...], x - shift, preferred_element_type=jnp.float32)
        by_class = out[rows:rows + CLASSES]
        total = jnp.sum(by_class, axis=0, keepdims=True) / tokens
        shift = shift.astype(jnp.float32)
        here = slice(i * width, (i + 1) * width)
        sums_ref[:, here] = by_class + columns[rows:rows + CLASSES, :1] * shift
        means_ref[i:i + 1, :] = total + shift
        split[...] = out[:rows] - columns[:rows, :1] * total
        keep_ref[:, here] = split[keep, :]
        send_ref[:, here] = split[send, :].astype(jnp.bfloat16)


def local_part(first, blocks, activations, pieces, onehot, meta, orders, rows, prepared=None):
    tokens, cols = activations.shape
    width = cols // CLASSES
    part = blocks * width
    vmem = pl.BlockSpec(memory_space=pltpu.VMEM)
    out_shape = [
        jax.ShapeDtypeStruct((rows // 2, part), jnp.bfloat16),
        jax.ShapeDtypeStruct((rows // 2, part), jnp.float32),
        jax.ShapeDtypeStruct((CLASSES, part), jnp.float32),
        jax.ShapeDtypeStruct((blocks, width), jnp.float32),
    ]
    if prepared is None:
        out_shape += [
            jax.ShapeDtypeStruct((rows + PAD, tokens), jnp.bfloat16),
            jax.ShapeDtypeStruct((rows + PAD, PANEL), jnp.float32),
            jax.ShapeDtypeStruct((CLASSES, 2 * PANEL), jnp.float32),
        ]
        args = [array for piece in pieces for array in piece] + [onehot]
    else:
        args = list(prepared)
    return pl.pallas_call(
        functools.partial(local_kernel, first, blocks, orders, [len(piece) for piece in pieces]),
        in_specs=[pl.BlockSpec(memory_space=pltpu.SMEM), pl.BlockSpec(memory_space=pl.ANY)]
        + [vmem] * len(args),
        out_specs=[vmem] * len(out_shape),
        scratch_shapes=[
            pltpu.VMEM((rows, width), jnp.float32),
            pltpu.VMEM((blocks, tokens, width), jnp.bfloat16),
            pltpu.SemaphoreType.DMA((blocks, PIECES)),
        ],
        out_shape=out_shape,
        compiler_params=pltpu.CompilerParams(vmem_limit_bytes=VMEM_LIMIT),
        cost_estimate=pl.CostEstimate(
            flops=2 * tokens * part * (rows + PAD),
            bytes_accessed=2 * tokens * part + 6 * (rows // 2) * part,
            transcendentals=0,
        ),
        name="local_sums",
    )(meta, activations, *args)


def finish_kernel(total, tokens, n, sums_ref, place_ref, away_ref, *refs):
    kept, came, (cov_hbm, cross_hbm, cov, cross, sems) = refs[:n], refs[n:2 * n], refs[2 * n:]
    cols = cov.shape[1]
    by_class = sums_ref[:, :cols]
    mean = jnp.sum(by_class, axis=0, keepdims=True) / total
    cross[...] = (by_class - sums_ref[:, cols:cols + 1] * mean) / total
    cross_copy = pltpu.make_async_copy(cross, cross_hbm, sems.at[0])
    cross_copy.start()
    between = jnp.dot(
        place_ref[...], away_ref[...],
        precision=lax.Precision.HIGHEST, preferred_element_type=jnp.float32,
    ) * (tokens / (total - 1))
    first = 0
    for mine, other in zip(kept, came):
        here = slice(first, first + mine.shape[1])
        within = mine[...] + other[...].astype(jnp.float32)
        cov[:, here] = within / (total - 1) + between[:, here]
        first += mine.shape[1]
    cov_copy = pltpu.make_async_copy(cov, cov_hbm, sems.at[1])
    cov_copy.start()
    cross_copy.wait()
    cov_copy.wait()


def finish(total, tokens, sums, place, away, kept, came):
    cols = away.shape[1]
    shapes = [(place.shape[0], cols), (CLASSES, cols)]
    args = [sums, place, away, *kept, *came]
    return pl.pallas_call(
        functools.partial(finish_kernel, total, tokens, len(kept)),
        in_specs=[pl.BlockSpec(memory_space=pltpu.VMEM)] * len(args),
        out_specs=[pl.BlockSpec(memory_space=pl.ANY)] * 2,
        out_shape=[jax.ShapeDtypeStruct(s, jnp.float32) for s in shapes],
        scratch_shapes=[pltpu.VMEM(s, jnp.float32) for s in shapes] + [pltpu.SemaphoreType.DMA((2,))],
        compiler_params=pltpu.CompilerParams(vmem_limit_bytes=16 * 2**20),
        name="finish",
    )(*args)


def after(value, *others):
    return lax.optimization_barrier((value, *others))[0]


def body(activations, labels):
    tokens, cols = activations.shape
    n_tok, n_feat = lax.axis_size("tok"), lax.axis_size("feat")
    levels = n_tok.bit_length() - 1
    assert n_tok == 1 << levels
    rows = PANEL * n_feat
    unit = rows // n_tok
    me, feat = lax.axis_index("tok"), lax.axis_index("feat")
    total = tokens * n_tok
    even, odd = orders_of(levels)
    parity = feat % 2
    bits = [(me >> jnp.where(parity == 0, a, b)) & 1 for a, b in zip(even, odd)]

    def swap(value, level):
        pairs = []
        for i in range(n_tok):
            for f in range(n_feat):
                bit = (even, odd)[f % 2][level]
                pairs.append((i * n_feat + f, (i ^ (1 << bit)) * n_feat + f))
        return lax.ppermute(value, ("tok", "feat"), pairs)

    own = activations[:, :PANEL]
    if n_feat == 2:
        other = lax.ppermute(own, "feat", [(0, 1), (1, 0)])
        pieces = [turn(own), [other]]
        places = [feat * PANEL // unit, (1 - feat) * PANEL // unit]
    else:
        pieces = [[lax.all_gather(own, "feat", axis=1, tiled=True)]]
        places = [0]
    meta = jnp.stack(places + [bits[0], parity]).astype(jnp.int32)
    onehot = (labels[None, :] == jnp.arange(PAD, dtype=jnp.int32)[:, None]).astype(jnp.bfloat16)

    sends, kept, sums, means, prepared = [], [], [], [], None
    for chunk, blocks in enumerate(CHUNKS):
        first = sum(CHUNKS[:chunk])
        out = local_part(first, blocks, activations, pieces, onehot, meta, (even, odd), rows, prepared)
        sends.append(out[0])
        kept.append(out[1])
        sums.append(out[2])
        means.append(out[3])
        if chunk == 0:
            prepared, extra = out[4:6], out[6]
    head, lanes = cols + PANEL, cols // CLASSES
    sums = jnp.concatenate(
        sums + [extra[:, :PANEL], jnp.concatenate(means, axis=0), extra[:, PANEL:]], axis=1
    )

    start = sum(bit * (rows >> (k + 1)) for k, bit in enumerate(bits))
    last = len(CHUNKS) - 1
    turns = []
    for level in range(levels - 1):
        turns += [(chunk, level) for chunk in range(last)]
        turns.insert(len(turns) - (level == 2), (SUMS, level))
        turns += [(last, level)]
    turns += [(SUMS, levels - 1)]

    came = [swap(send, 0) for send in sends]
    route = list(range(2, levels)) + [1, 0]
    came_sums = swap(sums, route[0])
    done = ()
    for chunk, level in turns:
        if chunk == SUMS:
            other = after(came_sums, *done)
            sums = jnp.concatenate([sums[:, :head] + other[:, :head], sums[:, head:], other[:, head:]], axis=1)
            if level + 1 < levels:
                came_sums = swap(sums, route[level + 1])
            done = (sums,)
        else:
            mine, other = kept[chunk], after(came[chunk], *done)
            half = mine.shape[0] // 2
            bit = bits[level + 1]

            def merged(bit):
                pick = lambda a: lax.dynamic_slice_in_dim(a, bit * half, half, 0)
                return pick(mine) + pick(other).astype(jnp.float32)

            send = merged(1 - bit).astype(jnp.bfloat16)
            kept[chunk] = merged(bit)
            came[chunk] = swap(send, level + 1)
            done = (send,)

    means = sums[:, head:].reshape(CLASSES, n_tok, lanes + PANEL)
    away = (means - jnp.mean(means, axis=1, keepdims=True)).transpose(1, 0, 2)
    place = lax.dynamic_slice(
        away, (0, start // PANEL, lanes + start % PANEL), (n_tok, 1, unit)
    ).reshape(n_tok, unit).T
    away = away[:, :, :lanes].reshape(n_tok, cols)
    sums = sums[:, :head]
    came = [after(c, place, away, sums) for c in came]
    return tuple(finish(total, tokens, sums, place, away, kept, came))


def solution(mesh):
    in_specs = (P("tok", "feat"), P("tok"))
    out_specs = (P("tok", "feat"), P(None, "feat"))
    return jax.shard_map(body, mesh=mesh, in_specs=in_specs, out_specs=out_specs, check_vma=False)
```

```python
import functools

import jax
import jax.numpy as jnp
from jax import lax
from jax.experimental import pallas as pl
from jax.experimental.pallas import tpu as pltpu
from jax.sharding import PartitionSpec as P

CLASSES = 8
PANEL = 128
PAD = 16
SHIFT_ROWS = 128
CHUNKS = (5, 3)
VMEM_LIMIT = 48 * 2**20
PIECES = 2
AHEAD = 2
SUMS = -1


def orders_of(levels):
    even = list(range(levels))
    odd = list(even)
    for i in range(0, levels - 1, 2):
        odd[i], odd[i + 1] = even[i + 1], even[i]
    return even, odd


def position(block, order):
    pos = 0
    for bit in order:
        pos = pos * 2 + ((block >> bit) & 1)
    return pos


def turned(raw):
    raw = raw.T
    shift = jnp.mean(raw[:, :SHIFT_ROWS].astype(jnp.float32), axis=1, keepdims=True)
    shift = shift.astype(jnp.bfloat16)
    return raw - shift, jnp.broadcast_to(shift.astype(jnp.float32), (raw.shape[0], PANEL))


def turn_kernel(raw_ref, y_ref, shift_ref):
    y_ref[...], shift_ref[...] = turned(raw_ref[...])


def turn(raw):
    tokens, size = raw.shape
    vmem = pl.BlockSpec(memory_space=pltpu.VMEM)
    return pl.pallas_call(
        turn_kernel,
        in_specs=[vmem],
        out_specs=[vmem] * 2,
        out_shape=[
            jax.ShapeDtypeStruct((size, tokens), jnp.bfloat16),
            jax.ShapeDtypeStruct((size, PANEL), jnp.float32),
        ],
        compiler_params=pltpu.CompilerParams(vmem_limit_bytes=16 * 2**20),
        cost_estimate=pl.CostEstimate(flops=0, bytes_accessed=4 * tokens * size, transcendentals=0),
        name="turn",
    )(raw)


def prepare(orders, meta_ref, pieces, onehot_ref, left, columns, extra_ref):
    tokens = left.shape[1]
    rows = left.shape[0] - PAD
    unit = rows // 2 ** len(orders[0])
    for i, piece in enumerate(pieces):
        if len(piece) == 2:
            y, shift = (ref[...] for ref in piece)
        else:
            y, shift = turned(piece[0][...])
        size = y.shape[0]
        first = meta_ref[i]
        for j in range(size // unit):
            block = first + j
            even, odd = (
                sum(((block >> bit) & 1) << k for k, bit in enumerate(reversed(order)))
                for order in orders
            )
            pos = jnp.where(meta_ref[len(pieces) + 1] == 0, even, odd)
            at = pl.ds(pl.multiple_of(pos * unit, unit), unit)
            here = slice(j * unit, (j + 1) * unit)
            left[at, :] = y[here]
            columns[at, :] = shift[here]
    left[rows:, :] = onehot_ref[...]
    shift = columns[:rows, :]
    total = jnp.sum(left[...].astype(jnp.float32), axis=1, keepdims=True)
    columns[...] = jnp.broadcast_to(total, columns.shape)
    extra_ref[...] = jnp.zeros(extra_ref.shape, jnp.float32)
    extra_ref[:, :PANEL] = columns[rows:rows + CLASSES, :]
    means = columns[:rows, :] / tokens + shift
    for i in range(rows // PANEL):
        extra_ref[i:i + 1, PANEL:] = means[i * PANEL:(i + 1) * PANEL].T[:1, :]


def local_kernel(first, blocks, orders, lengths, meta_ref, x_hbm, *refs):
    n_pieces = len(lengths)
    if first == 0:
        pieces = []
        for length in lengths:
            pieces.append(refs[:length])
            refs = refs[length:]
        onehot_ref, send_ref, keep_ref, sums_ref, means_ref, left, columns, extra_ref, split, x_vmem, sems = refs
    else:
        left, columns, send_ref, keep_ref, sums_ref, means_ref, split, x_vmem, sems = refs
    tokens, width = x_vmem.shape[1:]
    rows = left.shape[0] - PAD
    half = rows // 2
    size = tokens // PIECES
    copies = [
        [
            pltpu.make_async_copy(
                x_hbm.at[pl.ds(p * size, size), pl.ds((first + i) * width, width)],
                x_vmem.at[i, pl.ds(p * size, size), :],
                sems.at[i, p],
            )
            for p in range(PIECES)
        ]
        for i in range(blocks)
    ]
    for copy in copies[:AHEAD]:
        for piece in copy:
            piece.start()
    if first == 0:
        prepare(orders, meta_ref, pieces, onehot_ref, left, columns, extra_ref)

    mine = meta_ref[n_pieces]
    keep = pl.ds(pl.multiple_of(mine * half, half), half)
    send = pl.ds(pl.multiple_of((1 - mine) * half, half), half)
    for i, copy in enumerate(copies):
        for piece in copy:
            piece.wait()
        for copy in copies[i + AHEAD:i + AHEAD + 1]:
            for piece in copy:
                piece.start()
        x = x_vmem[i]
        shift = jnp.mean(x[:SHIFT_ROWS].astype(jnp.float32), axis=0, keepdims=True).astype(jnp.bfloat16)
        out = jnp.dot(left[...], x - shift, preferred_element_type=jnp.float32)
        by_class = out[rows:rows + CLASSES]
        total = jnp.sum(by_class, axis=0, keepdims=True) / tokens
        shift = shift.astype(jnp.float32)
        here = slice(i * width, (i + 1) * width)
        sums_ref[:, here] = by_class + columns[rows:rows + CLASSES, :1] * shift
        means_ref[i:i + 1, :] = total + shift
        split[...] = out[:rows] - columns[:rows, :1] * total
        keep_ref[:, here] = split[keep, :]
        send_ref[:, here] = split[send, :].astype(jnp.bfloat16)


def local_part(first, blocks, activations, pieces, onehot, meta, orders, rows, prepared=None):
    tokens, cols = activations.shape
    width = cols // CLASSES
    part = blocks * width
    vmem = pl.BlockSpec(memory_space=pltpu.VMEM)
    out_shape = [
        jax.ShapeDtypeStruct((rows // 2, part), jnp.bfloat16),
        jax.ShapeDtypeStruct((rows // 2, part), jnp.float32),
        jax.ShapeDtypeStruct((CLASSES, part), jnp.float32),
        jax.ShapeDtypeStruct((blocks, width), jnp.float32),
    ]
    if prepared is None:
        out_shape += [
            jax.ShapeDtypeStruct((rows + PAD, tokens), jnp.bfloat16),
            jax.ShapeDtypeStruct((rows + PAD, PANEL), jnp.float32),
            jax.ShapeDtypeStruct((CLASSES, 2 * PANEL), jnp.float32),
        ]
        args = [array for piece in pieces for array in piece] + [onehot]
    else:
        args = list(prepared)
    return pl.pallas_call(
        functools.partial(local_kernel, first, blocks, orders, [len(piece) for piece in pieces]),
        in_specs=[pl.BlockSpec(memory_space=pltpu.SMEM), pl.BlockSpec(memory_space=pl.ANY)]
        + [vmem] * len(args),
        out_specs=[vmem] * len(out_shape),
        scratch_shapes=[
            pltpu.VMEM((rows, width), jnp.float32),
            pltpu.VMEM((blocks, tokens, width), jnp.bfloat16),
            pltpu.SemaphoreType.DMA((blocks, PIECES)),
        ],
        out_shape=out_shape,
        compiler_params=pltpu.CompilerParams(vmem_limit_bytes=VMEM_LIMIT),
        cost_estimate=pl.CostEstimate(
            flops=2 * tokens * part * (rows + PAD),
            bytes_accessed=2 * tokens * part + 6 * (rows // 2) * part,
            transcendentals=0,
        ),
        name="local_sums",
    )(meta, activations, *args)


def finish_kernel(total, tokens, n, sums_ref, place_ref, away_ref, *refs):
    kept, came, (cov_hbm, cross_hbm, cov, cross, sems) = refs[:n], refs[n:2 * n], refs[2 * n:]
    cols = cov.shape[1]
    by_class = sums_ref[:, :cols]
    mean = jnp.sum(by_class, axis=0, keepdims=True) / total
    cross[...] = (by_class - sums_ref[:, cols:cols + 1] * mean) / total
    cross_copy = pltpu.make_async_copy(cross, cross_hbm, sems.at[0])
    cross_copy.start()
    between = jnp.dot(
        place_ref[...], away_ref[...],
        precision=lax.Precision.HIGHEST, preferred_element_type=jnp.float32,
    ) * (tokens / (total - 1))
    first = 0
    for mine, other in zip(kept, came):
        here = slice(first, first + mine.shape[1])
        within = mine[...] + other[...].astype(jnp.float32)
        cov[:, here] = within / (total - 1) + between[:, here]
        first += mine.shape[1]
    cov_copy = pltpu.make_async_copy(cov, cov_hbm, sems.at[1])
    cov_copy.start()
    cross_copy.wait()
    cov_copy.wait()


def finish(total, tokens, sums, place, away, kept, came):
    cols = away.shape[1]
    shapes = [(place.shape[0], cols), (CLASSES, cols)]
    args = [sums, place, away, *kept, *came]
    return pl.pallas_call(
        functools.partial(finish_kernel, total, tokens, len(kept)),
        in_specs=[pl.BlockSpec(memory_space=pltpu.VMEM)] * len(args),
        out_specs=[pl.BlockSpec(memory_space=pl.ANY)] * 2,
        out_shape=[jax.ShapeDtypeStruct(s, jnp.float32) for s in shapes],
        scratch_shapes=[pltpu.VMEM(s, jnp.float32) for s in shapes] + [pltpu.SemaphoreType.DMA((2,))],
        compiler_params=pltpu.CompilerParams(vmem_limit_bytes=16 * 2**20),
        name="finish",
    )(*args)


def after(value, *others):
    return lax.optimization_barrier((value, *others))[0]


def body(activations, labels):
    tokens, cols = activations.shape
    n_tok, n_feat = lax.axis_size("tok"), lax.axis_size("feat")
    levels = n_tok.bit_length() - 1
    assert n_tok == 1 << levels
    rows = PANEL * n_feat
    unit = rows // n_tok
    me, feat = lax.axis_index("tok"), lax.axis_index("feat")
    total = tokens * n_tok
    even, odd = orders_of(levels)
    parity = feat % 2
    bits = [(me >> jnp.where(parity == 0, a, b)) & 1 for a, b in zip(even, odd)]

    def swap(value, level):
        pairs = []
        for i in range(n_tok):
            for f in range(n_feat):
                bit = (even, odd)[f % 2][level]
                pairs.append((i * n_feat + f, (i ^ (1 << bit)) * n_feat + f))
        return lax.ppermute(value, ("tok", "feat"), pairs)

    own = activations[:, :PANEL]
    if n_feat == 2:
        other = lax.ppermute(own, "feat", [(0, 1), (1, 0)])
        pieces = [turn(own), [other]]
        places = [feat * PANEL // unit, (1 - feat) * PANEL // unit]
    else:
        pieces = [[lax.all_gather(own, "feat", axis=1, tiled=True)]]
        places = [0]
    meta = jnp.stack(places + [bits[0], parity]).astype(jnp.int32)
    onehot = (labels[None, :] == jnp.arange(PAD, dtype=jnp.int32)[:, None]).astype(jnp.bfloat16)

    sends, kept, sums, means, prepared = [], [], [], [], None
    for chunk, blocks in enumerate(CHUNKS):
        first = sum(CHUNKS[:chunk])
        out = local_part(first, blocks, activations, pieces, onehot, meta, (even, odd), rows, prepared)
        sends.append(out[0])
        kept.append(out[1])
        sums.append(out[2])
        means.append(out[3])
        if chunk == 0:
            prepared, extra = out[4:6], out[6]
    head, lanes = cols + PANEL, cols // CLASSES
    sums = jnp.concatenate(
        sums + [extra[:, :PANEL], jnp.concatenate(means, axis=0), extra[:, PANEL:]], axis=1
    )

    start = sum(bit * (rows >> (k + 1)) for k, bit in enumerate(bits))
    last = len(CHUNKS) - 1
    turns = []
    for level in range(levels - 1):
        turns += [(chunk, level) for chunk in range(last)]
        turns.insert(len(turns) - (level == 2), (SUMS, level))
        turns += [(last, level)]
    turns += [(SUMS, levels - 1)]

    came = [swap(send, 0) for send in sends]
    route = list(range(2, levels)) + [1, 0]
    came_sums = swap(sums, route[0])
    done = ()
    for chunk, level in turns:
        if chunk == SUMS:
            other = after(came_sums, *done)
            sums = jnp.concatenate([sums[:, :head] + other[:, :head], sums[:, head:], other[:, head:]], axis=1)
            if level + 1 < levels:
                came_sums = swap(sums, route[level + 1])
            done = (sums,)
        else:
            mine, other = kept[chunk], after(came[chunk], *done)
            half = mine.shape[0] // 2
            bit = bits[level + 1]

            def merged(bit):
                pick = lambda a: lax.dynamic_slice_in_dim(a, bit * half, half, 0)
                return pick(mine) + pick(other).astype(jnp.float32)

            send = merged(1 - bit).astype(jnp.bfloat16)
            kept[chunk] = merged(bit)
            came[chunk] = swap(send, level + 1)
            done = (send,)

    means = sums[:, head:].reshape(CLASSES, n_tok, lanes + PANEL)
    away = (means - jnp.mean(means, axis=1, keepdims=True)).transpose(1, 0, 2)
    place = lax.dynamic_slice(
        away, (0, start // PANEL, lanes + start % PANEL), (n_tok, 1, unit)
    ).reshape(n_tok, unit).T
    away = away[:, :, :lanes].reshape(n_tok, cols)
    sums = sums[:, :head]
    came = [after(c, place, away, sums) for c in came]
    return tuple(finish(total, tokens, sums, place, away, kept, came))


def solution(mesh):
    in_specs = (P("tok", "feat"), P("tok"))
    out_specs = (P("tok", "feat"), P(None, "feat"))
    return jax.shard_map(body, mesh=mesh, in_specs=in_specs, out_specs=out_specs, check_vma=False)
```

```python
import functools

import jax
import jax.numpy as jnp
from jax import lax
from jax.experimental import pallas as pl
from jax.experimental.pallas import tpu as pltpu
from jax.sharding import PartitionSpec as P

CLASSES = 8
PANEL = 128
PAD = 16
SHIFT_ROWS = 128
CHUNKS = (3, 3, 2)
VMEM_LIMIT = 48 * 2**20
PIECES = 2
SUMS = -1


def orders_of(levels):
    even = list(range(levels))
    odd = list(even)
    for i in range(0, levels - 1, 2):
        odd[i], odd[i + 1] = even[i + 1], even[i]
    return even, odd


def position(block, order):
    pos = 0
    for bit in order:
        pos = pos * 2 + ((block >> bit) & 1)
    return pos


def turned(raw):
    raw = raw.T
    shift = jnp.mean(raw[:, :SHIFT_ROWS].astype(jnp.float32), axis=1, keepdims=True)
    shift = shift.astype(jnp.bfloat16)
    return raw - shift, jnp.broadcast_to(shift.astype(jnp.float32), (raw.shape[0], PANEL))


def turn_kernel(raw_ref, y_ref, shift_ref):
    y_ref[...], shift_ref[...] = turned(raw_ref[...])


def turn(raw):
    tokens, size = raw.shape
    vmem = pl.BlockSpec(memory_space=pltpu.VMEM)
    return pl.pallas_call(
        turn_kernel,
        in_specs=[vmem],
        out_specs=[vmem] * 2,
        out_shape=[
            jax.ShapeDtypeStruct((size, tokens), jnp.bfloat16),
            jax.ShapeDtypeStruct((size, PANEL), jnp.float32),
        ],
        compiler_params=pltpu.CompilerParams(vmem_limit_bytes=16 * 2**20),
        cost_estimate=pl.CostEstimate(flops=0, bytes_accessed=4 * tokens * size, transcendentals=0),
        name="turn",
    )(raw)


def prepare(orders, meta_ref, pieces, onehot_ref, left, columns, extra_ref):
    tokens = left.shape[1]
    rows = left.shape[0] - PAD
    unit = rows // 2 ** len(orders[0])
    for i, piece in enumerate(pieces):
        if len(piece) == 2:
            y, shift = (ref[...] for ref in piece)
        else:
            y, shift = turned(piece[0][...])
        size = y.shape[0]
        first = meta_ref[i]
        for j in range(size // unit):
            block = first + j
            even, odd = (
                sum(((block >> bit) & 1) << k for k, bit in enumerate(reversed(order)))
                for order in orders
            )
            pos = jnp.where(meta_ref[len(pieces) + 1] == 0, even, odd)
            at = pl.ds(pl.multiple_of(pos * unit, unit), unit)
            here = slice(j * unit, (j + 1) * unit)
            left[at, :] = y[here]
            columns[at, :] = shift[here]
    left[rows:, :] = onehot_ref[...]
    shift = columns[:rows, :]
    total = jnp.sum(left[...].astype(jnp.float32), axis=1, keepdims=True)
    columns[...] = jnp.broadcast_to(total, columns.shape)
    extra_ref[...] = jnp.zeros(extra_ref.shape, jnp.float32)
    extra_ref[:, :PANEL] = columns[rows:rows + CLASSES, :]
    means = columns[:rows, :] / tokens + shift
    for i in range(rows // PANEL):
        extra_ref[i:i + 1, PANEL:] = means[i * PANEL:(i + 1) * PANEL].T[:1, :]


def local_kernel(first, blocks, orders, lengths, meta_ref, x_hbm, *refs):
    n_pieces = len(lengths)
    if first == 0:
        pieces = []
        for length in lengths:
            pieces.append(refs[:length])
            refs = refs[length:]
        onehot_ref, send_ref, keep_ref, sums_ref, means_ref, left, columns, extra_ref, split, x_vmem, sems = refs
    else:
        left, columns, send_ref, keep_ref, sums_ref, means_ref, split, x_vmem, sems = refs
    tokens, width = x_vmem.shape[1:]
    rows = left.shape[0] - PAD
    half = rows // 2
    size = tokens // PIECES
    copies = [
        [
            pltpu.make_async_copy(
                x_hbm.at[pl.ds(p * size, size), pl.ds((first + i) * width, width)],
                x_vmem.at[i, pl.ds(p * size, size), :],
                sems.at[i, p],
            )
            for p in range(PIECES)
        ]
        for i in range(blocks)
    ]
    for copy in copies:
        for piece in copy:
            piece.start()
    if first == 0:
        prepare(orders, meta_ref, pieces, onehot_ref, left, columns, extra_ref)

    mine = meta_ref[n_pieces]
    keep = pl.ds(pl.multiple_of(mine * half, half), half)
    send = pl.ds(pl.multiple_of((1 - mine) * half, half), half)
    for i, copy in enumerate(copies):
        for piece in copy:
            piece.wait()
        x = x_vmem[i]
        shift = jnp.mean(x[:SHIFT_ROWS].astype(jnp.float32), axis=0, keepdims=True).astype(jnp.bfloat16)
        out = jnp.dot(left[...], x - shift, preferred_element_type=jnp.float32)
        by_class = out[rows:rows + CLASSES]
        total = jnp.sum(by_class, axis=0, keepdims=True) / tokens
        shift = shift.astype(jnp.float32)
        here = slice(i * width, (i + 1) * width)
        sums_ref[:, here] = by_class + columns[rows:rows + CLASSES, :1] * shift
        means_ref[i:i + 1, :] = total + shift
        split[...] = out[:rows] - columns[:rows, :1] * total
        keep_ref[:, here] = split[keep, :]
        send_ref[:, here] = split[send, :].astype(jnp.bfloat16)


def local_part(first, blocks, activations, pieces, onehot, meta, orders, rows, prepared=None):
    tokens, cols = activations.shape
    width = cols // CLASSES
    part = blocks * width
    vmem = pl.BlockSpec(memory_space=pltpu.VMEM)
    out_shape = [
        jax.ShapeDtypeStruct((rows // 2, part), jnp.bfloat16),
        jax.ShapeDtypeStruct((rows // 2, part), jnp.float32),
        jax.ShapeDtypeStruct((CLASSES, part), jnp.float32),
        jax.ShapeDtypeStruct((blocks, width), jnp.float32),
    ]
    if prepared is None:
        out_shape += [
            jax.ShapeDtypeStruct((rows + PAD, tokens), jnp.bfloat16),
            jax.ShapeDtypeStruct((rows + PAD, PANEL), jnp.float32),
            jax.ShapeDtypeStruct((CLASSES, 2 * PANEL), jnp.float32),
        ]
        args = [array for piece in pieces for array in piece] + [onehot]
    else:
        args = list(prepared)
    return pl.pallas_call(
        functools.partial(local_kernel, first, blocks, orders, [len(piece) for piece in pieces]),
        in_specs=[pl.BlockSpec(memory_space=pltpu.SMEM), pl.BlockSpec(memory_space=pl.ANY)]
        + [vmem] * len(args),
        out_specs=[vmem] * len(out_shape),
        scratch_shapes=[
            pltpu.VMEM((rows, width), jnp.float32),
            pltpu.VMEM((blocks, tokens, width), jnp.bfloat16),
            pltpu.SemaphoreType.DMA((blocks, PIECES)),
        ],
        out_shape=out_shape,
        compiler_params=pltpu.CompilerParams(vmem_limit_bytes=VMEM_LIMIT),
        cost_estimate=pl.CostEstimate(
            flops=2 * tokens * part * (rows + PAD),
            bytes_accessed=2 * tokens * part + 6 * (rows // 2) * part,
            transcendentals=0,
        ),
        name="local_sums",
    )(meta, activations, *args)


def finish_kernel(total, tokens, n, sums_ref, place_ref, away_ref, *refs):
    kept, came, (cov_hbm, cross_hbm, cov, cross, sems) = refs[:n], refs[n:2 * n], refs[2 * n:]
    cols = cov.shape[1]
    by_class = sums_ref[:, :cols]
    mean = jnp.sum(by_class, axis=0, keepdims=True) / total
    cross[...] = (by_class - sums_ref[:, cols:cols + 1] * mean) / total
    cross_copy = pltpu.make_async_copy(cross, cross_hbm, sems.at[0])
    cross_copy.start()
    between = jnp.dot(
        place_ref[...], away_ref[...],
        precision=lax.Precision.HIGHEST, preferred_element_type=jnp.float32,
    ) * (tokens / (total - 1))
    first = 0
    for mine, other in zip(kept, came):
        here = slice(first, first + mine.shape[1])
        within = mine[...] + other[...].astype(jnp.float32)
        cov[:, here] = within / (total - 1) + between[:, here]
        first += mine.shape[1]
    cov_copy = pltpu.make_async_copy(cov, cov_hbm, sems.at[1])
    cov_copy.start()
    cross_copy.wait()
    cov_copy.wait()


def finish(total, tokens, sums, place, away, kept, came):
    cols = away.shape[1]
    shapes = [(place.shape[0], cols), (CLASSES, cols)]
    args = [sums, place, away, *kept, *came]
    return pl.pallas_call(
        functools.partial(finish_kernel, total, tokens, len(kept)),
        in_specs=[pl.BlockSpec(memory_space=pltpu.VMEM)] * len(args),
        out_specs=[pl.BlockSpec(memory_space=pl.ANY)] * 2,
        out_shape=[jax.ShapeDtypeStruct(s, jnp.float32) for s in shapes],
        scratch_shapes=[pltpu.VMEM(s, jnp.float32) for s in shapes] + [pltpu.SemaphoreType.DMA((2,))],
        compiler_params=pltpu.CompilerParams(vmem_limit_bytes=16 * 2**20),
        name="finish",
    )(*args)


def after(value, *others):
    return lax.optimization_barrier((value, *others))[0]


def body(activations, labels):
    tokens, cols = activations.shape
    n_tok, n_feat = lax.axis_size("tok"), lax.axis_size("feat")
    levels = n_tok.bit_length() - 1
    assert n_tok == 1 << levels
    rows = PANEL * n_feat
    unit = rows // n_tok
    me, feat = lax.axis_index("tok"), lax.axis_index("feat")
    total = tokens * n_tok
    even, odd = orders_of(levels)
    parity = feat % 2
    bits = [(me >> jnp.where(parity == 0, a, b)) & 1 for a, b in zip(even, odd)]

    def swap(value, level):
        pairs = []
        for i in range(n_tok):
            for f in range(n_feat):
                bit = (even, odd)[f % 2][level]
                pairs.append((i * n_feat + f, (i ^ (1 << bit)) * n_feat + f))
        return lax.ppermute(value, ("tok", "feat"), pairs)

    own = activations[:, :PANEL]
    if n_feat == 2:
        other = lax.ppermute(own, "feat", [(0, 1), (1, 0)])
        pieces = [turn(own), [other]]
        places = [feat * PANEL // unit, (1 - feat) * PANEL // unit]
    else:
        pieces = [[lax.all_gather(own, "feat", axis=1, tiled=True)]]
        places = [0]
    meta = jnp.stack(places + [bits[0], parity]).astype(jnp.int32)
    onehot = (labels[None, :] == jnp.arange(PAD, dtype=jnp.int32)[:, None]).astype(jnp.bfloat16)

    came, kept, sums, means, prepared = [], [], [], [], None
    for chunk, blocks in enumerate(CHUNKS):
        first = sum(CHUNKS[:chunk])
        if chunk == 2:
            meta = after(meta, came[0])
        out = local_part(first, blocks, activations, pieces, onehot, meta, (even, odd), rows, prepared)
        came.append(swap(out[0], 0))
        kept.append(out[1])
        sums.append(out[2])
        means.append(out[3])
        if chunk == 0:
            prepared, extra = out[4:6], out[6]
    head, lanes = cols + PANEL, cols // CLASSES
    sums = jnp.concatenate(
        sums + [extra[:, :PANEL], jnp.concatenate(means, axis=0), extra[:, PANEL:]], axis=1
    )

    start = sum(bit * (rows >> (k + 1)) for k, bit in enumerate(bits))
    last = len(CHUNKS) - 1
    turns = []
    for level in range(levels - 1):
        turns += [(chunk, level) for chunk in range(last)]
        turns.insert(len(turns) - (level == 2), (SUMS, level))
        turns += [(last, level)]
    turns += [(SUMS, levels - 1)]

    route = list(range(2, levels)) + [1, 0]
    came_sums = swap(sums, route[0])
    done = ()
    for chunk, level in turns:
        if chunk == SUMS:
            other = after(came_sums, *done)
            sums = jnp.concatenate([sums[:, :head] + other[:, :head], sums[:, head:], other[:, head:]], axis=1)
            if level + 1 < levels:
                came_sums = swap(sums, route[level + 1])
            done = (sums,)
        else:
            if chunk == 1 and level == 0 and last == 2:
                done += (sums,)
            mine, other = kept[chunk], after(came[chunk], *done)
            half = mine.shape[0] // 2
            bit = bits[level + 1]

            def merged(bit):
                pick = lambda a: lax.dynamic_slice_in_dim(a, bit * half, half, 0)
                return pick(mine) + pick(other).astype(jnp.float32)

            send = merged(1 - bit).astype(jnp.bfloat16)
            kept[chunk] = merged(bit)
            came[chunk] = swap(send, level + 1)
            done = (send,)

    means = sums[:, head:].reshape(CLASSES, n_tok, lanes + PANEL)
    away = (means - jnp.mean(means, axis=1, keepdims=True)).transpose(1, 0, 2)
    place = lax.dynamic_slice(
        away, (0, start // PANEL, lanes + start % PANEL), (n_tok, 1, unit)
    ).reshape(n_tok, unit).T
    away = away[:, :, :lanes].reshape(n_tok, cols)
    sums = sums[:, :head]
    came = [after(c, place, away, sums) for c in came]
    return tuple(finish(total, tokens, sums, place, away, kept, came))


def solution(mesh):
    in_specs = (P("tok", "feat"), P("tok"))
    out_specs = (P("tok", "feat"), P(None, "feat"))
    return jax.shard_map(body, mesh=mesh, in_specs=in_specs, out_specs=out_specs, check_vma=False)
```

```python
import functools

import jax
import jax.numpy as jnp
from jax import lax
from jax.experimental import pallas as pl
from jax.experimental.pallas import tpu as pltpu
from jax.sharding import PartitionSpec as P

CLASSES = 8
PANEL = 128
PAD = 16
SHIFT_ROWS = 128
CHUNKS = (5, 3)
VMEM_LIMIT = 48 * 2**20
PIECES = 2
AHEAD = 2
SUMS = -1


def orders_of(levels):
    even = list(range(levels))
    odd = list(even)
    for i in range(0, levels - 1, 2):
        odd[i], odd[i + 1] = even[i + 1], even[i]
    return even, odd


def position(block, order):
    pos = 0
    for bit in order:
        pos = pos * 2 + ((block >> bit) & 1)
    return pos


def turned(raw):
    raw = raw.T
    shift = jnp.mean(raw[:, :SHIFT_ROWS].astype(jnp.float32), axis=1, keepdims=True)
    shift = shift.astype(jnp.bfloat16)
    return raw - shift, jnp.broadcast_to(shift.astype(jnp.float32), (raw.shape[0], PANEL))


def turn_kernel(raw_ref, y_ref, shift_ref):
    y_ref[...], shift_ref[...] = turned(raw_ref[...])


def turn(raw):
    tokens, size = raw.shape
    vmem = pl.BlockSpec(memory_space=pltpu.VMEM)
    return pl.pallas_call(
        turn_kernel,
        in_specs=[vmem],
        out_specs=[vmem] * 2,
        out_shape=[
            jax.ShapeDtypeStruct((size, tokens), jnp.bfloat16),
            jax.ShapeDtypeStruct((size, PANEL), jnp.float32),
        ],
        compiler_params=pltpu.CompilerParams(vmem_limit_bytes=16 * 2**20),
        cost_estimate=pl.CostEstimate(flops=0, bytes_accessed=4 * tokens * size, transcendentals=0),
        name="turn",
    )(raw)


def prepare(orders, meta_ref, pieces, onehot_ref, left, columns, extra_ref):
    tokens = left.shape[1]
    rows = left.shape[0] - PAD
    unit = rows // 2 ** len(orders[0])
    for i, piece in enumerate(pieces):
        if len(piece) == 2:
            y, shift = (ref[...] for ref in piece)
        else:
            y, shift = turned(piece[0][...])
        size = y.shape[0]
        first = meta_ref[i]
        for j in range(size // unit):
            block = first + j
            even, odd = (
                sum(((block >> bit) & 1) << k for k, bit in enumerate(reversed(order)))
                for order in orders
            )
            pos = jnp.where(meta_ref[len(pieces) + 1] == 0, even, odd)
            at = pl.ds(pl.multiple_of(pos * unit, unit), unit)
            here = slice(j * unit, (j + 1) * unit)
            left[at, :] = y[here]
            columns[at, :] = shift[here]
    left[rows:, :] = onehot_ref[...]
    shift = columns[:rows, :]
    total = jnp.sum(left[...].astype(jnp.float32), axis=1, keepdims=True)
    columns[...] = jnp.broadcast_to(total, columns.shape)
    extra_ref[...] = jnp.zeros(extra_ref.shape, jnp.float32)
    extra_ref[:, :PANEL] = columns[rows:rows + CLASSES, :]
    means = columns[:rows, :] / tokens + shift
    for i in range(rows // PANEL):
        extra_ref[i:i + 1, PANEL:] = means[i * PANEL:(i + 1) * PANEL].T[:1, :]


def local_kernel(first, blocks, orders, lengths, meta_ref, x_hbm, *refs):
    n_pieces = len(lengths)
    if first == 0:
        pieces = []
        for length in lengths:
            pieces.append(refs[:length])
            refs = refs[length:]
        onehot_ref, send_ref, keep_ref, sums_ref, means_ref, left, columns, extra_ref, split, x_vmem, sems = refs
    else:
        left, columns, send_ref, keep_ref, sums_ref, means_ref, split, x_vmem, sems = refs
    tokens, width = x_vmem.shape[1:]
    rows = left.shape[0] - PAD
    half = rows // 2
    size = tokens // PIECES
    copies = [
        [
            pltpu.make_async_copy(
                x_hbm.at[pl.ds(p * size, size), pl.ds((first + i) * width, width)],
                x_vmem.at[i, pl.ds(p * size, size), :],
                sems.at[i, p],
            )
            for p in range(PIECES)
        ]
        for i in range(blocks)
    ]
    for copy in copies[:AHEAD]:
        for piece in copy:
            piece.start()
    if first == 0:
        prepare(orders, meta_ref, pieces, onehot_ref, left, columns, extra_ref)

    mine = meta_ref[n_pieces]
    keep = pl.ds(pl.multiple_of(mine * half, half), half)
    send = pl.ds(pl.multiple_of((1 - mine) * half, half), half)
    for i, copy in enumerate(copies):
        for piece in copy:
            piece.wait()
        for copy in copies[i + AHEAD:i + AHEAD + 1]:
            for piece in copy:
                piece.start()
        x = x_vmem[i]
        shift = jnp.mean(x[:SHIFT_ROWS].astype(jnp.float32), axis=0, keepdims=True).astype(jnp.bfloat16)
        out = jnp.dot(left[...], x - shift, preferred_element_type=jnp.float32)
        by_class = out[rows:rows + CLASSES]
        total = jnp.sum(by_class, axis=0, keepdims=True) / tokens
        shift = shift.astype(jnp.float32)
        here = slice(i * width, (i + 1) * width)
        sums_ref[:, here] = by_class + columns[rows:rows + CLASSES, :1] * shift
        means_ref[i:i + 1, :] = total + shift
        split[...] = out[:rows] - columns[:rows, :1] * total
        keep_ref[:, here] = split[keep, :]
        send_ref[:, here] = split[send, :].astype(jnp.bfloat16)


def local_part(first, blocks, activations, pieces, onehot, meta, orders, rows, prepared=None):
    tokens, cols = activations.shape
    width = cols // CLASSES
    part = blocks * width
    vmem = pl.BlockSpec(memory_space=pltpu.VMEM)
    out_shape = [
        jax.ShapeDtypeStruct((rows // 2, part), jnp.bfloat16),
        jax.ShapeDtypeStruct((rows // 2, part), jnp.float32),
        jax.ShapeDtypeStruct((CLASSES, part), jnp.float32),
        jax.ShapeDtypeStruct((blocks, width), jnp.float32),
    ]
    if prepared is None:
        out_shape += [
            jax.ShapeDtypeStruct((rows + PAD, tokens), jnp.bfloat16),
            jax.ShapeDtypeStruct((rows + PAD, PANEL), jnp.float32),
            jax.ShapeDtypeStruct((CLASSES, 2 * PANEL), jnp.float32),
        ]
        args = [array for piece in pieces for array in piece] + [onehot]
    else:
        args = list(prepared)
    return pl.pallas_call(
        functools.partial(local_kernel, first, blocks, orders, [len(piece) for piece in pieces]),
        in_specs=[pl.BlockSpec(memory_space=pltpu.SMEM), pl.BlockSpec(memory_space=pl.ANY)]
        + [vmem] * len(args),
        out_specs=[vmem] * len(out_shape),
        scratch_shapes=[
            pltpu.VMEM((rows, width), jnp.float32),
            pltpu.VMEM((blocks, tokens, width), jnp.bfloat16),
            pltpu.SemaphoreType.DMA((blocks, PIECES)),
        ],
        out_shape=out_shape,
        compiler_params=pltpu.CompilerParams(vmem_limit_bytes=VMEM_LIMIT),
        cost_estimate=pl.CostEstimate(
            flops=2 * tokens * part * (rows + PAD),
            bytes_accessed=2 * tokens * part + 6 * (rows // 2) * part,
            transcendentals=0,
        ),
        name="local_sums",
    )(meta, activations, *args)


def finish_kernel(total, tokens, n, sums_ref, place_ref, away_ref, *refs):
    kept, came, (cov_hbm, cross_hbm, cov, cross, sems) = refs[:n], refs[n:2 * n], refs[2 * n:]
    cols = cov.shape[1]
    by_class = sums_ref[:, :cols]
    mean = jnp.sum(by_class, axis=0, keepdims=True) / total
    cross[...] = (by_class - sums_ref[:, cols:cols + 1] * mean) / total
    cross_copy = pltpu.make_async_copy(cross, cross_hbm, sems.at[0])
    cross_copy.start()
    between = jnp.dot(
        place_ref[...], away_ref[...],
        precision=lax.Precision.HIGHEST, preferred_element_type=jnp.float32,
    ) * (tokens / (total - 1))
    first = 0
    for mine, other in zip(kept, came):
        here = slice(first, first + mine.shape[1])
        within = mine[...] + other[...].astype(jnp.float32)
        cov[:, here] = within / (total - 1) + between[:, here]
        first += mine.shape[1]
    cov_copy = pltpu.make_async_copy(cov, cov_hbm, sems.at[1])
    cov_copy.start()
    cross_copy.wait()
    cov_copy.wait()


def finish(total, tokens, sums, place, away, kept, came):
    cols = away.shape[1]
    shapes = [(place.shape[0], cols), (CLASSES, cols)]
    args = [sums, place, away, *kept, *came]
    return pl.pallas_call(
        functools.partial(finish_kernel, total, tokens, len(kept)),
        in_specs=[pl.BlockSpec(memory_space=pltpu.VMEM)] * len(args),
        out_specs=[pl.BlockSpec(memory_space=pl.ANY)] * 2,
        out_shape=[jax.ShapeDtypeStruct(s, jnp.float32) for s in shapes],
        scratch_shapes=[pltpu.VMEM(s, jnp.float32) for s in shapes] + [pltpu.SemaphoreType.DMA((2,))],
        compiler_params=pltpu.CompilerParams(vmem_limit_bytes=16 * 2**20),
        name="finish",
    )(*args)


def after(value, *others):
    return lax.optimization_barrier((value, *others))[0]


def body(activations, labels):
    tokens, cols = activations.shape
    n_tok, n_feat = lax.axis_size("tok"), lax.axis_size("feat")
    levels = n_tok.bit_length() - 1
    assert n_tok == 1 << levels
    rows = PANEL * n_feat
    unit = rows // n_tok
    me, feat = lax.axis_index("tok"), lax.axis_index("feat")
    total = tokens * n_tok
    even, odd = orders_of(levels)
    parity = feat % 2
    bits = [(me >> jnp.where(parity == 0, a, b)) & 1 for a, b in zip(even, odd)]

    def swap(value, level):
        pairs = []
        for i in range(n_tok):
            for f in range(n_feat):
                bit = (even, odd)[f % 2][level]
                pairs.append((i * n_feat + f, (i ^ (1 << bit)) * n_feat + f))
        return lax.ppermute(value, ("tok", "feat"), pairs)

    own = activations[:, :PANEL]
    if n_feat == 2:
        other = lax.ppermute(own, "feat", [(0, 1), (1, 0)])
        pieces = [turn(own), [other]]
        places = [feat * PANEL // unit, (1 - feat) * PANEL // unit]
    else:
        pieces = [[lax.all_gather(own, "feat", axis=1, tiled=True)]]
        places = [0]
    meta = jnp.stack(places + [bits[0], parity]).astype(jnp.int32)
    onehot = (labels[None, :] == jnp.arange(PAD, dtype=jnp.int32)[:, None]).astype(jnp.bfloat16)

    sends, kept, sums, means, prepared = [], [], [], [], None
    for chunk, blocks in enumerate(CHUNKS):
        first = sum(CHUNKS[:chunk])
        out = local_part(first, blocks, activations, pieces, onehot, meta, (even, odd), rows, prepared)
        sends.append(out[0])
        kept.append(out[1])
        sums.append(out[2])
        means.append(out[3])
        if chunk == 0:
            prepared, extra = out[4:6], out[6]
    head, lanes = cols + PANEL, cols // CLASSES
    sums = jnp.concatenate(
        sums + [extra[:, :PANEL], jnp.concatenate(means, axis=0), extra[:, PANEL:]], axis=1
    )

    start = sum(bit * (rows >> (k + 1)) for k, bit in enumerate(bits))
    last = len(CHUNKS) - 1
    turns = []
    for level in range(levels - 1):
        turns += [(chunk, level) for chunk in range(last)]
        turns.insert(len(turns) - (level == 2), (SUMS, level))
        turns += [(last, level)]
    turns += [(SUMS, levels - 1)]

    came = [swap(send, 0) for send in sends]
    route = list(range(2, levels)) + [0, 1]
    came_sums = swap(sums, route[0])
    done = ()
    for chunk, level in turns:
        if chunk == SUMS:
            other = after(came_sums, *done)
            sums = jnp.concatenate([sums[:, :head] + other[:, :head], sums[:, head:], other[:, head:]], axis=1)
            if level + 1 < levels:
                came_sums = swap(sums, route[level + 1])
            done = (sums,)
        else:
            mine, other = kept[chunk], after(came[chunk], *done)
            half = mine.shape[0] // 2
            bit = bits[level + 1]

            def merged(bit):
                pick = lambda a: lax.dynamic_slice_in_dim(a, bit * half, half, 0)
                return pick(mine) + pick(other).astype(jnp.float32)

            send = merged(1 - bit).astype(jnp.bfloat16)
            kept[chunk] = merged(bit)
            came[chunk] = swap(send, level + 1)
            done = (send,)

    means = sums[:, head:].reshape(CLASSES, n_tok, lanes + PANEL)
    away = (means - jnp.mean(means, axis=1, keepdims=True)).transpose(1, 0, 2)
    place = lax.dynamic_slice(
        away, (0, start // PANEL, lanes + start % PANEL), (n_tok, 1, unit)
    ).reshape(n_tok, unit).T
    away = away[:, :, :lanes].reshape(n_tok, cols)
    sums = sums[:, :head]
    came = [after(c, place, away, sums) for c in came]
    return tuple(finish(total, tokens, sums, place, away, kept, came))


def solution(mesh):
    in_specs = (P("tok", "feat"), P("tok"))
    out_specs = (P("tok", "feat"), P(None, "feat"))
    return jax.shard_map(body, mesh=mesh, in_specs=in_specs, out_specs=out_specs, check_vma=False)
```
